32 devices in a mesh: ctx: 4 (over y, core), wsh: 8 (over z, x).
Axes of the slice: x: 2, y: 2, z: 4, core: 2. Of those that a mesh axis runs over, the one named last changes fastest.
Arguments:
- stream_in: bfloat16 [8, 1024, 1024], P('wsh', 'ctx'), may hold values from -6 to 6
- doc_lengths: int32 [8, 16], P('wsh'), may hold values from 1 to 768, 1024 in all within a row
- cotangent: bfloat16 [8, 1024, 1024], P('wsh', 'ctx'), may hold values from -6 to 6
- weights: bfloat16 [2, 12, 1024, 1024], P(None, None, 'wsh')
- vec_params: float32 [2, 12288], replicated
- owner_slots: int32 [2, 12], replicated, may hold values from 0 to 23, as said below
- master: float32 [24, 1024, 1024], P('ctx', 'wsh'), may hold values from -1.5 to 1.5
- left_bases: float32 [24, 1024, 1024], P('ctx', 'wsh'), as said below
- right_bases: float32 [24, 1024, 1024], P('ctx'), as said below
- moment1: float32 [24, 1024, 1024], P('ctx', 'wsh'), may hold values from -4 to 4
- moment2: float32 [24, 1024, 1024], P('ctx', 'wsh'), may hold values from 0.01 to 1
- vec_moment1: float32 [2, 12288], replicated, may hold values from -4 to 4
- vec_moment2: float32 [2, 12288], replicated, may hold values from 0.01 to 1
Outputs:
- stream_out: bfloat16 [8, 1024, 1024], P('wsh', 'ctx')
- stream_grad: float32 [8, 1024, 1024], P('wsh', 'ctx')
- block_grads: float32 [24, 1024, 1024], P('ctx', 'wsh')
- new_moment1: float32 [24, 1024, 1024], P('ctx', 'wsh')
- new_moment2: float32 [24, 1024, 1024], P('ctx', 'wsh')
- new_master: float32 [24, 1024, 1024], P('ctx', 'wsh')
- new_weights: bfloat16 [2, 12, 1024, 1024], P(None, None, 'wsh')
- vec_grads: float32 [2, 12288], replicated
- new_vec_params: float32 [2, 12288], replicated
- new_vec_moment1: float32 [2, 12288], replicated
- new_vec_moment2: float32 [2, 12288], replicated
The draws below stay inside these ranges and needn't reach their ends.
Inputs may be any that keep to these rules, and one draw needn't show every extreme that they name: `doc_lengths`: the 16 lengths of a stream sum to 1024; the longest is exactly 768. `owner_slots`: all entries are distinct; the other 0 slots hold no block. Every left_bases[s] is an orthogonal matrix. Every right_bases[s] is an orthogonal matrix.
All inputs are finite; a program needn't handle non-finite values.
Results may differ from the reference program's by a relative error of at most 0.028.
Values may be sent and summed in bfloat16 or wider, within the bound.
No kernel may reach another device: no remote copies, remote signals or barrier semaphores. Data moves between devices by JAX's collectives and lax.ppermute only.
A program may use at most 448 MiB of HBM per device.

```python
import math
import jax
import jax.numpy as jnp
import numpy as np
from jax import lax

D = 1024
HEADS = 16
HEAD_DIM = 64
FF = 4096
BLK = 1024
LAYERS = 2
NDOC = 16
SEQ = 1024
STREAMS = 8
DOC_MOST = 768
NBLK = 12
SLOTS = 24
VEC = 12288


def draw_weights(key, part):
    rows_d = D // BLK
    rows_f = FF // BLK
    end_qkv = 3 * rows_d * rows_d
    end_out = end_qkv + rows_d * rows_d
    end_up = end_out + rows_d * rows_f
    block_at = jnp.arange(NBLK)
    scaling = jnp.where(block_at < end_qkv, D ** (-0.5), jnp.where(block_at < end_out, 5.0 * D ** (-0.5), jnp.where(block_at < end_up, D ** (-0.5), 1.5 * FF ** (-0.5))))
    normal = jax.random.normal(jax.random.fold_in(key, 3), (LAYERS, NBLK, BLK, BLK), jnp.float32)
    return (normal * scaling.astype(jnp.float32)[None, :, None, None]).astype(jnp.bfloat16)


def draw_vec_params(key, part):
    noise_vals = jax.random.normal(jax.random.fold_in(key, 5), (LAYERS, 8 * D + FF), jnp.float32)
    column = jnp.arange(8 * D + FF)
    is_gain = (column >= 4 * D) & (column < 5 * D) | (column >= 6 * D) & (column < 7 * D)
    return jnp.where(is_gain[None, :], 1.0 + 0.2 * noise_vals, 0.3 * noise_vals)


def draw_owner_slots(key, part):
    total = LAYERS * NBLK
    order = jax.random.permutation(jax.random.fold_in(key, 21), total)
    slot_of = (jnp.arange(total, dtype=jnp.int32) + 1) * SLOTS // total - 1
    return jnp.take(slot_of, order).reshape(LAYERS, NBLK).astype(jnp.int32)


def orthogonal_blocks(key):

    def single(sub_key):
        freq_order = jax.random.permutation(jax.random.fold_in(sub_key, 1), BLK)
        sign_vec = 2.0 * jax.random.randint(jax.random.fold_in(sub_key, 2), (BLK,), 0, 2).astype(jnp.float32) - 1.0
        frequency = freq_order.astype(jnp.float32)[None, :]
        sample_at = jnp.arange(BLK, dtype=jnp.float32)[:, None] + 0.5
        basis_mat = jnp.cos(math.pi * sample_at * frequency / BLK) * math.sqrt(2.0 / BLK)
        basis_mat = jnp.where(frequency == 0.0, basis_mat * math.sqrt(0.5), basis_mat)
        return basis_mat * sign_vec[None, :]
    sub_keys = jax.random.split(key, SLOTS)
    return jax.vmap(single)(sub_keys)


def draw_left_bases(key, part):
    return orthogonal_blocks(jax.random.fold_in(key, 11))


def draw_right_bases(key, part):
    return orthogonal_blocks(jax.random.fold_in(key, 12))


def block_levels(key, extent, cuts, smallest, largest):
    level, own = 1.0, jax.random.fold_in(key, 6)
    for dim, parts in cuts:
        steps = jnp.exp(jax.random.uniform(jax.random.fold_in(own, dim), (parts,), jnp.float32, smallest / len(cuts), largest / len(cuts)))
        level = level * jnp.repeat(steps, extent[dim] // parts).reshape([-1 if axis == dim else 1 for axis in range(len(extent))])
    return level


def profile(amount, total, limit, lean):
    weights = [(1 << 20) // math.isqrt(grade ** lean) + 1 for grade in range(2, amount + 1)]
    rest, given = total - limit - (amount - 1), [1] * (amount - 1)
    while rest > 0:
        free = [i for i in range(amount - 1) if given[i] < limit]
        pool, remaining = sum([weights[i] for i in free]), rest
        for i in free:
            more = min(limit - given[i], max(1, remaining * weights[i] // pool), rest)
            given[i] = given[i] + more
            rest = rest - more
    return np.array([limit] + given)


def ragged_sizes(rng, amount, total, most, skew):
    if amount == 2:
        one = jax.random.randint(rng, (), max(1, total - most), min(most, total - 1) + 1)
        return jnp.stack([one, total - one])
    sizes = jnp.asarray(profile(amount, total, most, skew), jnp.int32)
    pairs = (amount - 1) // 2
    giver, sink = sizes[1:1 + 2 * pairs:2], sizes[2:2 + 2 * pairs:2]
    margin = jnp.minimum(giver - 1, most - sink)
    shifted = jax.random.randint(jax.random.fold_in(rng, 1), (pairs,), 0, 1 << 20) % (margin + 1)
    sizes = sizes.at[1:1 + 2 * pairs:2].set(giver - shifted).at[2:2 + 2 * pairs:2].set(sink + shifted)
    return sizes[jax.random.permutation(jax.random.fold_in(rng, 2), amount)]


def noise(key, dims, scale, reach, shards=(), kind=jnp.bfloat16):
    gain = block_levels(key, dims, shards, -0.22, 0.18) if shards else 1.0
    entries = jax.random.normal(key, dims, jnp.float32) * scale * gain
    return jnp.minimum(jnp.maximum(entries, -reach), reach).astype(kind)


def setup_inputs(seed: int = 0) -> dict:
    splits = jax.random.split(jax.random.key(seed), 14)
    return {
        "stream_in": noise(splits[0], (STREAMS, SEQ, D), 1.0, 6.0, ((0, 8), (1, 4))),
        "doc_lengths": jax.vmap(lambda own: ragged_sizes(own, NDOC, SEQ, DOC_MOST, 2))(jax.random.split(splits[1], STREAMS)).reshape((STREAMS, NDOC)).astype(jnp.int32),
        "cotangent": noise(splits[2], (STREAMS, SEQ, D), 1.0, 6.0, ((0, 8), (1, 4))),
        "weights": draw_weights(jax.random.fold_in(splits[13], 71), 0),
        "vec_params": draw_vec_params(jax.random.fold_in(splits[13], 71), 0),
        "owner_slots": draw_owner_slots(jax.random.fold_in(splits[13], 71), 0),
        "master": noise(splits[6], (SLOTS, BLK, BLK), 0.1, 1.5, ((0, 4), (1, 8)), jnp.float32),
        "left_bases": draw_left_bases(jax.random.fold_in(splits[13], 71), 0),
        "right_bases": draw_right_bases(jax.random.fold_in(splits[13], 71), 0),
        "moment1": noise(splits[9], (SLOTS, BLK, BLK), 0.3, 4.0, ((0, 4), (1, 8)), jnp.float32),
        "moment2": jnp.clip(jnp.exp(math.log(1.0) - 4.6051702 * jax.random.uniform(splits[10], (SLOTS, BLK, BLK), jnp.float32) ** block_levels(splits[10], (SLOTS, BLK, BLK), ((0, 4), (1, 8)), -0.2, 0.2)), 0.01, 1.0),
        "vec_moment1": noise(splits[11], (LAYERS, VEC), 0.3, 4.0, (), jnp.float32),
        "vec_moment2": jnp.clip(jnp.exp(jax.random.uniform(splits[12], (LAYERS, VEC), jnp.float32, math.log(0.01), math.log(1.0))), 0.01, 1.0),
    }


EPS_NORM = 1e-05
EPS_ADAM = 1e-08
LR_BLOCK = 0.1
LR_VEC = 0.25
DECAY_RATE = 0.5
HIGHEST_PREC = lax.Precision.HIGHEST

@jax.custom_vjp
def low(v):
    return lax.optimization_barrier(v.astype(jnp.bfloat16)).astype(jnp.float32)

@jax.custom_vjp
def low_back(v):
    return v

def low_keep(v):
    return (low(v), None)

def low_pass(kept, grad):
    return (grad,)

def back_keep(v):
    return (v, None)

def back_low(kept, grad):
    return (low(grad),)
low.defvjp(low_keep, low_pass)
low_back.defvjp(back_keep, back_low)

def norm_rows(summed, gain_vec, shift_vec):
    average = lax.optimization_barrier(jnp.mean(summed, axis=-1, keepdims=True))
    centred = summed - average
    variance = lax.optimization_barrier(jnp.mean(centred * centred, axis=-1, keepdims=True))
    return centred * lax.rsqrt(variance + EPS_NORM) * gain_vec + shift_vec

def assemble(blocks, rows_b, cols_b):
    return blocks.reshape(rows_b, cols_b, BLK, BLK).transpose(0, 2, 1, 3).reshape(rows_b * BLK, cols_b * BLK)

def dense_dot(left_mat, right_mat):
    return jnp.dot(left_mat, right_mat, precision=HIGHEST_PREC)

def layer(activation, blocks, vector, same_doc):
    rows_d = D // BLK
    rows_f = FF // BLK
    end_qkv = 3 * rows_d * rows_d
    end_out = end_qkv + rows_d * rows_d
    end_up = end_out + rows_d * rows_f
    w_qkv = assemble(blocks[:end_qkv], rows_d, 3 * rows_d)
    w_out = assemble(blocks[end_qkv:end_out], rows_d, rows_d)
    w_up = assemble(blocks[end_out:end_up], rows_d, rows_f)
    w_down = assemble(blocks[end_up:], rows_f, rows_d)
    pieces = [vector[spot * D:(spot + 1) * D] for spot in range(8)]
    bias_q, bias_v, bias_o, bias_down, gain_one, shift_one, gain_two, shift_two = pieces
    bias_up = vector[8 * D:]
    seq_len = activation.shape[0]
    qkv_vals = dense_dot(low(activation), w_qkv) + jnp.concatenate([bias_q, jnp.zeros((D,), jnp.float32), bias_v])
    qkv_vals = low(low_back(qkv_vals))
    head_parts = qkv_vals.reshape(seq_len, 3, HEADS, HEAD_DIM).transpose(1, 2, 0, 3)

    def one_head(head_set):
        query_h, key_h, value_h = head_set
        scores = low_back(dense_dot(query_h, key_h.T) * HEAD_DIM ** (-0.5))
        scores = jnp.where(same_doc, scores, -1e+30)
        attn_prob = low(jax.nn.softmax(scores, axis=-1))
        return dense_dot(attn_prob, value_h)
    mixture = lax.map(jax.checkpoint(one_head), (head_parts[0], head_parts[1], head_parts[2]))
    attn_low = low(low_back(mixture.transpose(1, 0, 2).reshape(seq_len, D)))
    branch = low_back(dense_dot(attn_low, w_out) + bias_o)
    middle = norm_rows(activation + branch, gain_one, shift_one)
    hidden = low_back(dense_dot(low(middle), w_up) + bias_up)
    act_low = low(jax.nn.gelu(hidden, approximate=False))
    ffn_out = low_back(dense_dot(act_low, w_down) + bias_down)
    return norm_rows(middle + ffn_out, gain_two, shift_two)

def reference(stream_in, doc_lengths, cotangent, weights, vec_params, owner_slots, master, left_bases, right_bases, moment1, moment2, vec_moment1, vec_moment2):
    blocks = weights.astype(jnp.float32)
    position = jnp.arange(SEQ, dtype=jnp.int32)
    scaling = (STREAMS * SEQ) ** (-0.5)

    def one_stream(carried, item_set):
        grad_blocks, grad_vec = carried
        stream_x, lengths, stream_cot = item_set
        starts = jnp.cumsum(lengths) - lengths
        doc_id = lax.optimization_barrier(jnp.sum((position[:, None] >= starts[None, :]).astype(jnp.int32), axis=1))
        same_doc = doc_id[:, None] == doc_id[None, :]

        def forward(activation, block_set, vec_set):
            for layer_at in range(LAYERS):
                activation = layer(activation, block_set[layer_at], vec_set[layer_at], same_doc)
            return activation
        result, pullback = jax.vjp(forward, stream_x.astype(jnp.float32), blocks, vec_params)
        grad_x, grad_b, grad_v = pullback(stream_cot.astype(jnp.float32))
        return ((grad_blocks + grad_b, grad_vec + grad_v), (result.astype(jnp.bfloat16), grad_x))
    zero_state = (jnp.zeros(blocks.shape, jnp.float32), jnp.zeros(vec_params.shape, jnp.float32))
    (grad_blocks, grad_vec), (stream_out, stream_grad) = lax.scan(one_stream, zero_state, (stream_in, doc_lengths, cotangent))
    grad_blocks = grad_blocks * scaling
    vec_grads = grad_vec * scaling
    owner_flat = owner_slots.reshape(-1).astype(jnp.int32)
    flat_grads = grad_blocks.reshape(LAYERS * NBLK, BLK, BLK)
    block_grads = jnp.zeros((SLOTS, BLK, BLK), jnp.float32).at[owner_flat].set(flat_grads)
    product = jnp.einsum('sac,scd->sad', block_grads, right_bases, precision=HIGHEST_PREC)
    rotated = jnp.einsum('sab,sad->sbd', left_bases, product, precision=HIGHEST_PREC)
    new_moment1 = DECAY_RATE * moment1 + (1.0 - DECAY_RATE) * rotated
    new_moment2 = DECAY_RATE * moment2 + (1.0 - DECAY_RATE) * rotated * rotated
    direction = new_moment1 / (jnp.sqrt(new_moment2) + EPS_ADAM)
    partial_back = jnp.einsum('sbc,sdc->sbd', direction, right_bases, precision=HIGHEST_PREC)
    update = jnp.einsum('sab,sbd->sad', left_bases, partial_back, precision=HIGHEST_PREC)
    new_master = master - LR_BLOCK * update
    new_weights = jnp.take(new_master.astype(jnp.bfloat16), owner_flat, axis=0).reshape(LAYERS, NBLK, BLK, BLK)
    new_vec_moment1 = DECAY_RATE * vec_moment1 + (1.0 - DECAY_RATE) * vec_grads
    new_vec_moment2 = DECAY_RATE * vec_moment2 + (1.0 - DECAY_RATE) * vec_grads * vec_grads
    new_vec_params = vec_params - LR_VEC * new_vec_moment1 / (jnp.sqrt(new_vec_moment2) + EPS_ADAM)
    return (stream_out, stream_grad, block_grads, new_moment1, new_moment2, new_master, new_weights, vec_grads, new_vec_params, new_vec_moment1, new_vec_moment2)
```

```python
import functools

import jax
import jax.numpy as jnp
import numpy as np
from jax import lax
from jax.experimental import pallas as pl
from jax.experimental.pallas import tpu as pltpu
from jax.sharding import PartitionSpec as P

D = 1024
HEADS = 16
HEAD_DIM = 64
FF = 4096
BLK = 1024
LAYERS = 2
NBLK = 12
CORES = 2
DEPTH_Z = 4

EPS_NORM = 1e-05
EPS_ADAM = 1e-08
LR_BLOCK = 0.1
LR_VEC = 0.25
DECAY_RATE = 0.5
HEAD_GROUP = 4
BF16 = jnp.bfloat16
F32 = jnp.float32


class Place:
    def __init__(self, ctx_count, wsh_count):
        self.size = {
            "core": CORES,
            "y": ctx_count // CORES,
            "z": DEPTH_Z,
            "x": wsh_count // DEPTH_Z,
        }
        ctx_at = lax.axis_index("ctx")
        wsh_at = lax.axis_index("wsh")
        self.at = {
            "core": ctx_at % CORES,
            "y": ctx_at // CORES,
            "z": wsh_at // self.size["x"],
            "x": wsh_at % self.size["x"],
        }

    def take(self, value, axis, step):
        name, slow, fast = {
            "core": ("ctx", "y", "core"),
            "y": ("ctx", "y", "core"),
            "z": ("wsh", "z", "x"),
            "x": ("wsh", "z", "x"),
        }[axis]
        extent = self.size[axis]
        pairs = []
        for slow_at in range(self.size[slow]):
            for fast_at in range(self.size[fast]):
                if axis == fast:
                    other = (slow_at, (fast_at + step) % extent)
                else:
                    other = ((slow_at + step) % extent, fast_at)
                pairs.append(
                    (
                        other[0] * self.size[fast] + other[1],
                        slow_at * self.size[fast] + fast_at,
                    )
                )
        return lax.ppermute(value, name, pairs)

    def gather(self, value, axis):
        steps = range(1, self.size[axis])
        return jnp.stack([value] + [self.take(value, axis, step) for step in steps])

    def scatter(self, values, axis):
        total = values[0].astype(F32)
        for step in range(1, self.size[axis]):
            total = total + self.take(values[step], axis, -step).astype(F32)
        return total


def norm_rows(summed, gain_vec, shift_vec):
    average = jnp.mean(summed, axis=-1, keepdims=True)
    centred = summed - average
    variance = jnp.mean(centred * centred, axis=-1, keepdims=True)
    return centred * lax.rsqrt(variance + EPS_NORM) * gain_vec + shift_vec


def gelu_exact(values):
    return jax.nn.gelu(values, approximate=False)


def vector_parts(vector):
    pieces = [vector[spot * D : (spot + 1) * D] for spot in range(8)]
    return pieces + [vector[8 * D :]]


def dot(left, right):
    return jnp.dot(left, right, preferred_element_type=F32)


def dot_t(left, right):
    return lax.dot_general(left, right, (((1,), (1,)), ((), ())), preferred_element_type=F32)


def assemble_kernel(split_count, whole_count, has_y, where, *refs):
    if has_y:
        mine, other_y, core_mine, core_other_y, out = refs
    else:
        mine, core_mine, out = refs
    half_rows = mine.shape[3]
    half_cols = mine.shape[4]
    core_at = where[3]
    y_at = where[2]

    def put(block, rows, cols, value):
        out[block, 0, pl.ds(rows * half_rows, half_rows), pl.ds(cols * half_cols, half_cols)] = value

    for core in range(2):

        @pl.when(core_at == core)
        def _():
            if has_y:
                for y in range(2):

                    @pl.when(y_at == y)
                    def _():
                        for block in range(split_count):
                            put(block, core, y, mine[0, 0, block])
                            put(block, core, 1 - y, other_y[0, 0, block])
                            put(block, 1 - core, y, core_mine[0, 0, block])
                            put(block, 1 - core, 1 - y, core_other_y[0, 0, block])

            for block in range(whole_count):
                for cols in range(2):
                    entry = split_count + 2 * block + cols
                    put(split_count + block, core, cols, mine[0, 0, entry])
                    put(split_count + block, 1 - core, cols, core_mine[0, 0, entry])


def gather_blocks(place, shard):
    count, rows, _ = shard.shape
    half_rows, half_cols = rows // 2, BLK // 2
    has_y = place.size["y"] == 2
    split_count = count - 1 if has_y else 0
    whole_count = count - split_count
    mine = lax.dynamic_slice_in_dim(shard, place.at["core"] * half_rows, half_rows, 1)
    whole = mine[split_count:]
    pieces = [
        part for block in range(whole_count) for part in (whole[block, :, :half_cols], whole[block, :, half_cols:])
    ]
    piece = jnp.stack(pieces)
    if has_y:
        parts = lax.dynamic_slice_in_dim(
            mine[:split_count], place.at["y"] * half_cols, half_cols, 2
        )
        piece = jnp.concatenate([parts, piece])
    held = place.gather(place.gather(piece, "z"), "x")
    operands = [held]
    if has_y:
        other_y = place.take(held[:, :, :split_count], "y", 1)
        operands.append(other_y)
    operands += [place.take(value, "core", 1) for value in list(operands)]
    count_z, count_x = place.size["z"], place.size["x"]
    where = jnp.stack([place.at[name] for name in ("z", "x", "y", "core")]).astype(jnp.int32)

    def piece_at(z, x, where):
        return (
            lax.rem(x - where[1] + count_x, count_x),
            lax.rem(z - where[0] + count_z, count_z),
            0,
            0,
            0,
        )

    out = pl.pallas_call(
        functools.partial(assemble_kernel, split_count, whole_count, has_y),
        grid_spec=pltpu.PrefetchScalarGridSpec(
            num_scalar_prefetch=1,
            grid=(count_z, count_x),
            in_specs=[pl.BlockSpec((1, 1) + value.shape[2:], piece_at) for value in operands],
            out_specs=pl.BlockSpec(
                (count, 1, rows, BLK), lambda z, x, where: (0, z * count_x + x, 0, 0)
            ),
        ),
        out_shape=jax.ShapeDtypeStruct((count, count_z * count_x, rows, BLK), BF16),
        cost_estimate=pl.CostEstimate(
            flops=0, bytes_accessed=4 * count * BLK * BLK, transcendentals=0
        ),
        name="assemble",
    )(where, *operands)
    return out.reshape(count, BLK, BLK)


def group_scores(query_g, key_g, same_doc):
    scores = jnp.einsum(
        "thd,shd->hts", query_g, key_g, preferred_element_type=jnp.float32
    ) * HEAD_DIM ** (-0.5)
    return jnp.where(same_doc[None], scores, -1e30)


def attend_forward(queries, key_all, value_all, same_doc):
    tokens = queries.shape[0]
    group_width = HEAD_GROUP * HEAD_DIM
    out_parts = []
    total_parts = []
    for group_at in range(HEADS // HEAD_GROUP):
        low_col = group_at * group_width
        query_g = queries[:, low_col : low_col + group_width].reshape(tokens, HEAD_GROUP, HEAD_DIM)
        key_g = key_all[:, low_col : low_col + group_width].reshape(-1, HEAD_GROUP, HEAD_DIM)
        value_g = value_all[:, low_col : low_col + group_width].reshape(-1, HEAD_GROUP, HEAD_DIM)
        scores = group_scores(query_g, key_g, same_doc)
        row_peak = jnp.max(scores, axis=-1, keepdims=True)
        exp_scores = jnp.exp(scores - row_peak)
        row_total = jnp.sum(exp_scores, axis=-1, keepdims=True)
        probs_low = (exp_scores / row_total).astype(jnp.bfloat16)
        mixture = jnp.einsum("hts,shd->thd", probs_low, value_g, preferred_element_type=jnp.float32)
        out_parts.append(mixture.reshape(tokens, group_width))
        total_parts.append(row_peak + jnp.log(row_total))
    return (jnp.concatenate(out_parts, axis=1), total_parts)


def attend_backward(queries, key_all, value_all, grad_low, log_totals, same_doc):
    tokens = queries.shape[0]
    group_width = HEAD_GROUP * HEAD_DIM
    scale_qk = HEAD_DIM ** (-0.5)
    grad_q_parts = []
    grad_k_parts = []
    grad_v_parts = []
    for group_at in range(HEADS // HEAD_GROUP):
        low_col = group_at * group_width
        query_g = queries[:, low_col : low_col + group_width].reshape(tokens, HEAD_GROUP, HEAD_DIM)
        key_g = key_all[:, low_col : low_col + group_width].reshape(-1, HEAD_GROUP, HEAD_DIM)
        value_g = value_all[:, low_col : low_col + group_width].reshape(-1, HEAD_GROUP, HEAD_DIM)
        grad_g = grad_low[:, low_col : low_col + group_width].reshape(tokens, HEAD_GROUP, HEAD_DIM)
        scores = group_scores(query_g, key_g, same_doc)
        probs = jnp.exp(scores - log_totals[group_at])
        grad_prob = jnp.einsum("thd,shd->hts", grad_g, value_g, preferred_element_type=jnp.float32)
        inner_sum = jnp.sum(probs * grad_prob, axis=-1, keepdims=True)
        grad_score = (probs * (grad_prob - inner_sum)).astype(jnp.bfloat16)
        grad_q = (
            jnp.einsum("hts,shd->thd", grad_score, key_g, preferred_element_type=jnp.float32)
            * scale_qk
        )
        grad_q_parts.append(grad_q.reshape(tokens, group_width))
        grad_k = (
            jnp.einsum("hts,thd->shd", grad_score, query_g, preferred_element_type=jnp.float32)
            * scale_qk
        )
        grad_v = jnp.einsum(
            "hts,thd->shd", probs.astype(jnp.bfloat16), grad_g, preferred_element_type=jnp.float32
        )
        grad_k_parts.append(grad_k.reshape(-1, group_width))
        grad_v_parts.append(grad_v.reshape(-1, group_width))
    return (
        jnp.concatenate(grad_q_parts, axis=1),
        jnp.concatenate(grad_k_parts, axis=1),
        jnp.concatenate(grad_v_parts, axis=1),
    )


def layer_forward(place, activation, blocks, vector, same_doc):
    w_in, w_up, w_down = blocks
    bias_q, bias_v, bias_o, bias_down, gain_one, shift_one, gain_two, shift_two, bias_up = (
        vector_parts(vector)
    )
    x_low = activation.astype(BF16)
    query = (dot(x_low, w_in[0]) + bias_q).astype(BF16)
    keyval = jnp.concatenate([dot(x_low, w_in[1]), dot(x_low, w_in[2]) + bias_v], axis=1).astype(
        BF16
    )
    keyval_all = place.gather(place.gather(keyval, "y"), "core").reshape(-1, 2 * D)
    mixture, log_totals = attend_forward(
        query, keyval_all[:, :D], keyval_all[:, D:], same_doc
    )
    attn_low = mixture.astype(BF16)
    summed_one = activation + dot(attn_low, w_in[3]) + bias_o
    middle = norm_rows(summed_one, gain_one, shift_one)
    mid_low = middle.astype(BF16)
    hidden = (
        jnp.concatenate([dot(mid_low, w_up[spot]) for spot in range(FF // BLK)], axis=1) + bias_up
    )
    act_low = gelu_exact(hidden).astype(BF16)
    ffn_out = bias_down
    for spot in range(FF // BLK):
        ffn_out = ffn_out + dot(act_low[:, spot * BLK : (spot + 1) * BLK], w_down[spot])
    summed_two = middle + ffn_out
    result = norm_rows(summed_two, gain_two, shift_two)
    saved = (x_low, query, keyval_all, log_totals, attn_low, summed_one, mid_low, hidden, act_low, summed_two)
    return (result, saved)


def left_order(place, left):
    tokens, cols = left.shape
    count_z, count_x = place.size["z"], place.size["x"]
    blocks = cols // BLK
    rows = BLK // (count_z * count_x)
    value = left.reshape(tokens, blocks, count_z, count_x, rows)
    value = jnp.roll(value, (-place.at["z"], -place.at["x"]), axis=(2, 3))
    return value.transpose(0, 3, 2, 1, 4).reshape(tokens, cols)


def right_halves(place, right):
    tokens, cols = right.shape
    count_y = place.size["y"]
    width = BLK // (CORES * count_y)
    value = right.reshape(tokens, cols // BLK, CORES, count_y, width)
    halves = []
    for step in range(CORES):
        half = lax.dynamic_index_in_dim(value, (place.at["core"] + step) % CORES, 2, False)
        half = jnp.roll(half, -place.at["y"], axis=2)
        halves.append(half.transpose(2, 0, 1, 3).reshape(count_y, tokens, -1))
    return halves


def sum_job(place, left, right, first):
    count_z, count_x, count_y = place.size["z"], place.size["x"], place.size["y"]
    left = left_order(place, left)
    right_mine, right_other = right_halves(place, right)
    left_both = jnp.concatenate([left, place.take(left, "core", 1)], axis=0)
    right_both = jnp.concatenate([right_mine, place.take(right_other, "core", 1)], axis=1)
    partial = [
        lax.dot_general(left_both, right_both[step], (((0,), (0,)), ((), ())), preferred_element_type=F32)
        .astype(BF16)
        .reshape(count_x, count_z, -1, right_both.shape[2])
        for step in range(count_y)
    ]
    if first == "y":
        total = place.scatter(partial, "y").astype(BF16)
        total = place.scatter(total, "x").astype(BF16)
    else:
        parts = [[value[step] for value in partial] for step in range(count_x)]
        parts = [jnp.stack(part) for part in parts]
        total = place.scatter(parts, "x").astype(BF16)
        total = place.scatter(total, "y").astype(BF16)
    total = place.scatter(total, "z")
    rows = BLK // (count_z * count_x)
    width = BLK // (CORES * count_y)
    if left.shape[1] > BLK:
        return total.reshape(-1, rows, width)
    return total.reshape(rows, -1, width).transpose(1, 0, 2)


def layer_backward(place, grad_flow, blocks, vector, saved, same_doc):
    w_in, w_up, w_down = blocks
    bias_q, bias_v, bias_o, bias_down, gain_one, shift_one, gain_two, shift_two, bias_up = (
        vector_parts(vector)
    )
    x_low, query, keyval_all, log_totals, attn_low, summed_one, mid_low, hidden, act_low, summed_two = saved
    tokens = x_low.shape[0]
    norm_val, norm_pull = jax.vjp(norm_rows, summed_two, gain_two, shift_two)
    grad_s2, grad_g2, grad_e2 = norm_pull(grad_flow)
    ffn_low = grad_s2.astype(BF16)
    sum_down = sum_job(place, act_low, ffn_low, "y")
    grad_act = jnp.concatenate([dot_t(ffn_low, w_down[spot]) for spot in range(FF // BLK)], axis=1)
    gelu_val, gelu_pull = jax.vjp(gelu_exact, hidden)
    hid_low = gelu_pull(grad_act)[0].astype(BF16)
    sum_up = sum_job(place, mid_low, hid_low, "x")
    grad_mid = grad_s2
    for spot in range(FF // BLK):
        grad_mid = grad_mid + dot_t(hid_low[:, spot * BLK : (spot + 1) * BLK], w_up[spot])
    norm_val_one, norm_pull_one = jax.vjp(norm_rows, summed_one, gain_one, shift_one)
    grad_s1, grad_g1, grad_e1 = norm_pull_one(grad_mid)
    branch_low = grad_s1.astype(BF16)
    sum_out = sum_job(place, attn_low, branch_low, "y")
    attn_grad_low = dot_t(branch_low, w_in[3]).astype(BF16)
    grad_q, grad_k_all, grad_v_all = attend_backward(
        query, keyval_all[:, :D], keyval_all[:, D:], attn_grad_low, log_totals, same_doc
    )
    grad_kv = jnp.concatenate([grad_k_all, grad_v_all], axis=1).astype(BF16)
    grad_kv = grad_kv.reshape(CORES, -1, tokens, 2 * D)
    grad_kv = place.scatter(place.scatter(grad_kv, "core").astype(BF16), "y")
    qkv_grad_low = jnp.concatenate([grad_q, grad_kv], axis=1).astype(BF16)
    grad_x = grad_s1
    for spot in range(3):
        grad_x = grad_x + dot_t(qkv_grad_low[:, spot * D : (spot + 1) * D], w_in[spot])
    sum_in = sum_job(place, x_low, qkv_grad_low, "x")
    sums = jnp.concatenate([sum_in, sum_out, sum_up, sum_down])
    qkv_sum = jnp.sum(qkv_grad_low, axis=0, dtype=F32)
    vec_grad = jnp.concatenate(
        [
            qkv_sum[:D],
            qkv_sum[2 * D :],
            jnp.sum(branch_low, axis=0, dtype=F32),
            jnp.sum(ffn_low, axis=0, dtype=F32),
            grad_g1,
            grad_e1,
            grad_g2,
            grad_e2,
            jnp.sum(hid_low, axis=0, dtype=F32),
        ]
    )
    return (grad_x, sums, vec_grad)


def sum_everywhere(place, value):
    if place.size["y"] != 2 or place.size["x"] != 2:
        return lax.psum(value, ("ctx", "wsh"))
    for axis in ("core", "y", "x"):
        value = value + place.take(value, axis, 1)
    pairs = place.size["x"]
    for bit in (1, 2):
        swap = [
            (z * pairs + x, (z ^ bit) * pairs + x) for z in range(DEPTH_Z) for x in range(pairs)
        ]
        value = value + lax.ppermute(value, "wsh", swap)
    return value


def doc_ids(lengths, position):
    starts = jnp.cumsum(lengths) - lengths
    return jnp.sum((position[:, None] >= starts[None, :]).astype(jnp.int32), axis=1)


def to_owner(rows_value, wsh_count):
    slots = rows_value.shape[0]
    padded = jnp.pad(rows_value.astype(BF16), ((0, wsh_count - slots), (0, 0), (0, 0)))
    return lax.all_to_all(padded, "wsh", 0, 0, tiled=True).reshape(BLK, BLK)


def from_owner(whole, wsh_count, slots):
    cut = whole.astype(BF16).reshape(wsh_count, BLK // wsh_count, BLK)
    return lax.all_to_all(cut, "wsh", 0, 0, tiled=True)[:slots]


def on_device(
    stream_in,
    doc_lengths,
    cotangent,
    weights,
    vec_params,
    owner_slots,
    master,
    left_bases,
    right_bases,
    moment1,
    moment2,
    vec_moment1,
    vec_moment2,
):
    tokens = stream_in.shape[1]
    ctx_count = lax.axis_size("ctx")
    wsh_count = lax.axis_size("wsh")
    place = Place(ctx_count, wsh_count)
    seq_len = tokens * ctx_count
    scaling = (wsh_count * seq_len) ** (-0.5)
    slots_dev, rows_dev = master.shape[0], master.shape[1]
    slot_total = ctx_count * slots_dev
    count_y = place.size["y"]
    width = BLK // ctx_count

    core_of = (place.at["core"] + jnp.arange(CORES)) % CORES
    y_of = (place.at["y"] + jnp.arange(count_y)) % count_y
    ctx_of = (y_of[None, :] * CORES + core_of[:, None]).reshape(-1)
    key_pos = (ctx_of[:, None] * tokens + jnp.arange(tokens)[None, :]).reshape(-1)
    doc_keys = doc_ids(doc_lengths[0], key_pos)
    same_doc = doc_keys[:tokens, None] == doc_keys[None, :]

    blocks = []
    for layer_at in range(LAYERS):
        blocks.append(
            [
                gather_blocks(place, weights[layer_at, first : first + 4])
                for first in range(0, NBLK, 4)
            ]
        )
    activation = stream_in[0].astype(F32)
    kept = []
    for layer_at in range(LAYERS):
        activation, saved = layer_forward(
            place, activation, blocks[layer_at], vec_params[layer_at], same_doc
        )
        kept.append(saved)
    stream_out = activation.astype(BF16)[None]

    ahead, activation = lax.optimization_barrier(((left_bases, moment1, moment2), activation))
    left_own = to_owner(ahead[0], wsh_count)
    first_own = to_owner(ahead[1], wsh_count)
    second_own = to_owner(ahead[2], wsh_count)

    grad_flow = cotangent[0].astype(F32)
    sums = [None] * LAYERS
    vec_terms = [None] * LAYERS
    for layer_at in reversed(range(LAYERS)):
        grad_flow, sums[layer_at], vec_terms[layer_at] = layer_backward(
            place, grad_flow, blocks[layer_at], vec_params[layer_at], kept[layer_at], same_doc
        )
    stream_grad = grad_flow[None]
    vec_grads = sum_everywhere(place, jnp.stack(vec_terms)) * scaling

    all_sums = (jnp.concatenate(sums) * scaling).astype(BF16)
    owner_flat = owner_slots.reshape(-1)
    picks = (owner_flat[None, :] == jnp.arange(slot_total, dtype=jnp.int32)[:, None]).astype(BF16)
    by_slot = dot(picks, all_sums.reshape(LAYERS * NBLK, -1)).astype(BF16)
    by_slot = by_slot.reshape(ctx_count, slots_dev, rows_dev, width)

    quarters = lax.all_to_all(by_slot, "ctx", 0, 0, tiled=True)
    quarters = quarters.reshape(count_y, CORES, slots_dev, rows_dev, width)
    block_grads = quarters.transpose(2, 3, 1, 0, 4).reshape(slots_dev, rows_dev, BLK).astype(F32)

    padded = jnp.pad(by_slot, ((0, 0), (0, wsh_count - slots_dev), (0, 0), (0, 0)))
    arrived = lax.all_to_all(
        padded.reshape(ctx_count * wsh_count, rows_dev, width), ("ctx", "wsh"), 0, 0, tiled=True
    )
    arrived = arrived.reshape(count_y, CORES, wsh_count, rows_dev, width)
    grad_own = arrived.transpose(2, 3, 1, 0, 4).reshape(BLK, BLK)
    slot_own = jnp.minimum(lax.axis_index("wsh"), slots_dev - 1)
    right_own = lax.dynamic_index_in_dim(right_bases, slot_own, 0, False).astype(BF16)
    product = dot(grad_own, right_own).astype(BF16)
    rotated_own = lax.dot_general(
        left_own, product, (((0,), (0,)), ((), ())), preferred_element_type=F32
    )
    rotated = from_owner(rotated_own, wsh_count, slots_dev).astype(F32)
    first_new = DECAY_RATE * first_own.astype(F32) + (1.0 - DECAY_RATE) * rotated_own
    second_new = (
        DECAY_RATE * second_own.astype(F32) + (1.0 - DECAY_RATE) * rotated_own * rotated_own
    )
    direction = (first_new / (jnp.sqrt(second_new) + EPS_ADAM)).astype(BF16)
    back = dot_t(direction, right_own).astype(BF16)
    update = from_owner(dot(left_own, back), wsh_count, slots_dev).astype(F32)

    new_moment1 = DECAY_RATE * moment1 + (1.0 - DECAY_RATE) * rotated
    new_moment2 = DECAY_RATE * moment2 + (1.0 - DECAY_RATE) * rotated * rotated
    new_master = master - LR_BLOCK * update
    slot_rows = place.gather(place.gather(new_master.astype(BF16), "y"), "core")
    slot_rows = slot_rows.reshape(slot_total, rows_dev, BLK)
    owner_ctx, owner_at = owner_flat // slots_dev, owner_flat % slots_dev
    step_y = (owner_ctx // CORES - place.at["y"]) % count_y
    step_core = (owner_ctx % CORES - place.at["core"]) % CORES
    spot = (step_core * count_y + step_y) * slots_dev + owner_at
    new_weights = jnp.take(slot_rows, spot, axis=0).reshape(LAYERS, NBLK, rows_dev, BLK)

    new_vec_moment1 = DECAY_RATE * vec_moment1 + (1.0 - DECAY_RATE) * vec_grads
    new_vec_moment2 = DECAY_RATE * vec_moment2 + (1.0 - DECAY_RATE) * vec_grads * vec_grads
    new_vec_params = vec_params - LR_VEC * new_vec_moment1 / (jnp.sqrt(new_vec_moment2) + EPS_ADAM)
    return (
        stream_out,
        stream_grad,
        block_grads,
        new_moment1,
        new_moment2,
        new_master,
        new_weights,
        vec_grads,
        new_vec_params,
        new_vec_moment1,
        new_vec_moment2,
    )


def solution(mesh):
    rows = P("ctx", "wsh", None)
    placed = (
        P("wsh", "ctx", None),
        P("wsh", None),
        P("wsh", "ctx", None),
        P(None, None, "wsh", None),
        P(),
        P(),
        rows,
        rows,
        P("ctx", None, None),
        rows,
        rows,
        P(),
        P(),
    )
    return jax.shard_map(
        on_device,
        mesh=mesh,
        in_specs=placed,
        out_specs=(
            P("wsh", "ctx", None),
            P("wsh", "ctx", None),
            rows,
            rows,
            rows,
            rows,
            P(None, None, "wsh", None),
            P(),
            P(),
            P(),
            P(),
        ),
        check_vma=False,
    )
```

```python
import functools

import jax
import jax.numpy as jnp
import numpy as np
from jax import lax
from jax.experimental import pallas as pl
from jax.experimental.pallas import tpu as pltpu
from jax.sharding import PartitionSpec as P

D = 1024
HEADS = 16
HEAD_DIM = 64
FF = 4096
BLK = 1024
LAYERS = 2
NBLK = 12
CORES = 2
DEPTH_Z = 4

EPS_NORM = 1e-05
EPS_ADAM = 1e-08
LR_BLOCK = 0.1
LR_VEC = 0.25
DECAY_RATE = 0.5
VMEM_BYTES = 56 * 1024 * 1024
BF16 = jnp.bfloat16
F32 = jnp.float32


class Place:
    def __init__(self, ctx_count, wsh_count):
        self.size = {
            "core": CORES,
            "y": ctx_count // CORES,
            "z": DEPTH_Z,
            "x": wsh_count // DEPTH_Z,
        }
        ctx_at = lax.axis_index("ctx")
        wsh_at = lax.axis_index("wsh")
        self.at = {
            "core": ctx_at % CORES,
            "y": ctx_at // CORES,
            "z": wsh_at // self.size["x"],
            "x": wsh_at % self.size["x"],
        }

    def take(self, value, axis, step):
        name, slow, fast = {
            "core": ("ctx", "y", "core"),
            "y": ("ctx", "y", "core"),
            "z": ("wsh", "z", "x"),
            "x": ("wsh", "z", "x"),
        }[axis]
        extent = self.size[axis]
        pairs = []
        for slow_at in range(self.size[slow]):
            for fast_at in range(self.size[fast]):
                if axis == fast:
                    other = (slow_at, (fast_at + step) % extent)
                else:
                    other = ((slow_at + step) % extent, fast_at)
                pairs.append(
                    (
                        other[0] * self.size[fast] + other[1],
                        slow_at * self.size[fast] + fast_at,
                    )
                )
        return lax.ppermute(value, name, pairs)

    def gather(self, value, axis):
        steps = range(1, self.size[axis])
        return jnp.stack([value] + [self.take(value, axis, step) for step in steps])

    def collect(self, values, axis):
        steps = range(1, self.size[axis])
        return [values[0]] + [self.take(values[step], axis, -step) for step in steps]

    def scatter(self, values, axis):
        total = values[0].astype(F32)
        for step in range(1, self.size[axis]):
            total = total + self.take(values[step], axis, -step).astype(F32)
        return total


def vector_parts(vector):
    pieces = [vector[spot * D : (spot + 1) * D] for spot in range(8)]
    return pieces + [vector[8 * D :]]


def dot(left, right):
    return jnp.dot(left, right, preferred_element_type=F32)


def dot_t(left, right):
    return lax.dot_general(left, right, (((1,), (1,)), ((), ())), preferred_element_type=F32)


def assemble_kernel(split_count, whole_count, has_y, where, *refs):
    if has_y:
        mine, other_y, core_mine, core_other_y, out = refs
    else:
        mine, core_mine, out = refs
    half_rows = mine.shape[3]
    half_cols = mine.shape[4]
    core_at = where[3]
    y_at = where[2]

    def put(block, rows, cols, value):
        out[block, 0, pl.ds(rows * half_rows, half_rows), pl.ds(cols * half_cols, half_cols)] = value

    for core in range(2):

        @pl.when(core_at == core)
        def _():
            if has_y:
                for y in range(2):

                    @pl.when(y_at == y)
                    def _():
                        for block in range(split_count):
                            put(block, core, y, mine[0, 0, block])
                            put(block, core, 1 - y, other_y[0, 0, block])
                            put(block, 1 - core, y, core_mine[0, 0, block])
                            put(block, 1 - core, 1 - y, core_other_y[0, 0, block])

            for block in range(whole_count):
                for cols in range(2):
                    entry = split_count + 2 * block + cols
                    put(split_count + block, core, cols, mine[0, 0, entry])
                    put(split_count + block, 1 - core, cols, core_mine[0, 0, entry])


def after(value, *others):
    return lax.optimization_barrier((value,) + others)[0]


def together(*values):
    return lax.optimization_barrier(values)


def add_up(values):
    return sum(value.astype(F32) for value in values)


class Gathering:
    def __init__(self, place, shard):
        self.place = place
        self.count, self.rows, _ = shard.shape
        half_rows, half_cols = self.rows // 2, BLK // 2
        has_y = place.size["y"] == 2
        self.split_count = self.count // 2 if has_y else 0
        whole_count = self.count - self.split_count
        mine = lax.dynamic_slice_in_dim(shard, place.at["core"] * half_rows, half_rows, 1)
        whole = mine[self.split_count :]
        pieces = [
            part
            for block in range(whole_count)
            for part in (whole[block, :, :half_cols], whole[block, :, half_cols:])
        ]
        piece = jnp.stack(pieces)
        if has_y:
            parts = lax.dynamic_slice_in_dim(
                mine[: self.split_count], place.at["y"] * half_cols, half_cols, 2
            )
            piece = jnp.concatenate([parts, piece])
        self.held = [piece]
        self.crossed = []

    def step_z(self):
        self.held = gather_list(self.place, self.held[0], "z")

    def step_x(self):
        self.held = gather_list(self.place, jnp.stack(self.held), "x")

    def step_y(self):
        self.held = [jnp.stack(self.held)]
        if self.split_count:
            value = self.held[0][:, :, : self.split_count]
            self.held.append(self.place.take(value, "y", 1))
        self.crossed = [self.place.take(self.held[0], "core", 1)]

    def step_core(self):
        if self.split_count:
            self.crossed.append(self.place.take(self.held[1], "core", 1))

    def whole(self):
        place, operands = self.place, self.held + self.crossed
        count_z, count_x = place.size["z"], place.size["x"]
        where = jnp.stack([place.at[name] for name in ("z", "x", "y", "core")]).astype(jnp.int32)

        def piece_at(z, x, where):
            return (
                lax.rem(x - where[1] + count_x, count_x),
                lax.rem(z - where[0] + count_z, count_z),
                0,
                0,
                0,
            )

        out = call(
            functools.partial(
                assemble_kernel, self.split_count, self.count - self.split_count, self.split_count > 0
            ),
            (count_z, count_x),
            [pl.BlockSpec((1, 1) + value.shape[2:], piece_at) for value in operands],
            pl.BlockSpec(
                (self.count, 1, self.rows, BLK), lambda z, x, where: (0, z * count_x + x, 0, 0)
            ),
            shaped((self.count, count_z * count_x, self.rows, BLK), BF16),
            prefetch=1,
            cost=9.0,
            name="assemble",
        )(where, *operands)
        return out.reshape(self.count, BLK, BLK)


def call(body, grid, in_specs, out_specs, out_shape, scratch=(), prefetch=0, cost=1.0, name=None):
    return pl.pallas_call(
        body,
        grid_spec=pltpu.PrefetchScalarGridSpec(
            num_scalar_prefetch=prefetch,
            grid=grid,
            in_specs=in_specs,
            out_specs=out_specs,
            scratch_shapes=list(scratch),
        ),
        out_shape=out_shape,
        compiler_params=pltpu.CompilerParams(vmem_limit_bytes=VMEM_BYTES),
        cost_estimate=pl.CostEstimate(flops=int(cost * 1e9), bytes_accessed=0, transcendentals=0),
        name=name,
    )


def shaped(shape, dtype):
    return jax.ShapeDtypeStruct(shape, dtype)


def fixed(shape):
    return pl.BlockSpec(shape, lambda *at: (0,) * len(shape))


def norm_stats(summed):
    average = jnp.mean(summed, axis=-1, keepdims=True)
    centred = summed - average
    variance = jnp.mean(centred * centred, axis=-1, keepdims=True)
    scale = lax.rsqrt(variance + EPS_NORM)
    return centred * scale, scale


def norm_back(grad, normed, scale, gain):
    flow = grad * gain
    return (
        flow
        - jnp.mean(flow, axis=-1, keepdims=True)
        - normed * jnp.mean(flow * normed, axis=-1, keepdims=True)
    ) * scale


def project_kernel(x_low, weight, bias, query, keyval):
    value = (dot(x_low[...], weight[0]) + bias[0]).astype(BF16)

    @pl.when(pl.program_id(0) == 0)
    def _():
        query[...] = value

    @pl.when(pl.program_id(0) > 0)
    def _():
        keyval[...] = value


def project(x_low, w_in, bias):
    tokens = x_low.shape[0]
    return call(
        project_kernel,
        (3,),
        [
            fixed((tokens, D)),
            pl.BlockSpec((1, BLK, BLK), lambda i: (i, 0, 0)),
            pl.BlockSpec((1, 1, D), lambda i: (i, 0, 0)),
        ],
        [fixed((tokens, D)), pl.BlockSpec((tokens, D), lambda i: (0, jnp.maximum(i - 1, 0)))],
        [shaped((tokens, D), BF16), shaped((tokens, 2 * D), BF16)],
        cost=6.0,
        name="project",
    )(x_low, w_in, bias)


def head_probs(query_h, keys_h, masks):
    scores = [
        dot_t(key, query_h) * HEAD_DIM ** (-0.5) + mask for key, mask in zip(keys_h, masks)
    ]
    peak = functools.reduce(
        jnp.maximum, [jnp.max(score, axis=0, keepdims=True) for score in scores]
    )
    scores = [jnp.exp(score - peak) for score in scores]
    total = sum(jnp.sum(score, axis=0, keepdims=True) for score in scores)
    inverse = 1.0 / total
    return [score * inverse for score in scores]


def dot_tt(left, right):
    return lax.dot_general(left, right, (((0,), (0,)), ((), ())), preferred_element_type=F32)


def head_of(ref, head):
    return ref[:, pl.ds(head * HEAD_DIM, HEAD_DIM)]


def attend_kernel(count, tokens, query, mask, *refs):
    keys, values, out = refs[:count], refs[count : 2 * count], refs[-1]
    masks = [mask[pl.ds(spot * tokens, tokens), :] for spot in range(count)]
    mixed = []
    for head in range(2):
        probs = head_probs(head_of(query, head), [head_of(key, head) for key in keys], masks)
        mixed.append(
            sum(dot_tt(head_of(value, head), prob.astype(BF16)) for value, prob in zip(values, probs))
        )
    out[...] = jnp.concatenate(mixed, axis=0).T.astype(BF16)


def pair_specs(tokens, count):
    pair = 2 * HEAD_DIM
    half = D // pair
    return (
        [pl.BlockSpec((tokens, pair), lambda i: (0, i))] * count
        + [pl.BlockSpec((tokens, pair), lambda i: (0, half + i))] * count
    )


def attend(query, keyvals, mask):
    tokens = query.shape[0]
    count = len(keyvals)
    pair = 2 * HEAD_DIM
    return call(
        functools.partial(attend_kernel, count, tokens),
        (D // pair,),
        [pl.BlockSpec((tokens, pair), lambda i: (0, i)), fixed(mask.shape)]
        + pair_specs(tokens, count),
        pl.BlockSpec((tokens, pair), lambda i: (0, i)),
        shaped((tokens, D), BF16),
        cost=14.0,
        name="attend",
    )(query, mask, *keyvals, *keyvals)


def attend_back_kernel(count, count_y, tokens, query, grad, mask, *refs):
    keys, values = refs[:count], refs[count : 2 * count]
    grad_q, mine, other = refs[2 * count :]
    masks = [mask[pl.ds(spot * tokens, tokens), :] for spot in range(count)]
    scale = HEAD_DIM ** (-0.5)
    grads_q = []
    grads_k = [[] for _ in range(count)]
    grads_v = [[] for _ in range(count)]
    for head in range(2):
        query_h = head_of(query, head)
        grad_h = head_of(grad, head)
        keys_h = [head_of(key, head) for key in keys]
        probs = head_probs(query_h, keys_h, masks)
        grad_probs = [dot_t(head_of(value, head), grad_h) for value in values]
        inner = sum(
            jnp.sum(prob * grad_prob, axis=0, keepdims=True)
            for prob, grad_prob in zip(probs, grad_probs)
        )
        flow_q = 0.0
        for spot in range(count):
            grad_score = (probs[spot] * (grad_probs[spot] - inner)).astype(BF16)
            flow_q = flow_q + dot_tt(keys_h[spot], grad_score)
            grads_k[spot].append(dot(grad_score, query_h) * scale)
            grads_v[spot].append(dot(probs[spot].astype(BF16), grad_h))
        grads_q.append(flow_q * scale)
    grad_q[...] = jnp.concatenate(grads_q, axis=0).T.astype(BF16)
    for spot in range(count):
        out = mine if spot < count_y else other
        out[0, spot % count_y] = jnp.concatenate(grads_k[spot], axis=1).astype(BF16)
        out[1, spot % count_y] = jnp.concatenate(grads_v[spot], axis=1).astype(BF16)


def attend_back(query, keyvals, grad, mask):
    tokens = query.shape[0]
    count = len(keyvals)
    count_y = count // CORES
    pair = 2 * HEAD_DIM
    part = pl.BlockSpec((2, count_y, tokens, pair), lambda i: (0, 0, 0, i))
    return call(
        functools.partial(attend_back_kernel, count, count_y, tokens),
        (D // pair,),
        [pl.BlockSpec((tokens, pair), lambda i: (0, i))] * 2
        + [fixed(mask.shape)]
        + pair_specs(tokens, count),
        [pl.BlockSpec((tokens, pair), lambda i: (0, i)), part, part],
        [shaped((tokens, D), BF16)] + [shaped((2, count_y, tokens, D), BF16)] * 2,
        cost=21.0,
        name="attend_back",
    )(query, grad, mask, *keyvals, *keyvals)


def mix_kernel(attn, weight, carried, vecs, summed, middle, middle_low):
    value = carried[...].astype(F32) + (dot(attn[...], weight[0]) + vecs[0:1, :])
    summed[...] = value
    normed, _ = norm_stats(value)
    value = normed * vecs[1:2, :] + vecs[2:3, :]
    middle[...] = value
    middle_low[...] = value.astype(BF16)


def mix(attn, w_in, carried, vecs):
    tokens = attn.shape[0]
    full = fixed((tokens, D))
    return call(
        mix_kernel,
        (1,),
        [full, pl.BlockSpec((1, BLK, BLK), lambda i: (3, 0, 0)), full, fixed(vecs.shape)],
        [full, full, full],
        [shaped((tokens, D), F32), shaped((tokens, D), F32), shaped((tokens, D), BF16)],
        cost=4.0,
        name="mix",
    )(attn, w_in, carried, vecs)


def erf_part(hidden):
    return (1.0 + lax.erf(hidden * (0.5**0.5))) * 0.5


def up_kernel(middle_low, weight, bias, hidden, act):
    value = dot(middle_low[...], weight[0]) + bias[0]
    hidden[...] = value
    act[...] = (value * erf_part(value)).astype(BF16)


def up(middle_low, w_up, bias):
    tokens = middle_low.shape[0]
    part = pl.BlockSpec((tokens, BLK), lambda i: (0, i))
    return call(
        up_kernel,
        (FF // BLK,),
        [
            fixed((tokens, D)),
            pl.BlockSpec((1, BLK, BLK), lambda i: (i, 0, 0)),
            pl.BlockSpec((1, 1, BLK), lambda i: (i, 0, 0)),
        ],
        [part, part],
        [shaped((tokens, FF), F32), shaped((tokens, FF), BF16)],
        cost=8.0,
        name="up",
    )(middle_low, w_up, bias)


def down_kernel(act, weight, middle, vecs, summed, result, result_low, total):
    spot = pl.program_id(0)
    value = dot(act[...], weight[0])

    @pl.when(spot == 0)
    def _():
        total[...] = value

    @pl.when(spot > 0)
    def _():
        total[...] += value

    @pl.when(spot == pl.num_programs(0) - 1)
    def _():
        value = middle[...] + (total[...] + vecs[0:1, :])
        summed[...] = value
        normed, _ = norm_stats(value)
        value = normed * vecs[1:2, :] + vecs[2:3, :]
        result[...] = value
        result_low[...] = value.astype(BF16)


def down(act, w_down, middle, vecs):
    tokens = act.shape[0]
    full = fixed((tokens, D))
    return call(
        down_kernel,
        (FF // BLK,),
        [
            pl.BlockSpec((tokens, BLK), lambda i: (0, i)),
            pl.BlockSpec((1, BLK, BLK), lambda i: (i, 0, 0)),
            full,
            fixed(vecs.shape),
        ],
        [full, full, full],
        [shaped((tokens, D), F32), shaped((tokens, D), F32), shaped((tokens, D), BF16)],
        scratch=[pltpu.VMEM((tokens, D), F32)],
        cost=8.0,
        name="down",
    )(act, w_down, middle, vecs)


def column_sum(value):
    return jnp.sum(value, axis=0, keepdims=True)


def close_kernel(flow, summed, gain, back_out, low_out, sums):
    grad = flow[...].astype(F32)
    normed, scale = norm_stats(summed[...])
    back = norm_back(grad, normed, scale, gain[...])
    back_out[...] = back
    low = back.astype(BF16)
    low_out[...] = low
    sums[0:1, :] = column_sum(low.astype(F32))
    sums[1:2, :] = column_sum(grad * normed)
    sums[2:3, :] = column_sum(grad)
    sums[3:8, :] = jnp.zeros((5, D), F32)


def close(flow, summed, gain):
    tokens = flow.shape[0]
    full = fixed((tokens, D))
    return call(
        close_kernel,
        (1,),
        [full, full, fixed((1, D))],
        [full, full, fixed((8, D))],
        [shaped((tokens, D), F32), shaped((tokens, D), BF16), shaped((8, D), F32)],
        cost=3.0,
        name="close",
    )(flow, summed, gain)


def feed_back_kernel(
    grad_two, ffn_low, summed_one, hidden, w_down, w_up, w_out, gain,
    hid_low, branch_low, attn_grad, grad_one, sums, bias_sums, total,
):
    spot = pl.program_id(0)

    @pl.when(spot == 0)
    def _():
        total[...] = grad_two[...]

    value = hidden[...]
    slope = erf_part(value) + value * jnp.exp(-0.5 * value * value) * ((2.0 * np.pi) ** -0.5)
    low = (dot_t(ffn_low[...], w_down[0]) * slope).astype(BF16)
    hid_low[...] = low
    bias_sums[0] = column_sum(low.astype(F32))
    total[...] += dot_t(low, w_up[0])

    @pl.when(spot == pl.num_programs(0) - 1)
    def _():
        grad = total[...]
        normed, scale = norm_stats(summed_one[...])
        back = norm_back(grad, normed, scale, gain[...])
        grad_one[...] = back
        low = back.astype(BF16)
        branch_low[...] = low
        sums[0:1, :] = column_sum(low.astype(F32))
        sums[1:2, :] = column_sum(grad * normed)
        sums[2:3, :] = column_sum(grad)
        sums[3:8, :] = jnp.zeros((5, D), F32)
        attn_grad[...] = dot_t(low, w_out[0]).astype(BF16)


def feed_back(grad_two, ffn_low, summed_one, hidden, w_down, w_up, w_in, gain):
    tokens = ffn_low.shape[0]
    full = fixed((tokens, D))
    part = pl.BlockSpec((tokens, BLK), lambda i: (0, i))
    weight = pl.BlockSpec((1, BLK, BLK), lambda i: (i, 0, 0))
    return call(
        feed_back_kernel,
        (FF // BLK,),
        [full, full, full, part, weight, weight, pl.BlockSpec((1, BLK, BLK), lambda i: (3, 0, 0)), fixed((1, D))],
        [part, full, full, full, fixed((8, D)), pl.BlockSpec((1, 1, BLK), lambda i: (i, 0, 0))],
        [
            shaped((tokens, FF), BF16),
            shaped((tokens, D), BF16),
            shaped((tokens, D), BF16),
            shaped((tokens, D), F32),
            shaped((8, D), F32),
            shaped((FF // BLK, 1, BLK), F32),
        ],
        scratch=[pltpu.VMEM((tokens, D), F32)],
        cost=15.0,
        name="feed_back",
    )(grad_two, ffn_low, summed_one, hidden, w_down, w_up, w_in, gain)


def input_back_kernel(count, grad_q, grad_one, weight, *refs):
    parts, (joined, result, sums, total) = refs[:count], refs[count:]
    spot = pl.program_id(0)

    @pl.when(spot == 0)
    def _():
        joined[...] = grad_q[...]
        total[...] = grad_one[...]

    @pl.when(spot > 0)
    def _():
        joined[...] = sum(part[0].astype(F32) for part in parts).astype(BF16)

    low = joined[...]
    sums[0] = column_sum(low.astype(F32))
    total[...] += dot_t(low, weight[0])

    @pl.when(spot == pl.num_programs(0) - 1)
    def _():
        result[...] = total[...]


def input_back(grad_q, parts, grad_one, w_in):
    tokens = grad_q.shape[0]
    full = fixed((tokens, D))
    return call(
        functools.partial(input_back_kernel, len(parts)),
        (3,),
        [full, full, pl.BlockSpec((1, BLK, BLK), lambda i: (i, 0, 0))]
        + [pl.BlockSpec((1, tokens, D), lambda i: (jnp.maximum(i - 1, 0), 0, 0))] * len(parts),
        [pl.BlockSpec((tokens, D), lambda i: (0, i)), full, pl.BlockSpec((1, 1, D), lambda i: (i, 0, 0))],
        [shaped((tokens, 3 * D), BF16), shaped((tokens, D), F32), shaped((3, 1, D), F32)],
        scratch=[pltpu.VMEM((tokens, D), F32)],
        cost=8.0,
        name="input_back",
    )(grad_q, grad_one, w_in, *parts)


def gather_list(place, value, axis):
    return [value] + [place.take(value, axis, step) for step in range(1, place.size[axis])]


def project_step(place, carried_low, w_in, vector):
    parts = vector_parts(vector)
    bias_in = jnp.stack([parts[0], jnp.zeros((D,), F32), parts[1]])[:, None]
    query, keyval = project(carried_low, w_in, bias_in)
    return query, gather_list(place, keyval, "y")


def mix_step(query, keyvals, carried, w_in, vector, mask):
    parts = vector_parts(vector)
    attn_low = attend(query, keyvals, mask)
    return attn_low, *mix(attn_low, w_in, carried, jnp.stack([parts[2], parts[4], parts[5]]))


def up_step(mid_low, w_up, vector):
    return up(mid_low, w_up, vector[8 * D :].reshape(FF // BLK, 1, BLK))


def down_step(act_low, w_down, middle, vector):
    parts = vector_parts(vector)
    return down(act_low, w_down, middle, jnp.stack([parts[3], parts[6], parts[7]]))


def sum_kernel(count_one, first_half, sizes, where, *refs):
    sets = (refs[:4], refs[4:8]) if count_one is not None else (refs[:4],)
    outs, product = refs[4 * len(sets) : -1], refs[-1]
    z_at, x_at, y_at = where[0], where[1], where[2]
    extent_z, extent_x, extent_y, rows = sizes
    spot = pl.program_id(0)

    def multiply(left_mine, left_other, right_mine, right_other):
        left = jnp.concatenate([left_mine[...], left_other[...]], axis=0)
        right = jnp.concatenate([right_mine[...], right_other[...]], axis=0)
        product[...] = dot_tt(left, right)

    if len(sets) == 1:
        multiply(*sets[0])
    else:
        pl.when(spot < count_one)(lambda: multiply(*sets[0]))
        pl.when(spot >= count_one)(lambda: multiply(*sets[1]))
    cols = product.shape[1] // extent_y

    def put(y_first):
        for step_y in range(extent_y):
            from_col = pl.multiple_of(lax.rem(y_at + step_y, extent_y) * cols, cols)
            for step_x in range(extent_x):
                for step_z in range(extent_z):
                    row_block = lax.rem(z_at + step_z, extent_z) * extent_x + lax.rem(
                        x_at + step_x, extent_x
                    )
                    from_row = pl.multiple_of(row_block * rows, rows)
                    value = product[pl.ds(from_row, rows), pl.ds(from_col, cols)].astype(BF16)
                    if y_first:
                        outs[step_y][step_x, step_z, 0] = value
                    else:
                        outs[extent_y + step_x][step_y, step_z, 0] = value

    pl.when(spot < first_half)(lambda: put(True))
    pl.when(spot >= first_half)(lambda: put(False))


def partial_sums(place, sets):
    tokens = sets[0][0].shape[0]
    extent_z, extent_x, extent_y = (place.size[name] for name in ("z", "x", "y"))
    rows = BLK // (extent_z * extent_x)
    half = BLK // CORES
    cols = half // extent_y
    where = jnp.stack([place.at[name] for name in ("z", "x", "y", "core")]).astype(jnp.int32)
    counts = [max(one[0].shape[1], one[2].shape[1]) // BLK for one in sets]
    count = sum(counts)
    first_half = count // 2
    specs = []
    start = 0
    for one, amount in zip(sets, counts):

        def at(i, start=start, amount=amount):
            return jnp.clip(i - start, 0, amount - 1)

        many_left, many_right = one[0].shape[1] > BLK, one[2].shape[1] > BLK
        specs += [
            pl.BlockSpec((tokens, BLK), lambda i, where, at=at, many=many_left: (0, at(i) if many else 0))
        ] * 2
        specs += [
            pl.BlockSpec(
                (tokens, half),
                lambda i, where, at=at, many=many_right: (0, (at(i) * CORES if many else 0) + where[3]),
            )
        ] * 2
        start += amount
    part_y = (extent_x, extent_z, 1, rows, cols)
    part_x = (extent_y, extent_z, 1, rows, cols)
    spec_y = pl.BlockSpec(part_y, lambda i, where: (0, 0, jnp.minimum(i, first_half - 1), 0, 0))
    spec_x = pl.BlockSpec(part_x, lambda i, where: (0, 0, jnp.maximum(i - first_half, 0), 0, 0))
    outs = call(
        functools.partial(
            sum_kernel,
            counts[0] if len(sets) > 1 else None,
            first_half,
            (extent_z, extent_x, extent_y, rows),
        ),
        (count,),
        specs,
        [spec_y] * extent_y + [spec_x] * extent_x,
        [shaped((extent_x, extent_z, first_half, rows, cols), BF16)] * extent_y
        + [shaped((extent_y, extent_z, count - first_half, rows, cols), BF16)] * extent_x,
        scratch=[pltpu.VMEM((BLK, half), F32)],
        prefetch=1,
        cost=8.0,
        name="partial_sums",
    )(where, *[value for one in sets for value in one])
    return outs[:extent_y], outs[extent_y:]


class Summing:
    def __init__(self, place, sets):
        self.place = place
        if (BLK // (CORES * place.size["y"])) % 128:
            self.plain = True
            self.parts = self.by_y = self.by_x = ()
            self.groups = [[sum_job_plain(place, one[0], one[2], "y")] for one in sets]
        else:
            self.plain = False
            sets = [(one[0], one[1], one[2], place.take(one[2], "core", 1)) for one in sets]
            self.parts = partial_sums(place, sets)
            self.by_y = self.by_x = ()
            self.groups = ()

    def first_y(self):
        if not self.plain:
            self.by_y = self.place.collect(self.parts[0], "y")

    def first_x(self):
        if not self.plain:
            self.by_x = self.place.collect(self.parts[1], "x")

    def second_x(self):
        if not self.plain:
            total = add_up(self.by_y)
            parts = [total[step].astype(BF16) for step in range(self.place.size["x"])]
            self.by_y = self.place.collect(parts, "x")

    def second_y(self):
        if not self.plain:
            total = add_up(self.by_x)
            parts = [total[step].astype(BF16) for step in range(self.place.size["y"])]
            self.by_x = self.place.collect(parts, "y")

    def third(self):
        if not self.plain:
            by_y, by_x = add_up(self.by_y), add_up(self.by_x)
            both = [
                jnp.concatenate([by_y[step], by_x[step]]).astype(BF16)
                for step in range(self.place.size["z"])
            ]
            self.groups = [self.place.collect(both, "z")]


def route_kernel(groups, slots, scaling, spots, *refs):
    out, total = refs[-2:]
    refs = list(refs[:-2])
    at = 0
    for addends in groups:
        parts = [refs.pop(0) for _ in range(addends)]
        for block in range(parts[0].shape[0]):
            value = sum(part[block].astype(F32) for part in parts)
            total[at] = (value * scaling).astype(BF16)
            at += 1
    total[at] = jnp.zeros(total.shape[1:], BF16)
    for ctx in range(out.shape[0]):
        for spot in range(out.shape[1]):
            if spot < slots:
                out[ctx, spot] = total[spots[ctx * slots + spot]]
            else:
                out[ctx, spot] = total[at]


def route(groups, spots, slots, wsh_count, scaling):
    rows, cols = groups[0][0].shape[1:]
    blocks = sum(addends[0].shape[0] for addends in groups)
    flat = [value for addends in groups for value in addends]
    shape = (spots.shape[0] // slots, wsh_count, rows, cols)
    return call(
        functools.partial(route_kernel, [len(addends) for addends in groups], slots, scaling),
        (1,),
        [fixed(value.shape) for value in flat],
        fixed(shape),
        shaped(shape, BF16),
        scratch=[pltpu.VMEM((blocks + 1, rows, cols), BF16)],
        prefetch=1,
        cost=6.0,
        name="route",
    )(spots, *flat)


def rotate_kernel(quarters, where, grads, right, left, first, second, rotated, update, total, low, right_low):
    step = BLK // 4
    right_low[...] = right[0].astype(BF16)
    for at in range(4):
        rows = pl.ds(at * step, step)
        product = 0.0
        for source, quarter in enumerate(quarters):
            width = grads.shape[2]
            product = product + dot(
                grads[source, rows, :], right_low[pl.ds(quarter * width, width), :]
            )
        value = dot_tt(left[rows, :], product.astype(BF16))
        if at:
            total[...] += value
        else:
            total[...] = value
    for at in range(4):
        rows = pl.ds(at * step, step)
        turned = total[rows, :]
        rotated[rows, :] = turned.astype(BF16)
        first_new = DECAY_RATE * first[rows, :].astype(F32) + (1.0 - DECAY_RATE) * turned
        second_new = DECAY_RATE * second[rows, :].astype(F32) + (1.0 - DECAY_RATE) * turned * turned
        direction = first_new / (jnp.sqrt(second_new) + EPS_ADAM)
        low[rows, :] = dot_t(direction.astype(BF16), right_low[...]).astype(BF16)
    for at in range(4):
        rows = pl.ds(at * step, step)
        update[rows, :] = dot(left[rows, :], low[...]).astype(BF16)


def rotate(grads, quarters, right_bases, slot, left, first, second):
    full = fixed((BLK, BLK))
    return call(
        functools.partial(rotate_kernel, quarters),
        (1,),
        [
            fixed(grads.shape),
            pl.BlockSpec((1, BLK, BLK), lambda i, where: (where[0], 0, 0)),
            full,
            full,
            full,
        ],
        [full, full],
        [shaped((BLK, BLK), BF16)] * 2,
        scratch=[pltpu.VMEM((BLK, BLK), F32), pltpu.VMEM((BLK, BLK), BF16), pltpu.VMEM((BLK, BLK), BF16)],
        prefetch=1,
        cost=16.0,
        name="rotate",
    )(slot, grads, right_bases, left, first, second)


def pick_kernel(count, table, *refs):
    parts, out = refs[:count], refs[count]
    block = pl.program_id(0)

    def put(part):
        out[0] = parts[part][table[1, block]]

    for part in range(count):
        pl.when(table[0, block] == part)(functools.partial(put, part))


def pick(parts, table):
    blocks = table.shape[1]
    shape = (blocks,) + parts[0].shape[1:]
    return call(
        functools.partial(pick_kernel, len(parts)),
        (blocks,),
        [fixed(value.shape) for value in parts],
        pl.BlockSpec((1,) + shape[1:], lambda i, table: (i, 0, 0)),
        shaped(shape, BF16),
        prefetch=1,
        cost=12.0,
        name="pick",
    )(table, *parts)


def left_order(place, left):
    tokens, cols = left.shape
    count_z, count_x = place.size["z"], place.size["x"]
    blocks = cols // BLK
    rows = BLK // (count_z * count_x)
    value = left.reshape(tokens, blocks, count_z, count_x, rows)
    value = jnp.roll(value, (-place.at["z"], -place.at["x"]), axis=(2, 3))
    return value.transpose(0, 3, 2, 1, 4).reshape(tokens, cols)


def right_halves(place, right):
    tokens, cols = right.shape
    count_y = place.size["y"]
    width = BLK // (CORES * count_y)
    value = right.reshape(tokens, cols // BLK, CORES, count_y, width)
    halves = []
    for step in range(CORES):
        half = lax.dynamic_index_in_dim(value, (place.at["core"] + step) % CORES, 2, False)
        half = jnp.roll(half, -place.at["y"], axis=2)
        halves.append(half.transpose(2, 0, 1, 3).reshape(count_y, tokens, -1))
    return halves


def sum_job_plain(place, left, right, first):
    count_z, count_x, count_y = place.size["z"], place.size["x"], place.size["y"]
    left = left_order(place, left)
    right_mine, right_other = right_halves(place, right)
    left_both = jnp.concatenate([left, place.take(left, "core", 1)], axis=0)
    right_both = jnp.concatenate([right_mine, place.take(right_other, "core", 1)], axis=1)
    partial = [
        lax.dot_general(left_both, right_both[step], (((0,), (0,)), ((), ())), preferred_element_type=F32)
        .astype(BF16)
        .reshape(count_x, count_z, -1, right_both.shape[2])
        for step in range(count_y)
    ]
    if first == "y":
        total = place.scatter(partial, "y").astype(BF16)
        total = place.scatter(total, "x").astype(BF16)
    else:
        parts = [[value[step] for value in partial] for step in range(count_x)]
        parts = [jnp.stack(part) for part in parts]
        total = place.scatter(parts, "x").astype(BF16)
        total = place.scatter(total, "y").astype(BF16)
    total = place.scatter(total, "z")
    rows = BLK // (count_z * count_x)
    width = BLK // (CORES * count_y)
    if left.shape[1] > BLK:
        return total.reshape(-1, rows, width)
    return total.reshape(rows, -1, width).transpose(1, 0, 2)


def sum_everywhere(place, value):
    if place.size["y"] != 2 or place.size["x"] != 2:
        return lax.psum(value, ("ctx", "wsh"))
    for axis in ("core", "y", "x"):
        value = value + place.take(value, axis, 1)
    pairs = place.size["x"]
    for bit in (1, 2):
        swap = [
            (z * pairs + x, (z ^ bit) * pairs + x) for z in range(DEPTH_Z) for x in range(pairs)
        ]
        value = value + lax.ppermute(value, "wsh", swap)
    return value


def doc_ids(lengths, position):
    starts = jnp.cumsum(lengths) - lengths
    return jnp.sum((position[:, None] >= starts[None, :]).astype(jnp.int32), axis=1)


def to_owner(rows_value, wsh_count):
    slots = rows_value.shape[0]
    padded = jnp.pad(rows_value.astype(BF16), ((0, wsh_count - slots), (0, 0), (0, 0)))
    return lax.all_to_all(padded, "wsh", 0, 0, tiled=True).reshape(BLK, BLK)


def from_owner(whole, wsh_count, slots):
    cut = whole.astype(BF16).reshape(wsh_count, BLK // wsh_count, BLK)
    return lax.all_to_all(cut, "wsh", 0, 0, tiled=True)[:slots]


def on_device(
    stream_in,
    doc_lengths,
    cotangent,
    weights,
    vec_params,
    owner_slots,
    master,
    left_bases,
    right_bases,
    moment1,
    moment2,
    vec_moment1,
    vec_moment2,
):
    tokens = stream_in.shape[1]
    ctx_count = lax.axis_size("ctx")
    wsh_count = lax.axis_size("wsh")
    place = Place(ctx_count, wsh_count)
    seq_len = tokens * ctx_count
    scaling = (wsh_count * seq_len) ** (-0.5)
    slots_dev, rows_dev = master.shape[0], master.shape[1]
    slot_total = ctx_count * slots_dev
    count_y = place.size["y"]
    width = BLK // ctx_count

    core_of = (place.at["core"] + jnp.arange(CORES)) % CORES
    y_of = (place.at["y"] + jnp.arange(count_y)) % count_y
    ctx_of = (y_of[None, :] * CORES + core_of[:, None]).reshape(-1)
    key_pos = (ctx_of[:, None] * tokens + jnp.arange(tokens)[None, :]).reshape(-1)
    doc_keys = doc_ids(doc_lengths[0], key_pos)
    mask = jnp.where(doc_keys[:, None] == doc_keys[None, :tokens], 0.0, -1e30).astype(F32)

    chunks = [
        Gathering(place, weights[layer_at, first : first + 4])
        for layer_at in range(LAYERS)
        for first in range(0, NBLK, 4)
    ]

    live = {}

    def settle():
        state = [(chunk.held, chunk.crossed) for chunk in chunks]
        state, values = together(state, {name: live[name] for name in live})
        for chunk, (held, crossed) in zip(chunks, state):
            chunk.held, chunk.crossed = held, crossed
        live.update(values)

    def finish(spot):
        chunks[spot].step_core()
        whole = chunks[spot].whole()
        chunks[spot].held = chunks[spot].crossed = []
        return whole

    def keyvals_of(layer_at):
        keyvals = live[f"keyvals{layer_at}"]
        return keyvals + [place.take(value, "core", 1) for value in keyvals]

    kept = [{}, {}]
    chunks[0].step_z()
    settle()
    chunks[0].step_x()
    chunks[1].step_z()
    settle()
    chunks[0].step_y()
    chunks[1].step_x()
    chunks[2].step_z()
    settle()
    chunks[1].step_y()
    chunks[2].step_x()
    chunks[3].step_z()
    w_in_0 = finish(0)
    query_0, live["keyvals0"] = project_step(place, stream_in[0], w_in_0, vec_params[0])
    live["query"] = query_0
    settle()
    chunks[2].step_y()
    chunks[3].step_x()
    chunks[4].step_z()
    keyvals_0 = keyvals_of(0)
    query_0 = live["query"]
    attn_0, summed_one_0, middle_0, mid_low_0 = mix_step(
        query_0, keyvals_0, stream_in[0], w_in_0, vec_params[0], mask
    )
    w_up_0 = finish(1)
    hidden_0, live["act"] = up_step(mid_low_0, w_up_0, vec_params[0])
    settle()
    chunks[3].step_y()
    chunks[4].step_x()
    chunks[5].step_z()
    act_0 = live["act"]
    w_down_0 = finish(2)
    summed_two_0, live["result"], live["result_low"] = down_step(
        act_0, w_down_0, middle_0, vec_params[0]
    )
    settle()
    chunks[4].step_y()
    chunks[5].step_x()
    result_0, result_low_0 = live["result"], live["result_low"]
    w_in_1 = finish(3)
    query_1, live["keyvals1"] = project_step(place, result_low_0, w_in_1, vec_params[1])
    live["query"] = query_1
    live["own"] = left_bases
    settle()
    chunks[5].step_y()
    live["own"] = to_owner(live["own"], wsh_count)
    keyvals_1 = keyvals_of(1)
    query_1 = live["query"]
    attn_1, summed_one_1, middle_1, mid_low_1 = mix_step(
        query_1, keyvals_1, result_0, w_in_1, vec_params[1], mask
    )
    w_up_1 = finish(4)
    hidden_1, live["act"] = up_step(mid_low_1, w_up_1, vec_params[1])
    live["first"] = moment1
    settle()
    left_own = live["own"]
    first_own = to_owner(live["first"], wsh_count)
    act_1 = live["act"]
    w_down_1 = finish(5)
    summed_two_1, _, result_low_1 = down_step(act_1, w_down_1, middle_1, vec_params[1])
    stream_out = result_low_1[None]

    blocks = [(w_in_0, w_up_0, w_down_0), (w_in_1, w_up_1, w_down_1)]
    lefts = [
        (stream_in[0], attn_0, mid_low_0, act_0),
        (result_low_0, attn_1, mid_low_1, act_1),
    ]
    crossed = [[place.take(value, "core", 1) for value in values] for values in lefts]
    summed = [(summed_one_0, summed_two_0), (summed_one_1, summed_two_1)]
    hidden = [hidden_0, hidden_1]
    queries = [query_0, query_1]
    keyvals_all = [keyvals_0, keyvals_1]
    gains = [
        (vec_params[layer_at][None, 4 * D : 5 * D], vec_params[layer_at][None, 6 * D : 7 * D])
        for layer_at in range(LAYERS)
    ]
    live = {}
    jobs = []
    vec_terms = [None] * LAYERS

    def settle_back():
        state = [(job.parts, job.by_y, job.by_x, job.groups) for job in jobs]
        state, values = together(state, dict(live))
        for job, fields in zip(jobs, state):
            job.parts, job.by_y, job.by_x, job.groups = fields
        live.update(values)

    def begin(layer_at, *sets):
        jobs.append(
            Summing(place, [(lefts[layer_at][spot], crossed[layer_at][spot], right) for spot, right in sets])
        )
        return jobs[-1]

    def close_step(layer_at, flow):
        live["two"], live["ffn"], live["sums_two"] = close(flow, summed[layer_at][1], gains[layer_at][1])
        return begin(layer_at, (3, live["ffn"]))

    def feed_step(layer_at):
        w_in, w_up, w_down = blocks[layer_at]
        hid_low, live["branch"], attn_grad, live["one"], live["sums_one"], live["sums_up"] = feed_back(
            live["two"], live["ffn"], summed[layer_at][0], hidden[layer_at], w_down, w_up, w_in, gains[layer_at][0]
        )
        live["attn_grad"] = attn_grad
        return begin(layer_at, (2, hid_low))

    def attend_step(layer_at):
        live["grad_q"], mine, other = attend_back(
            queries[layer_at], keyvals_all[layer_at], live["attn_grad"], mask
        )
        live["pair"] = [mine, place.take(other, "core", 1)]

    def send_step():
        mine, arrived = live["pair"]
        sums = [mine[:, step].astype(F32) + arrived[:, step].astype(F32) for step in range(count_y)]
        live["kv"] = [sums[0]] + [
            place.take(sums[step].astype(BF16), "y", -step) for step in range(1, count_y)
        ]

    def input_step(layer_at):
        joined, grad_x, in_sums = input_back(live["grad_q"], live["kv"], live["one"], blocks[layer_at][0])
        sums_two, sums_one = live["sums_two"], live["sums_one"]
        vec_terms[layer_at] = jnp.concatenate(
            [
                in_sums[0, 0],
                in_sums[2, 0],
                sums_one[0],
                sums_two[0],
                sums_one[1:3].reshape(-1),
                sums_two[1:3].reshape(-1),
                live["sums_up"].reshape(-1),
            ]
        )
        return grad_x, begin(layer_at, (0, joined), (1, live["branch"]))

    down_1 = close_step(1, cotangent[0])
    settle_back()
    down_1.first_y()
    down_1.first_x()
    live["first"] = first_own
    live["second"] = moment2
    up_1 = feed_step(1)
    settle_back()
    live["second"] = to_owner(live["second"], wsh_count)
    down_1.second_x()
    down_1.second_y()
    up_1.first_y()
    up_1.first_x()
    attend_step(1)
    settle_back()
    down_1.third()
    send_step()
    up_1.second_x()
    settle_back()
    up_1.second_y()
    grad_flow, in_1 = input_step(1)
    down_0 = close_step(0, grad_flow)
    settle_back()
    up_1.third()
    in_1.first_y()
    in_1.first_x()
    down_0.first_y()
    down_0.first_x()
    up_0 = feed_step(0)
    attend_step(0)
    settle_back()
    send_step()
    in_1.second_x()
    in_1.second_y()
    down_0.second_x()
    down_0.second_y()
    up_0.first_x()
    settle_back()
    in_1.third()
    down_0.third()
    up_0.first_y()
    up_0.second_y()
    grad_flow, in_0 = input_step(0)
    settle_back()
    in_0.first_y()
    in_0.first_x()
    up_0.second_x()
    settle_back()
    in_0.second_x()
    in_0.second_y()
    up_0.third()
    settle_back()
    in_0.third()
    stream_grad = grad_flow[None]
    vec_grads = sum_everywhere(place, jnp.stack(vec_terms)) * scaling
    groups = [
        group for layer_jobs in ((in_0, up_0, down_0), (in_1, up_1, down_1)) for job in layer_jobs for group in job.groups
    ]

    owner_flat = owner_slots.reshape(-1)
    block_count = LAYERS * NBLK
    picks = owner_flat[None, :] == jnp.arange(slot_total, dtype=jnp.int32)[:, None]
    spots = jnp.where(
        jnp.any(picks, axis=1), jnp.argmax(picks, axis=1).astype(jnp.int32), block_count
    )
    by_slot = route(groups, spots, slots_dev, wsh_count, scaling)

    arrived = lax.all_to_all(
        by_slot.reshape(ctx_count * wsh_count, rows_dev, width), ("ctx", "wsh"), 0, 0, tiled=True
    )
    quarters = [(source % CORES) * count_y + source // CORES for source in range(ctx_count)]
    slot_own = jnp.minimum(lax.axis_index("wsh"), slots_dev - 1).reshape(1)
    rotated_own, update_own = rotate(
        arrived.reshape(ctx_count, BLK, width), quarters, right_bases, slot_own, left_own, live["first"], live["second"]
    )

    by_rows = after(by_slot[:, :slots_dev], arrived)
    by_rows = lax.all_to_all(by_rows, "ctx", 0, 0, tiled=True)
    update_own, rotated_own, by_rows = together(update_own, rotated_own, by_rows)
    update = from_owner(update_own, wsh_count, slots_dev)
    update, rotated_own = together(update, rotated_own)
    update = update.astype(F32)
    by_rows = by_rows.reshape(count_y, CORES, slots_dev, rows_dev, width)
    block_grads = by_rows.transpose(2, 3, 1, 0, 4).reshape(slots_dev, rows_dev, BLK).astype(F32)

    new_master = master - LR_BLOCK * update
    master_low = new_master.astype(BF16)
    parts = gather_list(place, master_low, "y")
    rotated = from_owner(rotated_own, wsh_count, slots_dev)
    parts, rotated = together(parts, rotated)
    rotated = rotated.astype(F32)
    parts = parts + [place.take(value, "core", 1) for value in parts]
    owner_ctx, owner_at = owner_flat // slots_dev, owner_flat % slots_dev
    step_y = (owner_ctx // CORES - place.at["y"]) % count_y
    step_core = (owner_ctx % CORES - place.at["core"]) % CORES
    table = jnp.stack([step_core * count_y + step_y, owner_at]).astype(jnp.int32)
    new_weights = pick(parts, table).reshape(LAYERS, NBLK, rows_dev, BLK)

    new_moment1 = DECAY_RATE * moment1 + (1.0 - DECAY_RATE) * rotated
    new_moment2 = DECAY_RATE * moment2 + (1.0 - DECAY_RATE) * rotated * rotated

    new_vec_moment1 = DECAY_RATE * vec_moment1 + (1.0 - DECAY_RATE) * vec_grads
    new_vec_moment2 = DECAY_RATE * vec_moment2 + (1.0 - DECAY_RATE) * vec_grads * vec_grads
    new_vec_params = vec_params - LR_VEC * new_vec_moment1 / (jnp.sqrt(new_vec_moment2) + EPS_ADAM)
    return (
        stream_out,
        stream_grad,
        block_grads,
        new_moment1,
        new_moment2,
        new_master,
        new_weights,
        vec_grads,
        new_vec_params,
        new_vec_moment1,
        new_vec_moment2,
    )


def solution(mesh):
    rows = P("ctx", "wsh", None)
    placed = (
        P("wsh", "ctx", None),
        P("wsh", None),
        P("wsh", "ctx", None),
        P(None, None, "wsh", None),
        P(),
        P(),
        rows,
        rows,
        P("ctx", None, None),
        rows,
        rows,
        P(),
        P(),
    )
    return jax.shard_map(
        on_device,
        mesh=mesh,
        in_specs=placed,
        out_specs=(
            P("wsh", "ctx", None),
            P("wsh", "ctx", None),
            rows,
            rows,
            rows,
            rows,
            P(None, None, "wsh", None),
            P(),
            P(),
            P(),
            P(),
        ),
        check_vma=False,
    )
```

```python
import functools

import jax
import jax.numpy as jnp
import numpy as np
from jax import lax
from jax.experimental import pallas as pl
from jax.experimental.pallas import tpu as pltpu
from jax.sharding import PartitionSpec as P

D = 1024
HEADS = 16
HEAD_DIM = 64
FF = 4096
BLK = 1024
LAYERS = 2
NBLK = 12
CORES = 2
DEPTH_Z = 4

EPS_NORM = 1e-05
EPS_ADAM = 1e-08
LR_BLOCK = 0.1
LR_VEC = 0.25
DECAY_RATE = 0.5
VMEM_BYTES = 56 * 1024 * 1024
BF16 = jnp.bfloat16
F32 = jnp.float32


class Place:
    def __init__(self, ctx_count, wsh_count):
        self.size = {
            "core": CORES,
            "y": ctx_count // CORES,
            "z": DEPTH_Z,
            "x": wsh_count // DEPTH_Z,
        }
        ctx_at = lax.axis_index("ctx")
        wsh_at = lax.axis_index("wsh")
        self.at = {
            "core": ctx_at % CORES,
            "y": ctx_at // CORES,
            "z": wsh_at // self.size["x"],
            "x": wsh_at % self.size["x"],
        }

    def take(self, value, axis, step):
        name, slow, fast = {
            "core": ("ctx", "y", "core"),
            "y": ("ctx", "y", "core"),
            "z": ("wsh", "z", "x"),
            "x": ("wsh", "z", "x"),
        }[axis]
        extent = self.size[axis]
        pairs = []
        for slow_at in range(self.size[slow]):
            for fast_at in range(self.size[fast]):
                if axis == fast:
                    other = (slow_at, (fast_at + step) % extent)
                else:
                    other = ((slow_at + step) % extent, fast_at)
                pairs.append(
                    (
                        other[0] * self.size[fast] + other[1],
                        slow_at * self.size[fast] + fast_at,
                    )
                )
        return lax.ppermute(value, name, pairs)

    def gather(self, value, axis):
        steps = range(1, self.size[axis])
        return jnp.stack([value] + [self.take(value, axis, step) for step in steps])

    def collect(self, values, axis):
        steps = range(1, self.size[axis])
        return [values[0]] + [self.take(values[step], axis, -step) for step in steps]

    def swap_z(self, values):
        count_x = self.size["x"]
        lines = [[z * count_x + x for z in range(self.size["z"])] for x in range(count_x)]
        return lax.all_to_all(values, "wsh", 0, 0, tiled=True, axis_index_groups=lines)

    def scatter(self, values, axis):
        total = values[0].astype(F32)
        for step in range(1, self.size[axis]):
            total = total + self.take(values[step], axis, -step).astype(F32)
        return total


def vector_parts(vector):
    pieces = [vector[spot * D : (spot + 1) * D] for spot in range(8)]
    return pieces + [vector[8 * D :]]


def dot(left, right):
    return jnp.dot(left, right, preferred_element_type=F32)


def dot_t(left, right):
    return lax.dot_general(left, right, (((1,), (1,)), ((), ())), preferred_element_type=F32)


def after(value, *others):
    return lax.optimization_barrier((value,) + others)[0]


def together(*values):
    return lax.optimization_barrier(values)


def add_up(values):
    return sum(value.astype(F32) for value in values)


class Gathering:
    def __init__(self, place, shard):
        self.place = place
        self.count, self.rows, _ = shard.shape
        half_rows, half_cols = self.rows // 2, BLK // 2
        has_y = place.size["y"] == 2
        self.split_count = self.count // 2 if has_y else 0
        whole_count = self.count - self.split_count
        mine = lax.dynamic_slice_in_dim(shard, place.at["core"] * half_rows, half_rows, 1)
        whole = mine[self.split_count :]
        pieces = [
            part
            for block in range(whole_count)
            for part in (whole[block, :, :half_cols], whole[block, :, half_cols:])
        ]
        piece = jnp.stack(pieces)
        if has_y:
            parts = lax.dynamic_slice_in_dim(
                mine[: self.split_count], place.at["y"] * half_cols, half_cols, 2
            )
            piece = jnp.concatenate([parts, piece])
        self.held = [piece]
        self.crossed = []

    def step_z(self):
        piece = self.held[0]
        copies = jnp.broadcast_to(piece[None], (self.place.size["z"],) + piece.shape)
        self.held = [self.place.swap_z(copies)]

    def step_x(self):
        self.held = gather_list(self.place, self.held[0], "x")

    def step_y(self):
        self.held = [jnp.stack(self.held)]
        if self.split_count:
            value = self.held[0][:, :, : self.split_count]
            self.held.append(self.place.take(value, "y", 1))
        self.crossed = [self.place.take(self.held[0], "core", 1)]

    def step_core(self):
        if self.split_count:
            self.crossed.append(self.place.take(self.held[1], "core", 1))

    def pieces(self):
        split, mine, crossed = self.split_count, self.held, self.crossed
        part = (mine[0].shape[:2]) + (1,) + mine[0].shape[3:]

        def spec(place_of):
            return pl.BlockSpec(part, lambda i, where: (0, 0, place_of(i), 0, 0))

        low = spec(lambda i: jnp.where(i < split, i, 2 * i - split))
        high = spec(lambda i: jnp.where(i < split, split + 1, 2 * i - split + 1))
        operands = [mine[0], crossed[0], mine[0], crossed[0]]
        specs = [low, low, high, high]
        if split:
            operands += [mine[1], crossed[1]]
            specs += [spec(lambda i: jnp.minimum(i, split - 1))] * 2
        return operands, specs

    def where(self):
        return jnp.stack([self.place.at[name] for name in ("x", "y", "core")]).astype(jnp.int32)


def open_block(split, where, pieces, out):
    spot = pl.program_id(0)
    extent_x, extent_z, _, half_rows, half_cols = pieces[0].shape
    x_at, y_at, core_at = where[0], where[1], where[2]

    def put(first_col, sources):
        low_col = pl.ds(pl.multiple_of(first_col * half_cols, half_cols), half_cols)
        high_col = pl.ds(pl.multiple_of((1 - first_col) * half_cols, half_cols), half_cols)
        for step_x in range(extent_x):
            for z in range(extent_z):
                base = (z * extent_x + lax.rem(x_at + step_x, extent_x)) * 2
                mine = pl.ds(pl.multiple_of((base + core_at) * half_rows, half_rows), half_rows)
                other = pl.ds(pl.multiple_of((base + 1 - core_at) * half_rows, half_rows), half_rows)
                out[0, mine, low_col] = sources[0][step_x, z, 0]
                out[0, other, low_col] = sources[1][step_x, z, 0]
                out[0, mine, high_col] = sources[2][step_x, z, 0]
                out[0, other, high_col] = sources[3][step_x, z, 0]

    if split:
        pl.when(spot < split)(lambda: put(y_at, list(pieces[:2]) + list(pieces[4:])))
        pl.when(spot >= split)(lambda: put(0, pieces[:4]))
    else:
        put(0, pieces[:4])


def call(body, grid, in_specs, out_specs, out_shape, scratch=(), prefetch=0, cost=1.0, name=None):
    return pl.pallas_call(
        body,
        grid_spec=pltpu.PrefetchScalarGridSpec(
            num_scalar_prefetch=prefetch,
            grid=grid,
            in_specs=in_specs,
            out_specs=out_specs,
            scratch_shapes=list(scratch),
        ),
        out_shape=out_shape,
        compiler_params=pltpu.CompilerParams(vmem_limit_bytes=VMEM_BYTES),
        cost_estimate=pl.CostEstimate(flops=int(cost * 2e7), bytes_accessed=0, transcendentals=0),
        name=name,
    )


def shaped(shape, dtype):
    return jax.ShapeDtypeStruct(shape, dtype)


def fixed(shape):
    return pl.BlockSpec(shape, lambda *at: (0,) * len(shape))


def norm_stats(summed):
    average = jnp.mean(summed, axis=-1, keepdims=True)
    centred = summed - average
    variance = jnp.mean(centred * centred, axis=-1, keepdims=True)
    scale = lax.rsqrt(variance + EPS_NORM)
    return centred * scale, scale


def norm_back(grad, normed, scale, gain):
    flow = grad * gain
    return (
        flow
        - jnp.mean(flow, axis=-1, keepdims=True)
        - normed * jnp.mean(flow * normed, axis=-1, keepdims=True)
    ) * scale


BLOCK = pl.BlockSpec((1, BLK, BLK), lambda i, *at: (i, 0, 0))
BLOCKS = jax.ShapeDtypeStruct((4, BLK, BLK), BF16)


def project_kernel(split, where, x_low, bias, *refs):
    pieces, (query, keyval, weight) = refs[:-3], refs[-3:]
    open_block(split, where, pieces, weight)

    def value():
        return (dot(x_low[...], weight[0]) + bias[0]).astype(BF16)

    @pl.when(pl.program_id(0) == 0)
    def _():
        query[...] = value()

    @pl.when((pl.program_id(0) > 0) & (pl.program_id(0) < 3))
    def _():
        keyval[...] = value()


def project(x_low, chunk, bias):
    tokens = x_low.shape[0]
    pieces, specs = chunk.pieces()
    return call(
        functools.partial(project_kernel, chunk.split_count),
        (4,),
        [fixed((tokens, D)), pl.BlockSpec((1, 1, D), lambda i, where: (jnp.minimum(i, 2), 0, 0))] + specs,
        [
            fixed((tokens, D)),
            pl.BlockSpec((tokens, D), lambda i, where: (0, jnp.clip(i - 1, 0, 1))),
            BLOCK,
        ],
        [shaped((tokens, D), BF16), shaped((tokens, 2 * D), BF16), BLOCKS],
        prefetch=1,
        cost=8.0,
        name="project",
    )(chunk.where(), x_low, bias, *pieces)


def head_probs(query_h, keys_h, masks):
    scores = [
        dot_t(key, query_h) * HEAD_DIM ** (-0.5) + mask for key, mask in zip(keys_h, masks)
    ]
    peak = functools.reduce(
        jnp.maximum, [jnp.max(score, axis=0, keepdims=True) for score in scores]
    )
    scores = [jnp.exp(score - peak) for score in scores]
    total = sum(jnp.sum(score, axis=0, keepdims=True) for score in scores)
    inverse = 1.0 / total
    return [score * inverse for score in scores]


def dot_tt(left, right):
    return lax.dot_general(left, right, (((0,), (0,)), ((), ())), preferred_element_type=F32)


def head_of(ref, head):
    return ref[:, pl.ds(head * HEAD_DIM, HEAD_DIM)]


def attend_kernel(count, tokens, query, mask, *refs):
    keys, values, out = refs[:count], refs[count : 2 * count], refs[-1]
    masks = [mask[pl.ds(spot * tokens, tokens), :] for spot in range(count)]
    mixed = []
    for head in range(2):
        probs = head_probs(head_of(query, head), [head_of(key, head) for key in keys], masks)
        mixed.append(
            sum(dot_tt(head_of(value, head), prob.astype(BF16)) for value, prob in zip(values, probs))
        )
    out[...] = jnp.concatenate(mixed, axis=0).T.astype(BF16)


def pair_specs(tokens, count):
    pair = 2 * HEAD_DIM
    half = D // pair
    return (
        [pl.BlockSpec((tokens, pair), lambda i: (0, i))] * count
        + [pl.BlockSpec((tokens, pair), lambda i: (0, half + i))] * count
    )


def attend(query, keyvals, mask):
    tokens = query.shape[0]
    count = len(keyvals)
    pair = 2 * HEAD_DIM
    return call(
        functools.partial(attend_kernel, count, tokens),
        (D // pair,),
        [pl.BlockSpec((tokens, pair), lambda i: (0, i)), fixed(mask.shape)]
        + pair_specs(tokens, count),
        pl.BlockSpec((tokens, pair), lambda i: (0, i)),
        shaped((tokens, D), BF16),
        cost=14.0,
        name="attend",
    )(query, mask, *keyvals, *keyvals)


def attend_back_kernel(count, count_y, tokens, query, grad, mask, *refs):
    keys, values = refs[:count], refs[count : 2 * count]
    grad_q, mine, other = refs[2 * count :]
    masks = [mask[pl.ds(spot * tokens, tokens), :] for spot in range(count)]
    scale = HEAD_DIM ** (-0.5)
    grads_q = []
    grads_k = [[] for _ in range(count)]
    grads_v = [[] for _ in range(count)]
    for head in range(2):
        query_h = head_of(query, head)
        grad_h = head_of(grad, head)
        keys_h = [head_of(key, head) for key in keys]
        probs = head_probs(query_h, keys_h, masks)
        grad_probs = [dot_t(head_of(value, head), grad_h) for value in values]
        inner = sum(
            jnp.sum(prob * grad_prob, axis=0, keepdims=True)
            for prob, grad_prob in zip(probs, grad_probs)
        )
        flow_q = 0.0
        for spot in range(count):
            grad_score = (probs[spot] * (grad_probs[spot] - inner)).astype(BF16)
            flow_q = flow_q + dot_tt(keys_h[spot], grad_score)
            grads_k[spot].append(dot(grad_score, query_h) * scale)
            grads_v[spot].append(dot(probs[spot].astype(BF16), grad_h))
        grads_q.append(flow_q * scale)
    grad_q[...] = jnp.concatenate(grads_q, axis=0).T.astype(BF16)
    for spot in range(count):
        out = mine if spot < count_y else other
        out[0, spot % count_y] = jnp.concatenate(grads_k[spot], axis=1).astype(BF16)
        out[1, spot % count_y] = jnp.concatenate(grads_v[spot], axis=1).astype(BF16)


def attend_back(query, keyvals, grad, mask):
    tokens = query.shape[0]
    count = len(keyvals)
    count_y = count // CORES
    pair = 2 * HEAD_DIM
    part = pl.BlockSpec((2, count_y, tokens, pair), lambda i: (0, 0, 0, i))
    return call(
        functools.partial(attend_back_kernel, count, count_y, tokens),
        (D // pair,),
        [pl.BlockSpec((tokens, pair), lambda i: (0, i))] * 2
        + [fixed(mask.shape)]
        + pair_specs(tokens, count),
        [pl.BlockSpec((tokens, pair), lambda i: (0, i)), part, part],
        [shaped((tokens, D), BF16)] + [shaped((2, count_y, tokens, D), BF16)] * 2,
        cost=21.0,
        name="attend_back",
    )(query, grad, mask, *keyvals, *keyvals)


def mix_kernel(attn, weight, carried, vecs, summed, middle, middle_low):
    value = carried[...].astype(F32) + (dot(attn[...], weight[0]) + vecs[0:1, :])
    summed[...] = value
    normed, _ = norm_stats(value)
    value = normed * vecs[1:2, :] + vecs[2:3, :]
    middle[...] = value
    middle_low[...] = value.astype(BF16)


def mix(attn, w_in, carried, vecs):
    tokens = attn.shape[0]
    full = fixed((tokens, D))
    return call(
        mix_kernel,
        (1,),
        [full, pl.BlockSpec((1, BLK, BLK), lambda i: (3, 0, 0)), full, fixed(vecs.shape)],
        [full, full, full],
        [shaped((tokens, D), F32), shaped((tokens, D), F32), shaped((tokens, D), BF16)],
        cost=4.0,
        name="mix",
    )(attn, w_in, carried, vecs)


def erf_part(hidden):
    return (1.0 + lax.erf(hidden * (0.5**0.5))) * 0.5


def up_kernel(split, where, middle_low, bias, *refs):
    pieces, (hidden, act, weight) = refs[:-3], refs[-3:]
    open_block(split, where, pieces, weight)
    value = dot(middle_low[...], weight[0]) + bias[0]
    hidden[...] = value
    act[...] = (value * erf_part(value)).astype(BF16)


def up(middle_low, chunk, bias):
    tokens = middle_low.shape[0]
    pieces, specs = chunk.pieces()
    part = pl.BlockSpec((tokens, BLK), lambda i, where: (0, i))
    return call(
        functools.partial(up_kernel, chunk.split_count),
        (FF // BLK,),
        [fixed((tokens, D)), pl.BlockSpec((1, 1, BLK), lambda i, where: (i, 0, 0))] + specs,
        [part, part, BLOCK],
        [shaped((tokens, FF), F32), shaped((tokens, FF), BF16), BLOCKS],
        prefetch=1,
        cost=8.0,
        name="up",
    )(chunk.where(), middle_low, bias, *pieces)


def down_kernel(split, where, act, middle, vecs, *refs):
    pieces, (summed, result, result_low, weight, total) = refs[:-5], refs[-5:]
    open_block(split, where, pieces, weight)
    spot = pl.program_id(0)
    value = dot(act[...], weight[0])

    @pl.when(spot == 0)
    def _():
        total[...] = value

    @pl.when(spot > 0)
    def _():
        total[...] += value

    @pl.when(spot == pl.num_programs(0) - 1)
    def _():
        value = middle[...] + (total[...] + vecs[0:1, :])
        summed[...] = value
        normed, _ = norm_stats(value)
        value = normed * vecs[1:2, :] + vecs[2:3, :]
        result[...] = value
        result_low[...] = value.astype(BF16)


def down(act, chunk, middle, vecs):
    tokens = act.shape[0]
    full = fixed((tokens, D))
    pieces, specs = chunk.pieces()
    return call(
        functools.partial(down_kernel, chunk.split_count),
        (FF // BLK,),
        [pl.BlockSpec((tokens, BLK), lambda i, where: (0, i)), full, fixed(vecs.shape)] + specs,
        [full, full, full, BLOCK],
        [shaped((tokens, D), F32), shaped((tokens, D), F32), shaped((tokens, D), BF16), BLOCKS],
        scratch=[pltpu.VMEM((tokens, D), F32)],
        prefetch=1,
        cost=8.0,
        name="down",
    )(chunk.where(), act, middle, vecs, *pieces)


def column_sum(value):
    return jnp.sum(value, axis=0, keepdims=True)


def close_kernel(flow, summed, gain, back_out, low_out, sums):
    grad = flow[...].astype(F32)
    normed, scale = norm_stats(summed[...])
    back = norm_back(grad, normed, scale, gain[...])
    back_out[...] = back
    low = back.astype(BF16)
    low_out[...] = low
    sums[0:1, :] = column_sum(low.astype(F32))
    sums[1:2, :] = column_sum(grad * normed)
    sums[2:3, :] = column_sum(grad)
    sums[3:8, :] = jnp.zeros((5, D), F32)


def close(flow, summed, gain):
    tokens = flow.shape[0]
    full = fixed((tokens, D))
    return call(
        close_kernel,
        (1,),
        [full, full, fixed((1, D))],
        [full, full, fixed((8, D))],
        [shaped((tokens, D), F32), shaped((tokens, D), BF16), shaped((8, D), F32)],
        cost=3.0,
        name="close",
    )(flow, summed, gain)


def feed_back_kernel(
    grad_two, ffn_low, summed_one, hidden, w_down, w_up, w_out, gain,
    hid_low, branch_low, attn_grad, grad_one, sums, bias_sums, total,
):
    spot = pl.program_id(0)

    @pl.when(spot == 0)
    def _():
        total[...] = grad_two[...]

    value = hidden[...]
    slope = erf_part(value) + value * jnp.exp(-0.5 * value * value) * ((2.0 * np.pi) ** -0.5)
    low = (dot_t(ffn_low[...], w_down[0]) * slope).astype(BF16)
    hid_low[...] = low
    bias_sums[0] = column_sum(low.astype(F32))
    total[...] += dot_t(low, w_up[0])

    @pl.when(spot == pl.num_programs(0) - 1)
    def _():
        grad = total[...]
        normed, scale = norm_stats(summed_one[...])
        back = norm_back(grad, normed, scale, gain[...])
        grad_one[...] = back
        low = back.astype(BF16)
        branch_low[...] = low
        sums[0:1, :] = column_sum(low.astype(F32))
        sums[1:2, :] = column_sum(grad * normed)
        sums[2:3, :] = column_sum(grad)
        sums[3:8, :] = jnp.zeros((5, D), F32)
        attn_grad[...] = dot_t(low, w_out[0]).astype(BF16)


def feed_back(grad_two, ffn_low, summed_one, hidden, w_down, w_up, w_in, gain):
    tokens = ffn_low.shape[0]
    full = fixed((tokens, D))
    part = pl.BlockSpec((tokens, BLK), lambda i: (0, i))
    weight = pl.BlockSpec((1, BLK, BLK), lambda i: (i, 0, 0))
    return call(
        feed_back_kernel,
        (FF // BLK,),
        [full, full, full, part, weight, weight, pl.BlockSpec((1, BLK, BLK), lambda i: (3, 0, 0)), fixed((1, D))],
        [part, full, full, full, fixed((8, D)), pl.BlockSpec((1, 1, BLK), lambda i: (i, 0, 0))],
        [
            shaped((tokens, FF), BF16),
            shaped((tokens, D), BF16),
            shaped((tokens, D), BF16),
            shaped((tokens, D), F32),
            shaped((8, D), F32),
            shaped((FF // BLK, 1, BLK), F32),
        ],
        scratch=[pltpu.VMEM((tokens, D), F32)],
        cost=15.0,
        name="feed_back",
    )(grad_two, ffn_low, summed_one, hidden, w_down, w_up, w_in, gain)


def input_back_kernel(count, grad_q, grad_one, weight, *refs):
    parts, (joined, result, sums, total) = refs[:count], refs[count:]
    spot = pl.program_id(0)

    @pl.when(spot == 0)
    def _():
        joined[...] = grad_q[...]
        total[...] = grad_one[...]

    @pl.when(spot > 0)
    def _():
        joined[...] = sum(part[0].astype(F32) for part in parts).astype(BF16)

    low = joined[...]
    sums[0] = column_sum(low.astype(F32))
    total[...] += dot_t(low, weight[0])

    @pl.when(spot == pl.num_programs(0) - 1)
    def _():
        result[...] = total[...]


def input_back(grad_q, parts, grad_one, w_in):
    tokens = grad_q.shape[0]
    full = fixed((tokens, D))
    return call(
        functools.partial(input_back_kernel, len(parts)),
        (3,),
        [full, full, pl.BlockSpec((1, BLK, BLK), lambda i: (i, 0, 0))]
        + [pl.BlockSpec((1, tokens, D), lambda i: (jnp.maximum(i - 1, 0), 0, 0))] * len(parts),
        [pl.BlockSpec((tokens, D), lambda i: (0, i)), full, pl.BlockSpec((1, 1, D), lambda i: (i, 0, 0))],
        [shaped((tokens, 3 * D), BF16), shaped((tokens, D), F32), shaped((3, 1, D), F32)],
        scratch=[pltpu.VMEM((tokens, D), F32)],
        cost=8.0,
        name="input_back",
    )(grad_q, grad_one, w_in, *parts)


def gather_list(place, value, axis):
    return [value] + [place.take(value, axis, step) for step in range(1, place.size[axis])]


def project_step(place, carried_low, chunk, vector):
    parts = vector_parts(vector)
    bias_in = jnp.stack([parts[0], jnp.zeros((D,), F32), parts[1]])[:, None]
    query, keyval, w_in = project(carried_low, chunk, bias_in)
    keyvals = [keyval, *gather_list(place, keyval, "y")[1:], place.take(keyval, "core", 1)]
    return query, keyvals, w_in


def mix_step(query, keyvals, carried, w_in, vector, mask):
    parts = vector_parts(vector)
    attn_low = attend(query, keyvals, mask)
    return attn_low, *mix(attn_low, w_in, carried, jnp.stack([parts[2], parts[4], parts[5]]))


def up_step(mid_low, chunk, vector):
    return up(mid_low, chunk, vector[8 * D :].reshape(FF // BLK, 1, BLK))


def down_step(act_low, chunk, middle, vector):
    parts = vector_parts(vector)
    return down(act_low, chunk, middle, jnp.stack([parts[3], parts[6], parts[7]]))


def sum_kernel(count_one, first_half, sizes, where, *refs):
    sets = (refs[:4], refs[4:8]) if count_one is not None else (refs[:4],)
    outs, product = refs[4 * len(sets) : -1], refs[-1]
    x_at, y_at = where[1], where[2]
    extent_z, extent_x, extent_y, rows = sizes
    spot = pl.program_id(0)

    def multiply(left_mine, left_other, right_mine, right_other):
        left = jnp.concatenate([left_mine[...], left_other[...]], axis=0)
        right = jnp.concatenate([right_mine[...], right_other[...]], axis=0)
        product[...] = dot_tt(left, right)

    if len(sets) == 1:
        multiply(*sets[0])
    else:
        pl.when(spot < count_one)(lambda: multiply(*sets[0]))
        pl.when(spot >= count_one)(lambda: multiply(*sets[1]))
    cols = product.shape[1] // extent_y

    def put(y_first):
        for step_y in range(extent_y):
            from_col = pl.multiple_of(lax.rem(y_at + step_y, extent_y) * cols, cols)
            for step_x in range(extent_x):
                for step_z in range(extent_z):
                    row_block = step_z * extent_x + lax.rem(x_at + step_x, extent_x)
                    from_row = pl.multiple_of(row_block * rows, rows)
                    value = product[pl.ds(from_row, rows), pl.ds(from_col, cols)].astype(BF16)
                    if y_first:
                        outs[step_y][step_x, step_z, 0] = value
                    else:
                        outs[extent_y + step_x][step_y, step_z, 0] = value

    pl.when(spot < first_half)(lambda: put(True))
    pl.when(spot >= first_half)(lambda: put(False))


def partial_sums(place, sets):
    tokens = sets[0][0].shape[0]
    extent_z, extent_x, extent_y = (place.size[name] for name in ("z", "x", "y"))
    rows = BLK // (extent_z * extent_x)
    half = BLK // CORES
    cols = half // extent_y
    where = jnp.stack([place.at[name] for name in ("z", "x", "y", "core")]).astype(jnp.int32)
    counts = [max(one[0].shape[1], one[2].shape[1]) // BLK for one in sets]
    count = sum(counts)
    first_half = count // 2
    specs = []
    start = 0
    for one, amount in zip(sets, counts):

        def at(i, start=start, amount=amount):
            return jnp.clip(i - start, 0, amount - 1)

        many_left, many_right = one[0].shape[1] > BLK, one[2].shape[1] > BLK
        for first in (0, one[4]):
            specs.append(
                pl.BlockSpec(
                    (tokens, BLK),
                    lambda i, where, at=at, many=many_left, first=first: (0, first + (at(i) if many else 0)),
                )
            )
        specs += [
            pl.BlockSpec(
                (tokens, half),
                lambda i, where, at=at, many=many_right: (0, (at(i) * CORES if many else 0) + where[3]),
            )
        ] * 2
        start += amount
    part_y = (extent_x, extent_z, 1, rows, cols)
    part_x = (extent_y, extent_z, 1, rows, cols)
    spec_y = pl.BlockSpec(part_y, lambda i, where: (0, 0, jnp.minimum(i, first_half - 1), 0, 0))
    spec_x = pl.BlockSpec(part_x, lambda i, where: (0, 0, jnp.maximum(i - first_half, 0), 0, 0))
    outs = call(
        functools.partial(
            sum_kernel,
            counts[0] if len(sets) > 1 else None,
            first_half,
            (extent_z, extent_x, extent_y, rows),
        ),
        (count,),
        specs,
        [spec_y] * extent_y + [spec_x] * extent_x,
        [shaped((extent_x, extent_z, first_half, rows, cols), BF16)] * extent_y
        + [shaped((extent_y, extent_z, count - first_half, rows, cols), BF16)] * extent_x,
        scratch=[pltpu.VMEM((BLK, half), F32)],
        prefetch=1,
        cost=8.0,
        name="partial_sums",
    )(where, *[value for one in sets for value in one[:4]])
    return outs[:extent_y], outs[extent_y:]


class Summing:
    def __init__(self, place, ids, sets):
        self.place = place
        self.ids = ids
        if (BLK // (CORES * place.size["y"])) % 128:
            self.plain = True
            self.parts = self.by_y = self.by_x = ()
            self.groups = [sum_job_plain(place, one[0], one[2], "y")[None] for one in sets]
        else:
            self.plain = False
            sets = [(one[0], one[1], one[2], place.take(one[2], "core", 1), one[3]) for one in sets]
            self.parts = partial_sums(place, sets)
            self.by_y = self.by_x = ()
            self.groups = ()

    def first_y(self):
        if not self.plain:
            self.by_y = self.place.collect(self.parts[0], "y")

    def first_x(self):
        if not self.plain:
            self.by_x = self.place.collect(self.parts[1], "x")

    def second_x(self):
        if not self.plain:
            total = add_up(self.by_y)
            parts = [total[step].astype(BF16) for step in range(self.place.size["x"])]
            self.by_y = self.place.collect(parts, "x")

    def second_y(self):
        if not self.plain:
            total = add_up(self.by_x)
            parts = [total[step].astype(BF16) for step in range(self.place.size["y"])]
            self.by_x = self.place.collect(parts, "y")

    def third(self):
        if not self.plain:
            both = jnp.concatenate([add_up(self.by_y), add_up(self.by_x)], axis=1)
            self.groups = [self.place.swap_z(both.astype(BF16))]


def route_kernel(count, slots, scaling, spots, *refs):
    parts, (out, total) = refs[:count], refs[count:]
    at = 0
    for part in parts:
        for block in range(part.shape[1]):
            value = sum(part[addend, block].astype(F32) for addend in range(part.shape[0]))
            total[at] = (value * scaling).astype(BF16)
            at += 1
    total[at] = jnp.zeros(total.shape[1:], BF16)
    for ctx in range(out.shape[0]):
        for spot in range(out.shape[1]):
            if spot < slots:
                out[ctx, spot] = total[spots[ctx * slots + spot]]
            else:
                out[ctx, spot] = total[at]


def route(groups, spots, slots, wsh_count, scaling):
    rows, cols = groups[0].shape[2:]
    blocks = sum(group.shape[1] for group in groups)
    shape = (spots.shape[0] // slots, wsh_count, rows, cols)
    return call(
        functools.partial(route_kernel, len(groups), slots, scaling),
        (1,),
        [fixed(group.shape) for group in groups],
        fixed(shape),
        shaped(shape, BF16),
        scratch=[pltpu.VMEM((blocks + 1, rows, cols), BF16)],
        prefetch=1,
        cost=6.0,
        name="route",
    )(spots, *groups)


def rotate_kernel(quarters, where, grads, right, left, first, second, rotated, update, total, low, right_low):
    step = BLK // 4
    right_low[...] = right[0].astype(BF16)
    for at in range(4):
        rows = pl.ds(at * step, step)
        product = 0.0
        for source, quarter in enumerate(quarters):
            width = grads.shape[2]
            product = product + dot(
                grads[source, rows, :], right_low[pl.ds(quarter * width, width), :]
            )
        value = dot_tt(left[rows, :], product.astype(BF16))
        if at:
            total[...] += value
        else:
            total[...] = value
    for at in range(4):
        rows = pl.ds(at * step, step)
        turned = total[rows, :]
        rotated[rows, :] = turned.astype(BF16)
        first_new = DECAY_RATE * first[rows, :].astype(F32) + (1.0 - DECAY_RATE) * turned
        second_new = DECAY_RATE * second[rows, :].astype(F32) + (1.0 - DECAY_RATE) * turned * turned
        direction = first_new / (jnp.sqrt(second_new) + EPS_ADAM)
        low[rows, :] = dot_t(direction.astype(BF16), right_low[...]).astype(BF16)
    for at in range(4):
        rows = pl.ds(at * step, step)
        update[rows, :] = dot(left[rows, :], low[...]).astype(BF16)


def rotate(grads, quarters, right_bases, slot, left, first, second):
    full = fixed((BLK, BLK))
    return call(
        functools.partial(rotate_kernel, quarters),
        (1,),
        [
            fixed(grads.shape),
            pl.BlockSpec((1, BLK, BLK), lambda i, where: (where[0], 0, 0)),
            full,
            full,
            full,
        ],
        [full, full],
        [shaped((BLK, BLK), BF16)] * 2,
        scratch=[pltpu.VMEM((BLK, BLK), F32), pltpu.VMEM((BLK, BLK), BF16), pltpu.VMEM((BLK, BLK), BF16)],
        prefetch=1,
        cost=16.0,
        name="rotate",
    )(slot, grads, right_bases, left, first, second)


def pick_kernel(count, amount, table, *refs):
    parts, out = refs[:count], refs[count]
    first = pl.program_id(0) * amount

    def put(spot, part):
        out[spot] = parts[part][table[1, first + spot]]

    for spot in range(amount):
        for part in range(count):
            pl.when(table[0, first + spot] == part)(functools.partial(put, spot, part))


def pick(parts, table):
    blocks = table.shape[1]
    amount = 4
    shape = (blocks,) + parts[0].shape[1:]
    return call(
        functools.partial(pick_kernel, len(parts), amount),
        (blocks // amount,),
        [fixed(value.shape) for value in parts],
        pl.BlockSpec((amount,) + shape[1:], lambda i, table: (i, 0, 0)),
        shaped(shape, BF16),
        prefetch=1,
        cost=12.0,
        name="pick",
    )(table, *parts)


def left_order(place, left):
    tokens, cols = left.shape
    count_z, count_x = place.size["z"], place.size["x"]
    blocks = cols // BLK
    rows = BLK // (count_z * count_x)
    value = left.reshape(tokens, blocks, count_z, count_x, rows)
    value = jnp.roll(value, (-place.at["z"], -place.at["x"]), axis=(2, 3))
    return value.transpose(0, 3, 2, 1, 4).reshape(tokens, cols)


def right_halves(place, right):
    tokens, cols = right.shape
    count_y = place.size["y"]
    width = BLK // (CORES * count_y)
    value = right.reshape(tokens, cols // BLK, CORES, count_y, width)
    halves = []
    for step in range(CORES):
        half = lax.dynamic_index_in_dim(value, (place.at["core"] + step) % CORES, 2, False)
        half = jnp.roll(half, -place.at["y"], axis=2)
        halves.append(half.transpose(2, 0, 1, 3).reshape(count_y, tokens, -1))
    return halves


def sum_job_plain(place, left, right, first):
    count_z, count_x, count_y = place.size["z"], place.size["x"], place.size["y"]
    left = left_order(place, left)
    right_mine, right_other = right_halves(place, right)
    left_both = jnp.concatenate([left, place.take(left, "core", 1)], axis=0)
    right_both = jnp.concatenate([right_mine, place.take(right_other, "core", 1)], axis=1)
    partial = [
        lax.dot_general(left_both, right_both[step], (((0,), (0,)), ((), ())), preferred_element_type=F32)
        .astype(BF16)
        .reshape(count_x, count_z, -1, right_both.shape[2])
        for step in range(count_y)
    ]
    if first == "y":
        total = place.scatter(partial, "y").astype(BF16)
        total = place.scatter(total, "x").astype(BF16)
    else:
        parts = [[value[step] for value in partial] for step in range(count_x)]
        parts = [jnp.stack(part) for part in parts]
        total = place.scatter(parts, "x").astype(BF16)
        total = place.scatter(total, "y").astype(BF16)
    total = place.scatter(total, "z")
    rows = BLK // (count_z * count_x)
    width = BLK // (CORES * count_y)
    if left.shape[1] > BLK:
        return total.reshape(-1, rows, width)
    return total.reshape(rows, -1, width).transpose(1, 0, 2)


def sum_everywhere(place, value):
    if place.size["y"] != 2 or place.size["x"] != 2:
        return lax.psum(value, ("ctx", "wsh"))
    for axis in ("core", "y", "x"):
        value = value + place.take(value, axis, 1)
    pairs = place.size["x"]
    for bit in (1, 2):
        swap = [
            (z * pairs + x, (z ^ bit) * pairs + x) for z in range(DEPTH_Z) for x in range(pairs)
        ]
        value = value + lax.ppermute(value, "wsh", swap)
    return value


def doc_ids(lengths, position):
    starts = jnp.cumsum(lengths) - lengths
    return jnp.sum((position[:, None] >= starts[None, :]).astype(jnp.int32), axis=1)


def to_owner(rows_value, wsh_count):
    slots = rows_value.shape[0]
    padded = jnp.pad(rows_value.astype(BF16), ((0, wsh_count - slots), (0, 0), (0, 0)))
    return lax.all_to_all(padded, "wsh", 0, 0, tiled=True).reshape(BLK, BLK)


def from_owner(whole, wsh_count, slots):
    cut = whole.astype(BF16).reshape(wsh_count, BLK // wsh_count, BLK)
    return lax.all_to_all(cut, "wsh", 0, 0, tiled=True)[:slots]


def on_device(
    stream_in,
    doc_lengths,
    cotangent,
    weights,
    vec_params,
    owner_slots,
    master,
    left_bases,
    right_bases,
    moment1,
    moment2,
    vec_moment1,
    vec_moment2,
):
    tokens = stream_in.shape[1]
    ctx_count = lax.axis_size("ctx")
    wsh_count = lax.axis_size("wsh")
    place = Place(ctx_count, wsh_count)
    seq_len = tokens * ctx_count
    scaling = (wsh_count * seq_len) ** (-0.5)
    slots_dev, rows_dev = master.shape[0], master.shape[1]
    slot_total = ctx_count * slots_dev
    count_y = place.size["y"]
    width = BLK // ctx_count

    core_of = (place.at["core"] + jnp.arange(CORES)) % CORES
    y_of = (place.at["y"] + jnp.arange(count_y)) % count_y
    ctx_of = (y_of[None, :] * CORES + core_of[:, None]).reshape(-1)
    key_pos = (ctx_of[:, None] * tokens + jnp.arange(tokens)[None, :]).reshape(-1)
    doc_keys = doc_ids(doc_lengths[0], key_pos)
    mask = jnp.where(doc_keys[:, None] == doc_keys[None, :tokens], 0.0, -1e30).astype(F32)

    chunks = [
        Gathering(place, weights[layer_at, first : first + 4])
        for layer_at in range(LAYERS)
        for first in range(0, NBLK, 4)
    ]

    live = {}

    def settle():
        going = [chunk for chunk in chunks if chunk]
        state = [(chunk.held, chunk.crossed) for chunk in going]
        state, values = together(state, {name: live[name] for name in live})
        for chunk, (held, crossed) in zip(going, state):
            chunk.held, chunk.crossed = held, crossed
        live.update(values)

    def finish(spot):
        chunk = chunks[spot]
        chunk.step_core()
        chunks[spot] = None
        return chunk

    def keyvals_of(layer_at):
        keyvals = live[f"keyvals{layer_at}"]
        return keyvals + [place.take(value, "core", 1) for value in keyvals[1:count_y]]

    kept = [{}, {}]
    chunks[0].step_z()
    settle()
    chunks[0].step_x()
    chunks[1].step_z()
    settle()
    chunks[0].step_y()
    chunks[1].step_x()
    chunks[2].step_z()
    settle()
    chunks[1].step_y()
    chunks[2].step_x()
    chunks[3].step_z()
    query_0, live["keyvals0"], w_in_0 = project_step(place, stream_in[0], finish(0), vec_params[0])
    live["query"] = query_0
    settle()
    chunks[2].step_y()
    chunks[3].step_x()
    chunks[4].step_z()
    keyvals_0 = keyvals_of(0)
    query_0 = live["query"]
    attn_0, summed_one_0, middle_0, mid_low_0 = mix_step(
        query_0, keyvals_0, stream_in[0], w_in_0, vec_params[0], mask
    )
    hidden_0, live["act"], w_up_0 = up_step(mid_low_0, finish(1), vec_params[0])
    settle()
    chunks[3].step_y()
    chunks[4].step_x()
    chunks[5].step_z()
    act_0 = live["act"]
    summed_two_0, live["result"], live["result_low"], w_down_0 = down_step(
        act_0, finish(2), middle_0, vec_params[0]
    )
    settle()
    chunks[4].step_y()
    chunks[5].step_x()
    result_0, result_low_0 = live["result"], live["result_low"]
    query_1, live["keyvals1"], w_in_1 = project_step(place, result_low_0, finish(3), vec_params[1])
    live["query"] = query_1
    live["own"] = left_bases
    settle()
    chunks[5].step_y()
    left_own = to_owner(live.pop("own"), wsh_count)
    keyvals_1 = keyvals_of(1)
    query_1 = live["query"]
    attn_1, summed_one_1, middle_1, mid_low_1 = mix_step(
        query_1, keyvals_1, result_0, w_in_1, vec_params[1], mask
    )
    hidden_1, live["act"], w_up_1 = up_step(mid_low_1, finish(4), vec_params[1])
    settle()
    act_1 = live["act"]
    summed_two_1, _, result_low_1, w_down_1 = down_step(act_1, finish(5), middle_1, vec_params[1])
    stream_out = result_low_1[None]

    blocks = [(w_in_0, w_up_0, w_down_0), (w_in_1, w_up_1, w_down_1)]
    lefts = [
        (stream_in[0], attn_0, mid_low_0, act_0),
        (result_low_0, attn_1, mid_low_1, act_1),
    ]
    crossed = [
        (place.take(jnp.concatenate(values[:3], axis=1), "core", 1), place.take(values[3], "core", 1))
        for values in lefts
    ]
    summed = [(summed_one_0, summed_two_0), (summed_one_1, summed_two_1)]
    hidden = [hidden_0, hidden_1]
    queries = [query_0, query_1]
    keyvals_all = [keyvals_0, keyvals_1]
    gains = [
        (vec_params[layer_at][None, 4 * D : 5 * D], vec_params[layer_at][None, 6 * D : 7 * D])
        for layer_at in range(LAYERS)
    ]
    live = {"crossed": crossed}
    jobs = []
    vec_terms = [None] * LAYERS

    def settle_back():
        state = [(job.parts, job.by_y, job.by_x, job.groups) for job in jobs]
        state, values = together(state, dict(live))
        for job, fields in zip(jobs, state):
            job.parts, job.by_y, job.by_x, job.groups = fields
        live.update(values)

    def begin(layer_at, first_block, *sets):
        ids = [layer_at * NBLK + first_block + spot for spot in range(4)]
        jobs.append(
            Summing(
                place,
                ids,
                [
                    (lefts[layer_at][spot], live["crossed"][layer_at][spot // 3], right, spot % 3)
                    for spot, right in sets
                ],
            )
        )
        return jobs[-1]

    def close_step(layer_at, flow):
        live["two"], live["ffn"], live["sums_two"] = close(flow, summed[layer_at][1], gains[layer_at][1])

    def down_job(layer_at):
        return begin(layer_at, 8, (3, live["ffn"]))

    def in_job(layer_at):
        return begin(layer_at, 0, (0, live["joined"]), (1, live["branch_in"]))

    def up_job(layer_at):
        return begin(layer_at, 4, (2, live["hid"]))

    def feed_step(layer_at):
        w_in, w_up, w_down = blocks[layer_at]
        live["hid"], live["branch"], attn_grad, live["one"], live["sums_one"], live["sums_up"] = feed_back(
            live["two"], live["ffn"], summed[layer_at][0], hidden[layer_at], w_down, w_up, w_in, gains[layer_at][0]
        )
        live["attn_grad"] = attn_grad

    def attend_step(layer_at):
        live["grad_q"], mine, other = attend_back(
            queries[layer_at], keyvals_all[layer_at], live["attn_grad"], mask
        )
        live["pair"] = [mine, other]

    def send_step():
        mine, other = live["pair"]
        arrived = place.take(other, "core", 1)
        sums = [mine[:, step].astype(F32) + arrived[:, step].astype(F32) for step in range(count_y)]
        live["kv"] = [sums[0]] + [
            place.take(sums[step].astype(BF16), "y", -step) for step in range(1, count_y)
        ]

    def input_step(layer_at):
        live["joined"], grad_x, in_sums = input_back(live["grad_q"], live["kv"], live["one"], blocks[layer_at][0])
        sums_two, sums_one = live["sums_two"], live["sums_one"]
        vec_terms[layer_at] = jnp.concatenate(
            [
                in_sums[0, 0],
                in_sums[2, 0],
                sums_one[0],
                sums_two[0],
                sums_one[1:3].reshape(-1),
                sums_two[1:3].reshape(-1),
                live["sums_up"].reshape(-1),
            ]
        )
        live["branch_in"] = live["branch"]
        return grad_x

    close_step(1, cotangent[0])
    down_1 = down_job(1)
    live["left"] = left_own
    live["first"] = moment1
    settle_back()
    down_1.first_y()
    down_1.first_x()
    background = to_owner(live["first"], wsh_count)
    feed_step(1)
    settle_back()
    down_1.second_x()
    down_1.second_y()
    up_1 = up_job(1)
    live["first"] = background
    settle_back()
    down_1.third()
    up_1.first_y()
    up_1.first_x()
    attend_step(1)
    live["second"] = moment2
    settle_back()
    send_step()
    up_1.second_x()
    up_1.second_y()
    live["second"] = to_owner(live["second"], wsh_count)
    settle_back()
    grad_flow = input_step(1)
    close_step(0, grad_flow)
    settle_back()
    in_1 = in_job(1)
    down_0 = down_job(0)
    settle_back()
    up_1.third()
    in_1.first_y()
    in_1.first_x()
    feed_step(0)
    settle_back()
    in_1.second_x()
    in_1.second_y()
    down_0.first_y()
    down_0.first_x()
    attend_step(0)
    settle_back()
    send_step()
    in_1.third()
    down_0.second_x()
    down_0.second_y()
    up_0 = up_job(0)
    settle_back()
    down_0.third()
    up_0.first_y()
    up_0.first_x()
    grad_flow = input_step(0)
    settle_back()
    up_0.second_x()
    up_0.second_y()
    in_0 = in_job(0)
    settle_back()
    up_0.third()
    in_0.first_y()
    in_0.first_x()
    settle_back()
    in_0.second_x()
    in_0.second_y()
    settle_back()
    in_0.third()
    stream_grad = grad_flow[None]
    vec_grads = sum_everywhere(place, jnp.stack(vec_terms)) * scaling
    groups = [group for job in jobs for group in job.groups]
    ids = [block for job in jobs for block in job.ids]

    owner_flat = owner_slots.reshape(-1)
    block_count = LAYERS * NBLK
    owner_sorted = jnp.stack([owner_flat[block] for block in ids])
    picks = owner_sorted[None, :] == jnp.arange(slot_total, dtype=jnp.int32)[:, None]
    spots = jnp.where(
        jnp.any(picks, axis=1), jnp.argmax(picks, axis=1).astype(jnp.int32), block_count
    )
    by_slot = route(groups, spots, slots_dev, wsh_count, scaling)

    arrived = lax.all_to_all(
        by_slot.reshape(ctx_count * wsh_count, rows_dev, width), ("ctx", "wsh"), 0, 0, tiled=True
    )
    quarters = [(source % CORES) * count_y + source // CORES for source in range(ctx_count)]
    slot_own = jnp.minimum(lax.axis_index("wsh"), slots_dev - 1).reshape(1)
    rotated_own, update_own = rotate(
        arrived.reshape(ctx_count, BLK, width), quarters, right_bases, slot_own, live["left"], live["first"], live["second"]
    )

    by_rows = after(by_slot[:, :slots_dev], arrived)
    by_rows = lax.all_to_all(by_rows, "ctx", 0, 0, tiled=True)
    update_own, rotated_own, by_rows = together(update_own, rotated_own, by_rows)
    update = from_owner(update_own, wsh_count, slots_dev)
    by_rows = by_rows.reshape(count_y, CORES, slots_dev, rows_dev, width)
    block_grads = by_rows.transpose(2, 3, 1, 0, 4).reshape(slots_dev, rows_dev, BLK).astype(F32)
    update, rotated_own, block_grads = together(update, rotated_own, block_grads)
    update = update.astype(F32)

    new_master = master - LR_BLOCK * update
    master_low = new_master.astype(BF16)
    parts = gather_list(place, master_low, "y")
    rotated = from_owner(rotated_own, wsh_count, slots_dev)
    parts, rotated = together(parts, rotated)
    rotated = rotated.astype(F32)
    parts = parts + [place.take(value, "core", 1) for value in parts]
    owner_ctx, owner_at = owner_flat // slots_dev, owner_flat % slots_dev
    step_y = (owner_ctx // CORES - place.at["y"]) % count_y
    step_core = (owner_ctx % CORES - place.at["core"]) % CORES
    table = jnp.stack([step_core * count_y + step_y, owner_at]).astype(jnp.int32)
    new_weights = pick(parts, table).reshape(LAYERS, NBLK, rows_dev, BLK)

    new_moment1 = DECAY_RATE * moment1 + (1.0 - DECAY_RATE) * rotated
    new_moment2 = DECAY_RATE * moment2 + (1.0 - DECAY_RATE) * rotated * rotated

    new_vec_moment1 = DECAY_RATE * vec_moment1 + (1.0 - DECAY_RATE) * vec_grads
    new_vec_moment2 = DECAY_RATE * vec_moment2 + (1.0 - DECAY_RATE) * vec_grads * vec_grads
    new_vec_params = vec_params - LR_VEC * new_vec_moment1 / (jnp.sqrt(new_vec_moment2) + EPS_ADAM)
    return (
        stream_out,
        stream_grad,
        block_grads,
        new_moment1,
        new_moment2,
        new_master,
        new_weights,
        vec_grads,
        new_vec_params,
        new_vec_moment1,
        new_vec_moment2,
    )


def solution(mesh):
    rows = P("ctx", "wsh", None)
    placed = (
        P("wsh", "ctx", None),
        P("wsh", None),
        P("wsh", "ctx", None),
        P(None, None, "wsh", None),
        P(),
        P(),
        rows,
        rows,
        P("ctx", None, None),
        rows,
        rows,
        P(),
        P(),
    )
    return jax.shard_map(
        on_device,
        mesh=mesh,
        in_specs=placed,
        out_specs=(
            P("wsh", "ctx", None),
            P("wsh", "ctx", None),
            rows,
            rows,
            rows,
            rows,
            P(None, None, "wsh", None),
            P(),
            P(),
            P(),
            P(),
        ),
        check_vma=False,
    )
```

```python
import functools

import jax
import jax.numpy as jnp
import numpy as np
from jax import lax
from jax.experimental import pallas as pl
from jax.experimental.pallas import tpu as pltpu
from jax.sharding import PartitionSpec as P

D = 1024
HEADS = 16
HEAD_DIM = 64
FF = 4096
BLK = 1024
LAYERS = 2
NBLK = 12
CORES = 2
DEPTH_Z = 4

EPS_NORM = 1e-05
EPS_ADAM = 1e-08
LR_BLOCK = 0.1
LR_VEC = 0.25
DECAY_RATE = 0.5
VMEM_BYTES = 56 * 1024 * 1024
BF16 = jnp.bfloat16
F32 = jnp.float32


class Place:
    def __init__(self, ctx_count, wsh_count):
        self.size = {
            "core": CORES,
            "y": ctx_count // CORES,
            "z": DEPTH_Z,
            "x": wsh_count // DEPTH_Z,
        }
        ctx_at = lax.axis_index("ctx")
        wsh_at = lax.axis_index("wsh")
        self.at = {
            "core": ctx_at % CORES,
            "y": ctx_at // CORES,
            "z": wsh_at // self.size["x"],
            "x": wsh_at % self.size["x"],
        }

    def take(self, value, axis, step):
        name, slow, fast = {
            "core": ("ctx", "y", "core"),
            "y": ("ctx", "y", "core"),
            "z": ("wsh", "z", "x"),
            "x": ("wsh", "z", "x"),
        }[axis]
        extent = self.size[axis]
        pairs = []
        for slow_at in range(self.size[slow]):
            for fast_at in range(self.size[fast]):
                if axis == fast:
                    other = (slow_at, (fast_at + step) % extent)
                else:
                    other = ((slow_at + step) % extent, fast_at)
                pairs.append(
                    (
                        other[0] * self.size[fast] + other[1],
                        slow_at * self.size[fast] + fast_at,
                    )
                )
        return lax.ppermute(value, name, pairs)

    def gather(self, value, axis):
        steps = range(1, self.size[axis])
        return jnp.stack([value] + [self.take(value, axis, step) for step in steps])

    def collect(self, values, axis):
        steps = range(1, self.size[axis])
        return [values[0]] + [self.take(values[step], axis, -step) for step in steps]

    def swap_z(self, values):
        count_x = self.size["x"]
        lines = [[z * count_x + x for z in range(self.size["z"])] for x in range(count_x)]
        return lax.all_to_all(values, "wsh", 0, 0, tiled=True, axis_index_groups=lines)

    def scatter(self, values, axis):
        total = values[0].astype(F32)
        for step in range(1, self.size[axis]):
            total = total + self.take(values[step], axis, -step).astype(F32)
        return total


def vector_parts(vector):
    pieces = [vector[spot * D : (spot + 1) * D] for spot in range(8)]
    return pieces + [vector[8 * D :]]


def dot(left, right):
    return jnp.dot(left, right, preferred_element_type=F32)


def dot_t(left, right):
    return lax.dot_general(left, right, (((1,), (1,)), ((), ())), preferred_element_type=F32)


def after(value, *others):
    return lax.optimization_barrier((value,) + others)[0]


def together(*values):
    return lax.optimization_barrier(values)


def add_up(values):
    return sum(value.astype(F32) for value in values)


class Gathering:
    def __init__(self, place, shard, split_count):
        self.place = place
        self.count, self.rows, _ = shard.shape
        half_rows, half_cols = self.rows // 2, BLK // 2
        has_y = place.size["y"] == 2
        self.split_count = split_count if has_y else 0
        whole_count = self.count - self.split_count
        mine = lax.dynamic_slice_in_dim(shard, place.at["core"] * half_rows, half_rows, 1)
        whole = mine[self.split_count :]
        pieces = [
            part
            for block in range(whole_count)
            for part in (whole[block, :, :half_cols], whole[block, :, half_cols:])
        ]
        parts = []
        if pieces:
            parts.append(jnp.stack(pieces))
        if has_y:
            parts.insert(
                0,
                lax.dynamic_slice_in_dim(
                    mine[: self.split_count], place.at["y"] * half_cols, half_cols, 2
                ),
            )
        self.held = [jnp.concatenate(parts)]
        self.crossed = []

    def step_z(self):
        piece = self.held[0]
        copies = jnp.broadcast_to(piece[None], (self.place.size["z"],) + piece.shape)
        self.held = [self.place.swap_z(copies)]

    def step_x(self):
        self.held = gather_list(self.place, self.held[0], "x")

    def step_y(self):
        self.held = [jnp.stack(self.held)]
        if self.split_count:
            value = self.held[0][:, :, : self.split_count]
            self.held.append(self.place.take(value, "y", 1))
        self.crossed = [self.place.take(self.held[0], "core", 1)]

    def step_core(self):
        if self.split_count:
            self.crossed.append(self.place.take(self.held[1], "core", 1))

    def pieces(self):
        split, mine, crossed = self.split_count, self.held, self.crossed
        part = (mine[0].shape[:2]) + (1,) + mine[0].shape[3:]

        def spec(place_of):
            return pl.BlockSpec(part, lambda i, where: (0, 0, place_of(i), 0, 0))

        last = mine[0].shape[2] - 1
        low = spec(lambda i: jnp.where(i < split, i, 2 * i - split))
        high = spec(lambda i: jnp.minimum(jnp.where(i < split, split + 1, 2 * i - split + 1), last))
        operands = [mine[0], crossed[0], mine[0], crossed[0]]
        specs = [low, low, high, high]
        if split:
            operands += [mine[1], crossed[1]]
            specs += [spec(lambda i: jnp.minimum(i, split - 1))] * 2
        return operands, specs

    def where(self):
        return jnp.stack([self.place.at[name] for name in ("x", "y", "core")]).astype(jnp.int32)


def open_block(split, where, pieces, out):
    spot = pl.program_id(0)
    extent_x, extent_z, _, half_rows, half_cols = pieces[0].shape
    x_at, y_at, core_at = where[0], where[1], where[2]

    def put(first_col, sources):
        low_col = pl.ds(pl.multiple_of(first_col * half_cols, half_cols), half_cols)
        high_col = pl.ds(pl.multiple_of((1 - first_col) * half_cols, half_cols), half_cols)
        for step_x in range(extent_x):
            for z in range(extent_z):
                base = (z * extent_x + lax.rem(x_at + step_x, extent_x)) * 2
                mine = pl.ds(pl.multiple_of((base + core_at) * half_rows, half_rows), half_rows)
                other = pl.ds(pl.multiple_of((base + 1 - core_at) * half_rows, half_rows), half_rows)
                out[0, mine, low_col] = sources[0][step_x, z, 0]
                out[0, other, low_col] = sources[1][step_x, z, 0]
                out[0, mine, high_col] = sources[2][step_x, z, 0]
                out[0, other, high_col] = sources[3][step_x, z, 0]

    if split:
        pl.when(spot < split)(lambda: put(y_at, list(pieces[:2]) + list(pieces[4:])))
        pl.when(spot >= split)(lambda: put(0, pieces[:4]))
    else:
        put(0, pieces[:4])


def call(body, grid, in_specs, out_specs, out_shape, scratch=(), prefetch=0, cost=1.0, name=None):
    return pl.pallas_call(
        body,
        grid_spec=pltpu.PrefetchScalarGridSpec(
            num_scalar_prefetch=prefetch,
            grid=grid,
            in_specs=in_specs,
            out_specs=out_specs,
            scratch_shapes=list(scratch),
        ),
        out_shape=out_shape,
        compiler_params=pltpu.CompilerParams(vmem_limit_bytes=VMEM_BYTES),
        cost_estimate=pl.CostEstimate(flops=int(cost * 2e7), bytes_accessed=0, transcendentals=0),
        name=name,
    )


def shaped(shape, dtype):
    return jax.ShapeDtypeStruct(shape, dtype)


def fixed(shape):
    return pl.BlockSpec(shape, lambda *at: (0,) * len(shape))


def norm_stats(summed):
    average = jnp.mean(summed, axis=-1, keepdims=True)
    centred = summed - average
    variance = jnp.mean(centred * centred, axis=-1, keepdims=True)
    scale = lax.rsqrt(variance + EPS_NORM)
    return centred * scale, scale


def norm_back(grad, normed, scale, gain):
    flow = grad * gain
    return (
        flow
        - jnp.mean(flow, axis=-1, keepdims=True)
        - normed * jnp.mean(flow * normed, axis=-1, keepdims=True)
    ) * scale


BLOCK = pl.BlockSpec((1, BLK, BLK), lambda i, *at: (i, 0, 0))
BLOCKS = jax.ShapeDtypeStruct((4, BLK, BLK), BF16)


def project_kernel(split, where, x_low, bias, *refs):
    pieces, (query, keyval, weight) = refs[:-3], refs[-3:]
    open_block(split, where, pieces, weight)

    def value():
        return (dot(x_low[...], weight[0]) + bias[0]).astype(BF16)

    @pl.when(pl.program_id(0) == 0)
    def _():
        query[...] = value()

    @pl.when((pl.program_id(0) > 0) & (pl.program_id(0) < 3))
    def _():
        keyval[...] = value()


def project(x_low, chunk, bias):
    tokens = x_low.shape[0]
    pieces, specs = chunk.pieces()
    return call(
        functools.partial(project_kernel, chunk.split_count),
        (4,),
        [fixed((tokens, D)), pl.BlockSpec((1, 1, D), lambda i, where: (jnp.minimum(i, 2), 0, 0))] + specs,
        [
            fixed((tokens, D)),
            pl.BlockSpec((tokens, D), lambda i, where: (0, jnp.clip(i - 1, 0, 1))),
            BLOCK,
        ],
        [shaped((tokens, D), BF16), shaped((tokens, 2 * D), BF16), BLOCKS],
        prefetch=1,
        cost=8.0,
        name="project",
    )(chunk.where(), x_low, bias, *pieces)


def head_probs(query_h, keys_h, masks):
    scores = [
        dot_t(key, query_h) * HEAD_DIM ** (-0.5) + mask for key, mask in zip(keys_h, masks)
    ]
    peak = functools.reduce(
        jnp.maximum, [jnp.max(score, axis=0, keepdims=True) for score in scores]
    )
    scores = [jnp.exp(score - peak) for score in scores]
    total = sum(jnp.sum(score, axis=0, keepdims=True) for score in scores)
    inverse = 1.0 / total
    return [score * inverse for score in scores]


def dot_tt(left, right):
    return lax.dot_general(left, right, (((0,), (0,)), ((), ())), preferred_element_type=F32)


def head_of(ref, head):
    return ref[:, pl.ds(head * HEAD_DIM, HEAD_DIM)]


def attend_kernel(count, tokens, query, mask, *refs):
    keys, values, out = refs[:count], refs[count : 2 * count], refs[-1]
    masks = [mask[pl.ds(spot * tokens, tokens), :] for spot in range(count)]
    mixed = []
    for head in range(2):
        probs = head_probs(head_of(query, head), [head_of(key, head) for key in keys], masks)
        mixed.append(
            sum(dot_tt(head_of(value, head), prob.astype(BF16)) for value, prob in zip(values, probs))
        )
    out[...] = jnp.concatenate(mixed, axis=0).T.astype(BF16)


def pair_specs(tokens, count):
    pair = 2 * HEAD_DIM
    half = D // pair
    return (
        [pl.BlockSpec((tokens, pair), lambda i: (0, i))] * count
        + [pl.BlockSpec((tokens, pair), lambda i: (0, half + i))] * count
    )


def attend(query, keyvals, mask):
    tokens = query.shape[0]
    count = len(keyvals)
    pair = 2 * HEAD_DIM
    return call(
        functools.partial(attend_kernel, count, tokens),
        (D // pair,),
        [pl.BlockSpec((tokens, pair), lambda i: (0, i)), fixed(mask.shape)]
        + pair_specs(tokens, count),
        pl.BlockSpec((tokens, pair), lambda i: (0, i)),
        shaped((tokens, D), BF16),
        cost=14.0,
        name="attend",
    )(query, mask, *keyvals, *keyvals)


def attend_back_kernel(count, count_y, tokens, query, grad, mask, *refs):
    keys, values = refs[:count], refs[count : 2 * count]
    grad_q, mine, other = refs[2 * count :]
    masks = [mask[pl.ds(spot * tokens, tokens), :] for spot in range(count)]
    scale = HEAD_DIM ** (-0.5)
    grads_q = []
    grads_k = [[] for _ in range(count)]
    grads_v = [[] for _ in range(count)]
    for head in range(2):
        query_h = head_of(query, head)
        grad_h = head_of(grad, head)
        keys_h = [head_of(key, head) for key in keys]
        probs = head_probs(query_h, keys_h, masks)
        grad_probs = [dot_t(head_of(value, head), grad_h) for value in values]
        inner = sum(
            jnp.sum(prob * grad_prob, axis=0, keepdims=True)
            for prob, grad_prob in zip(probs, grad_probs)
        )
        flow_q = 0.0
        for spot in range(count):
            grad_score = (probs[spot] * (grad_probs[spot] - inner)).astype(BF16)
            flow_q = flow_q + dot_tt(keys_h[spot], grad_score)
            grads_k[spot].append(dot(grad_score, query_h) * scale)
            grads_v[spot].append(dot(probs[spot].astype(BF16), grad_h))
        grads_q.append(flow_q * scale)
    grad_q[...] = jnp.concatenate(grads_q, axis=0).T.astype(BF16)
    for spot in range(count):
        out = mine if spot < count_y else other
        out[0, spot % count_y] = jnp.concatenate(grads_k[spot], axis=1).astype(BF16)
        out[1, spot % count_y] = jnp.concatenate(grads_v[spot], axis=1).astype(BF16)


def attend_back(query, keyvals, grad, mask):
    tokens = query.shape[0]
    count = len(keyvals)
    count_y = count // CORES
    pair = 2 * HEAD_DIM
    part = pl.BlockSpec((2, count_y, tokens, pair), lambda i: (0, 0, 0, i))
    return call(
        functools.partial(attend_back_kernel, count, count_y, tokens),
        (D // pair,),
        [pl.BlockSpec((tokens, pair), lambda i: (0, i))] * 2
        + [fixed(mask.shape)]
        + pair_specs(tokens, count),
        [pl.BlockSpec((tokens, pair), lambda i: (0, i)), part, part],
        [shaped((tokens, D), BF16)] + [shaped((2, count_y, tokens, D), BF16)] * 2,
        cost=21.0,
        name="attend_back",
    )(query, grad, mask, *keyvals, *keyvals)


def mix_kernel(attn, weight, carried, vecs, summed, middle, middle_low):
    value = carried[...].astype(F32) + (dot(attn[...], weight[0]) + vecs[0:1, :])
    summed[...] = value
    normed, _ = norm_stats(value)
    value = normed * vecs[1:2, :] + vecs[2:3, :]
    middle[...] = value
    middle_low[...] = value.astype(BF16)


def mix(attn, w_in, carried, vecs):
    tokens = attn.shape[0]
    full = fixed((tokens, D))
    return call(
        mix_kernel,
        (1,),
        [full, pl.BlockSpec((1, BLK, BLK), lambda i: (3, 0, 0)), full, fixed(vecs.shape)],
        [full, full, full],
        [shaped((tokens, D), F32), shaped((tokens, D), F32), shaped((tokens, D), BF16)],
        cost=4.0,
        name="mix",
    )(attn, w_in, carried, vecs)


def erf_part(hidden):
    return (1.0 + lax.erf(hidden * (0.5**0.5))) * 0.5


def up_kernel(split, where, middle_low, bias, *refs):
    pieces, (hidden, act, weight) = refs[:-3], refs[-3:]
    open_block(split, where, pieces, weight)
    value = dot(middle_low[...], weight[0]) + bias[0]
    hidden[...] = value
    act[...] = (value * erf_part(value)).astype(BF16)


def up(middle_low, chunk, bias):
    tokens = middle_low.shape[0]
    pieces, specs = chunk.pieces()
    part = pl.BlockSpec((tokens, BLK), lambda i, where: (0, i))
    return call(
        functools.partial(up_kernel, chunk.split_count),
        (FF // BLK,),
        [fixed((tokens, D)), pl.BlockSpec((1, 1, BLK), lambda i, where: (i, 0, 0))] + specs,
        [part, part, BLOCK],
        [shaped((tokens, FF), F32), shaped((tokens, FF), BF16), BLOCKS],
        prefetch=1,
        cost=8.0,
        name="up",
    )(chunk.where(), middle_low, bias, *pieces)


def down_kernel(split, where, act, middle, vecs, *refs):
    pieces, (summed, result, result_low, weight, total) = refs[:-5], refs[-5:]
    open_block(split, where, pieces, weight)
    spot = pl.program_id(0)
    value = dot(act[...], weight[0])

    @pl.when(spot == 0)
    def _():
        total[...] = value

    @pl.when(spot > 0)
    def _():
        total[...] += value

    @pl.when(spot == pl.num_programs(0) - 1)
    def _():
        value = middle[...] + (total[...] + vecs[0:1, :])
        summed[...] = value
        normed, _ = norm_stats(value)
        value = normed * vecs[1:2, :] + vecs[2:3, :]
        result[...] = value
        result_low[...] = value.astype(BF16)


def down(act, chunk, middle, vecs):
    tokens = act.shape[0]
    full = fixed((tokens, D))
    pieces, specs = chunk.pieces()
    return call(
        functools.partial(down_kernel, chunk.split_count),
        (FF // BLK,),
        [pl.BlockSpec((tokens, BLK), lambda i, where: (0, i)), full, fixed(vecs.shape)] + specs,
        [full, full, full, BLOCK],
        [shaped((tokens, D), F32), shaped((tokens, D), F32), shaped((tokens, D), BF16), BLOCKS],
        scratch=[pltpu.VMEM((tokens, D), F32)],
        prefetch=1,
        cost=8.0,
        name="down",
    )(chunk.where(), act, middle, vecs, *pieces)


def column_sum(value):
    return jnp.sum(value, axis=0, keepdims=True)


def close_kernel(flow, summed, gain, back_out, low_out, sums):
    grad = flow[...].astype(F32)
    normed, scale = norm_stats(summed[...])
    back = norm_back(grad, normed, scale, gain[...])
    back_out[...] = back
    low = back.astype(BF16)
    low_out[...] = low
    sums[0:1, :] = column_sum(low.astype(F32))
    sums[1:2, :] = column_sum(grad * normed)
    sums[2:3, :] = column_sum(grad)
    sums[3:8, :] = jnp.zeros((5, D), F32)


def close(flow, summed, gain):
    tokens = flow.shape[0]
    full = fixed((tokens, D))
    return call(
        close_kernel,
        (1,),
        [full, full, fixed((1, D))],
        [full, full, fixed((8, D))],
        [shaped((tokens, D), F32), shaped((tokens, D), BF16), shaped((8, D), F32)],
        cost=3.0,
        name="close",
    )(flow, summed, gain)


def feed_back_kernel(
    grad_two, ffn_low, summed_one, hidden, w_down, w_up, w_out, gain,
    hid_low, branch_low, attn_grad, grad_one, sums, bias_sums, total,
):
    spot = pl.program_id(0)

    @pl.when(spot == 0)
    def _():
        total[...] = grad_two[...]

    value = hidden[...]
    slope = erf_part(value) + value * jnp.exp(-0.5 * value * value) * ((2.0 * np.pi) ** -0.5)
    low = (dot_t(ffn_low[...], w_down[0]) * slope).astype(BF16)
    hid_low[...] = low
    bias_sums[0] = column_sum(low.astype(F32))
    total[...] += dot_t(low, w_up[0])

    @pl.when(spot == pl.num_programs(0) - 1)
    def _():
        grad = total[...]
        normed, scale = norm_stats(summed_one[...])
        back = norm_back(grad, normed, scale, gain[...])
        grad_one[...] = back
        low = back.astype(BF16)
        branch_low[...] = low
        sums[0:1, :] = column_sum(low.astype(F32))
        sums[1:2, :] = column_sum(grad * normed)
        sums[2:3, :] = column_sum(grad)
        sums[3:8, :] = jnp.zeros((5, D), F32)
        attn_grad[...] = dot_t(low, w_out[0]).astype(BF16)


def feed_back(grad_two, ffn_low, summed_one, hidden, w_down, w_up, w_in, gain):
    tokens = ffn_low.shape[0]
    full = fixed((tokens, D))
    part = pl.BlockSpec((tokens, BLK), lambda i: (0, i))
    weight = pl.BlockSpec((1, BLK, BLK), lambda i: (i, 0, 0))
    return call(
        feed_back_kernel,
        (FF // BLK,),
        [full, full, full, part, weight, weight, pl.BlockSpec((1, BLK, BLK), lambda i: (3, 0, 0)), fixed((1, D))],
        [part, full, full, full, fixed((8, D)), pl.BlockSpec((1, 1, BLK), lambda i: (i, 0, 0))],
        [
            shaped((tokens, FF), BF16),
            shaped((tokens, D), BF16),
            shaped((tokens, D), BF16),
            shaped((tokens, D), F32),
            shaped((8, D), F32),
            shaped((FF // BLK, 1, BLK), F32),
        ],
        scratch=[pltpu.VMEM((tokens, D), F32)],
        cost=15.0,
        name="feed_back",
    )(grad_two, ffn_low, summed_one, hidden, w_down, w_up, w_in, gain)


def input_back_kernel(count, grad_q, grad_one, weight, *refs):
    parts, (joined, result, sums, total) = refs[:count], refs[count:]
    spot = pl.program_id(0)

    @pl.when(spot == 0)
    def _():
        joined[...] = grad_q[...]
        total[...] = grad_one[...]

    @pl.when(spot > 0)
    def _():
        joined[...] = sum(part[0].astype(F32) for part in parts).astype(BF16)

    low = joined[...]
    sums[0] = column_sum(low.astype(F32))
    total[...] += dot_t(low, weight[0])

    @pl.when(spot == pl.num_programs(0) - 1)
    def _():
        result[...] = total[...]


def input_back(grad_q, parts, grad_one, w_in):
    tokens = grad_q.shape[0]
    full = fixed((tokens, D))
    return call(
        functools.partial(input_back_kernel, len(parts)),
        (3,),
        [full, full, pl.BlockSpec((1, BLK, BLK), lambda i: (i, 0, 0))]
        + [pl.BlockSpec((1, tokens, D), lambda i: (jnp.maximum(i - 1, 0), 0, 0))] * len(parts),
        [pl.BlockSpec((tokens, D), lambda i: (0, i)), full, pl.BlockSpec((1, 1, D), lambda i: (i, 0, 0))],
        [shaped((tokens, 3 * D), BF16), shaped((tokens, D), F32), shaped((3, 1, D), F32)],
        scratch=[pltpu.VMEM((tokens, D), F32)],
        cost=8.0,
        name="input_back",
    )(grad_q, grad_one, w_in, *parts)


def gather_list(place, value, axis):
    return [value] + [place.take(value, axis, step) for step in range(1, place.size[axis])]


def project_step(place, carried_low, chunk, vector):
    parts = vector_parts(vector)
    bias_in = jnp.stack([parts[0], jnp.zeros((D,), F32), parts[1]])[:, None]
    query, keyval, w_in = project(carried_low, chunk, bias_in)
    keyvals = [keyval, *gather_list(place, keyval, "y")[1:], place.take(keyval, "core", 1)]
    return query, keyvals, w_in


def mix_step(query, keyvals, carried, w_in, vector, mask):
    parts = vector_parts(vector)
    attn_low = attend(query, keyvals, mask)
    return attn_low, *mix(attn_low, w_in, carried, jnp.stack([parts[2], parts[4], parts[5]]))


def up_step(mid_low, chunk, vector):
    return up(mid_low, chunk, vector[8 * D :].reshape(FF // BLK, 1, BLK))


def down_step(act_low, chunk, middle, vector):
    parts = vector_parts(vector)
    return down(act_low, chunk, middle, jnp.stack([parts[3], parts[6], parts[7]]))


def sum_kernel(count_one, first_half, sizes, where, *refs):
    sets = (refs[:4], refs[4:8]) if count_one is not None else (refs[:4],)
    outs, product = refs[4 * len(sets) : -1], refs[-1]
    x_at, y_at = where[1], where[2]
    extent_z, extent_x, extent_y, rows = sizes
    spot = pl.program_id(0)

    def multiply(left_mine, left_other, right_mine, right_other):
        left = jnp.concatenate([left_mine[...], left_other[...]], axis=0)
        right = jnp.concatenate([right_mine[...], right_other[...]], axis=0)
        product[...] = dot_tt(left, right)

    if len(sets) == 1:
        multiply(*sets[0])
    else:
        pl.when(spot < count_one)(lambda: multiply(*sets[0]))
        pl.when(spot >= count_one)(lambda: multiply(*sets[1]))
    cols = product.shape[1] // extent_y

    def put(y_first):
        for step_y in range(extent_y):
            from_col = pl.multiple_of(lax.rem(y_at + step_y, extent_y) * cols, cols)
            for step_x in range(extent_x):
                for step_z in range(extent_z):
                    row_block = step_z * extent_x + lax.rem(x_at + step_x, extent_x)
                    from_row = pl.multiple_of(row_block * rows, rows)
                    value = product[pl.ds(from_row, rows), pl.ds(from_col, cols)].astype(BF16)
                    if y_first:
                        outs[step_y][step_x, step_z, 0] = value
                    else:
                        outs[extent_y + step_x][step_y, step_z, 0] = value

    pl.when(spot < first_half)(lambda: put(True))
    pl.when(spot >= first_half)(lambda: put(False))


def partial_sums(place, sets):
    tokens = sets[0][0].shape[0]
    extent_z, extent_x, extent_y = (place.size[name] for name in ("z", "x", "y"))
    rows = BLK // (extent_z * extent_x)
    half = BLK // CORES
    cols = half // extent_y
    where = jnp.stack([place.at[name] for name in ("z", "x", "y", "core")]).astype(jnp.int32)
    counts = [max(one[0].shape[1], one[2].shape[1]) // BLK for one in sets]
    count = sum(counts)
    first_half = count // 2
    specs = []
    start = 0
    for one, amount in zip(sets, counts):

        def at(i, start=start, amount=amount):
            return jnp.clip(i - start, 0, amount - 1)

        many_left, many_right = one[0].shape[1] > BLK, one[2].shape[1] > BLK
        for first in (0, one[4]):
            specs.append(
                pl.BlockSpec(
                    (tokens, BLK),
                    lambda i, where, at=at, many=many_left, first=first: (0, first + (at(i) if many else 0)),
                )
            )
        specs += [
            pl.BlockSpec(
                (tokens, half),
                lambda i, where, at=at, many=many_right: (0, (at(i) * CORES if many else 0) + where[3]),
            )
        ] * 2
        start += amount
    part_y = (extent_x, extent_z, 1, rows, cols)
    part_x = (extent_y, extent_z, 1, rows, cols)
    spec_y = pl.BlockSpec(part_y, lambda i, where: (0, 0, jnp.minimum(i, first_half - 1), 0, 0))
    spec_x = pl.BlockSpec(part_x, lambda i, where: (0, 0, jnp.maximum(i - first_half, 0), 0, 0))
    outs = call(
        functools.partial(
            sum_kernel,
            counts[0] if len(sets) > 1 else None,
            first_half,
            (extent_z, extent_x, extent_y, rows),
        ),
        (count,),
        specs,
        [spec_y] * extent_y + [spec_x] * extent_x,
        [shaped((extent_x, extent_z, first_half, rows, cols), BF16)] * extent_y
        + [shaped((extent_y, extent_z, count - first_half, rows, cols), BF16)] * extent_x,
        scratch=[pltpu.VMEM((BLK, half), F32)],
        prefetch=1,
        cost=8.0,
        name="partial_sums",
    )(where, *[value for one in sets for value in one[:4]])
    return outs[:extent_y], outs[extent_y:]


class Summing:
    def __init__(self, place, ids, sets):
        self.place = place
        self.ids = ids
        if (BLK // (CORES * place.size["y"])) % 128:
            self.plain = True
            self.parts = self.by_y = self.by_x = ()
            self.groups = [sum_job_plain(place, one[0], one[2], "y")[None] for one in sets]
        else:
            self.plain = False
            sets = [(one[0], one[1], one[2], place.take(one[2], "core", 1), one[3]) for one in sets]
            self.parts = partial_sums(place, sets)
            self.by_y = self.by_x = ()
            self.groups = ()

    def first_y(self):
        if not self.plain:
            self.by_y = self.place.collect(self.parts[0], "y")

    def first_x(self):
        if not self.plain:
            self.by_x = self.place.collect(self.parts[1], "x")

    def second_x(self):
        if not self.plain:
            total = add_up(self.by_y)
            parts = [total[step].astype(BF16) for step in range(self.place.size["x"])]
            self.by_y = self.place.collect(parts, "x")

    def second_y(self):
        if not self.plain:
            total = add_up(self.by_x)
            parts = [total[step].astype(BF16) for step in range(self.place.size["y"])]
            self.by_x = self.place.collect(parts, "y")

    def third(self):
        if not self.plain:
            both = jnp.concatenate([add_up(self.by_y), add_up(self.by_x)], axis=1)
            self.groups = [self.place.swap_z(both.astype(BF16))]


def route_kernel(count, slots, scaling, spots, *refs):
    parts, (out, total) = refs[:count], refs[count:]
    at = 0
    for part in parts:
        for block in range(part.shape[1]):
            value = sum(part[addend, block].astype(F32) for addend in range(part.shape[0]))
            total[at] = (value * scaling).astype(BF16)
            at += 1
    total[at] = jnp.zeros(total.shape[1:], BF16)
    for ctx in range(out.shape[0]):
        for spot in range(out.shape[1]):
            if spot < slots:
                out[ctx, spot] = total[spots[ctx * slots + spot]]
            else:
                out[ctx, spot] = total[at]


def route(groups, spots, slots, wsh_count, scaling):
    rows, cols = groups[0].shape[2:]
    blocks = sum(group.shape[1] for group in groups)
    shape = (spots.shape[0] // slots, wsh_count, rows, cols)
    return call(
        functools.partial(route_kernel, len(groups), slots, scaling),
        (1,),
        [fixed(group.shape) for group in groups],
        fixed(shape),
        shaped(shape, BF16),
        scratch=[pltpu.VMEM((blocks + 1, rows, cols), BF16)],
        prefetch=1,
        cost=6.0,
        name="route",
    )(spots, *groups)


def rotate_kernel(quarters, where, grads, right, left, first, second, rotated, update, total, low, right_low):
    step = BLK // 4
    right_low[...] = right[0].astype(BF16)
    for at in range(4):
        rows = pl.ds(at * step, step)
        product = 0.0
        for source, quarter in enumerate(quarters):
            width = grads.shape[2]
            product = product + dot(
                grads[source, rows, :], right_low[pl.ds(quarter * width, width), :]
            )
        value = dot_tt(left[rows, :], product.astype(BF16))
        if at:
            total[...] += value
        else:
            total[...] = value
    for at in range(4):
        rows = pl.ds(at * step, step)
        turned = total[rows, :]
        rotated[rows, :] = turned.astype(BF16)
        first_new = DECAY_RATE * first[rows, :].astype(F32) + (1.0 - DECAY_RATE) * turned
        second_new = DECAY_RATE * second[rows, :].astype(F32) + (1.0 - DECAY_RATE) * turned * turned
        direction = first_new / (jnp.sqrt(second_new) + EPS_ADAM)
        low[rows, :] = dot_t(direction.astype(BF16), right_low[...]).astype(BF16)
    for at in range(4):
        rows = pl.ds(at * step, step)
        update[rows, :] = dot(left[rows, :], low[...]).astype(BF16)


def rotate(grads, quarters, right_bases, slot, left, first, second):
    full = fixed((BLK, BLK))
    return call(
        functools.partial(rotate_kernel, quarters),
        (1,),
        [
            fixed(grads.shape),
            pl.BlockSpec((1, BLK, BLK), lambda i, where: (where[0], 0, 0)),
            full,
            full,
            full,
        ],
        [full, full],
        [shaped((BLK, BLK), BF16)] * 2,
        scratch=[pltpu.VMEM((BLK, BLK), F32), pltpu.VMEM((BLK, BLK), BF16), pltpu.VMEM((BLK, BLK), BF16)],
        prefetch=1,
        cost=16.0,
        name="rotate",
    )(slot, grads, right_bases, left, first, second)


def pick_kernel(count, amount, table, *refs):
    parts, out = refs[:count], refs[count]
    first = pl.program_id(0) * amount

    def put(spot, part):
        out[spot] = parts[part][table[1, first + spot]]

    for spot in range(amount):
        for part in range(count):
            pl.when(table[0, first + spot] == part)(functools.partial(put, spot, part))


def pick(parts, table):
    blocks = table.shape[1]
    amount = 4
    shape = (blocks,) + parts[0].shape[1:]
    return call(
        functools.partial(pick_kernel, len(parts), amount),
        (blocks // amount,),
        [fixed(value.shape) for value in parts],
        pl.BlockSpec((amount,) + shape[1:], lambda i, table: (i, 0, 0)),
        shaped(shape, BF16),
        prefetch=1,
        cost=12.0,
        name="pick",
    )(table, *parts)


def left_order(place, left):
    tokens, cols = left.shape
    count_z, count_x = place.size["z"], place.size["x"]
    blocks = cols // BLK
    rows = BLK // (count_z * count_x)
    value = left.reshape(tokens, blocks, count_z, count_x, rows)
    value = jnp.roll(value, (-place.at["z"], -place.at["x"]), axis=(2, 3))
    return value.transpose(0, 3, 2, 1, 4).reshape(tokens, cols)


def right_halves(place, right):
    tokens, cols = right.shape
    count_y = place.size["y"]
    width = BLK // (CORES * count_y)
    value = right.reshape(tokens, cols // BLK, CORES, count_y, width)
    halves = []
    for step in range(CORES):
        half = lax.dynamic_index_in_dim(value, (place.at["core"] + step) % CORES, 2, False)
        half = jnp.roll(half, -place.at["y"], axis=2)
        halves.append(half.transpose(2, 0, 1, 3).reshape(count_y, tokens, -1))
    return halves


def sum_job_plain(place, left, right, first):
    count_z, count_x, count_y = place.size["z"], place.size["x"], place.size["y"]
    left = left_order(place, left)
    right_mine, right_other = right_halves(place, right)
    left_both = jnp.concatenate([left, place.take(left, "core", 1)], axis=0)
    right_both = jnp.concatenate([right_mine, place.take(right_other, "core", 1)], axis=1)
    partial = [
        lax.dot_general(left_both, right_both[step], (((0,), (0,)), ((), ())), preferred_element_type=F32)
        .astype(BF16)
        .reshape(count_x, count_z, -1, right_both.shape[2])
        for step in range(count_y)
    ]
    if first == "y":
        total = place.scatter(partial, "y").astype(BF16)
        total = place.scatter(total, "x").astype(BF16)
    else:
        parts = [[value[step] for value in partial] for step in range(count_x)]
        parts = [jnp.stack(part) for part in parts]
        total = place.scatter(parts, "x").astype(BF16)
        total = place.scatter(total, "y").astype(BF16)
    total = place.scatter(total, "z")
    rows = BLK // (count_z * count_x)
    width = BLK // (CORES * count_y)
    if left.shape[1] > BLK:
        return total.reshape(-1, rows, width)
    return total.reshape(rows, -1, width).transpose(1, 0, 2)


class EverySum:
    def __init__(self, place, value):
        self.place = place
        self.terms = [value]
        self.plain = place.size["y"] != 2 or place.size["x"] != 2

    def step(self, axis, bit=0):
        if self.plain:
            return
        value = sum(self.terms)
        if axis == "z":
            pairs = self.place.size["x"]
            swap = [
                (z * pairs + x, (z ^ bit) * pairs + x) for z in range(DEPTH_Z) for x in range(pairs)
            ]
            self.terms = [value, lax.ppermute(value, "wsh", swap)]
        else:
            self.terms = [value, self.place.take(value, axis, 1)]

    def total(self):
        if self.plain:
            return lax.psum(self.terms[0], ("ctx", "wsh"))
        return sum(self.terms)


def doc_ids(lengths, position):
    starts = jnp.cumsum(lengths) - lengths
    return jnp.sum((position[:, None] >= starts[None, :]).astype(jnp.int32), axis=1)


def to_owner(rows_value, wsh_count):
    slots = rows_value.shape[0]
    padded = jnp.pad(rows_value.astype(BF16), ((0, wsh_count - slots), (0, 0), (0, 0)))
    return lax.all_to_all(padded, "wsh", 0, 0, tiled=True).reshape(BLK, BLK)


def from_owner(whole, wsh_count, slots):
    cut = whole.astype(BF16).reshape(wsh_count, BLK // wsh_count, BLK)
    return lax.all_to_all(cut, "wsh", 0, 0, tiled=True)[:slots]


def on_device(
    stream_in,
    doc_lengths,
    cotangent,
    weights,
    vec_params,
    owner_slots,
    master,
    left_bases,
    right_bases,
    moment1,
    moment2,
    vec_moment1,
    vec_moment2,
):
    tokens = stream_in.shape[1]
    ctx_count = lax.axis_size("ctx")
    wsh_count = lax.axis_size("wsh")
    place = Place(ctx_count, wsh_count)
    seq_len = tokens * ctx_count
    scaling = (wsh_count * seq_len) ** (-0.5)
    slots_dev, rows_dev = master.shape[0], master.shape[1]
    slot_total = ctx_count * slots_dev
    count_y = place.size["y"]
    width = BLK // ctx_count

    core_of = (place.at["core"] + jnp.arange(CORES)) % CORES
    y_of = (place.at["y"] + jnp.arange(count_y)) % count_y
    ctx_of = (y_of[None, :] * CORES + core_of[:, None]).reshape(-1)
    key_pos = (ctx_of[:, None] * tokens + jnp.arange(tokens)[None, :]).reshape(-1)
    doc_keys = doc_ids(doc_lengths[0], key_pos)
    mask = jnp.where(doc_keys[:, None] == doc_keys[None, :tokens], 0.0, -1e30).astype(F32)

    chunks = [
        Gathering(place, weights[layer_at, first : first + 4], split_count)
        for layer_at, first, split_count in (
            (0, 0, 2),
            (0, 4, 2),
            (0, 8, 2),
            (1, 0, 2),
            (1, 4, 2),
            (1, 8, 4),
        )
    ]

    live = {}

    def settle():
        going = [chunk for chunk in chunks if chunk]
        state = [(chunk.held, chunk.crossed) for chunk in going]
        state, values = together(state, {name: live[name] for name in live})
        for chunk, (held, crossed) in zip(going, state):
            chunk.held, chunk.crossed = held, crossed
        live.update(values)

    def finish(spot):
        chunk = chunks[spot]
        chunk.step_core()
        chunks[spot] = None
        return chunk

    def keyvals_of(layer_at):
        keyvals = live[f"keyvals{layer_at}"]
        return keyvals + [place.take(value, "core", 1) for value in keyvals[1:count_y]]

    kept = [{}, {}]
    chunks[0].step_z()
    settle()
    chunks[0].step_x()
    chunks[1].step_z()
    settle()
    chunks[0].step_y()
    chunks[1].step_x()
    chunks[2].step_z()
    settle()
    chunks[1].step_y()
    chunks[2].step_x()
    chunks[3].step_z()
    query_0, live["keyvals0"], w_in_0 = project_step(place, stream_in[0], finish(0), vec_params[0])
    live["query"] = query_0
    settle()
    chunks[2].step_y()
    chunks[3].step_x()
    chunks[4].step_z()
    keyvals_0 = keyvals_of(0)
    query_0 = live["query"]
    attn_0, summed_one_0, middle_0, mid_low_0 = mix_step(
        query_0, keyvals_0, stream_in[0], w_in_0, vec_params[0], mask
    )
    hidden_0, live["act"], w_up_0 = up_step(mid_low_0, finish(1), vec_params[0])
    settle()
    chunks[3].step_y()
    chunks[4].step_x()
    chunks[5].step_z()
    act_0 = live["act"]
    summed_two_0, live["result"], live["result_low"], w_down_0 = down_step(
        act_0, finish(2), middle_0, vec_params[0]
    )
    live["left"] = left_bases
    settle()
    chunks[4].step_y()
    chunks[5].step_x()
    result_0, result_low_0 = live["result"], live["result_low"]
    query_1, live["keyvals1"], w_in_1 = project_step(place, result_low_0, finish(3), vec_params[1])
    live["query"] = query_1
    live["left"] = to_owner(live["left"], wsh_count)
    live["first"] = moment1
    settle()
    chunks[5].step_y()
    live["first"] = to_owner(live["first"], wsh_count)
    live["second"] = moment2
    keyvals_1 = keyvals_of(1)
    query_1 = live["query"]
    attn_1, summed_one_1, middle_1, mid_low_1 = mix_step(
        query_1, keyvals_1, result_0, w_in_1, vec_params[1], mask
    )
    hidden_1, live["act"], w_up_1 = up_step(mid_low_1, finish(4), vec_params[1])
    settle()
    act_1 = live["act"]
    summed_two_1, _, result_low_1, w_down_1 = down_step(act_1, finish(5), middle_1, vec_params[1])
    stream_out = result_low_1[None]

    blocks = [(w_in_0, w_up_0, w_down_0), (w_in_1, w_up_1, w_down_1)]
    lefts = [
        (stream_in[0], attn_0, mid_low_0, act_0),
        (result_low_0, attn_1, mid_low_1, act_1),
    ]
    crossed = [
        (place.take(jnp.concatenate(values[:3], axis=1), "core", 1), place.take(values[3], "core", 1))
        for values in lefts
    ]
    summed = [(summed_one_0, summed_two_0), (summed_one_1, summed_two_1)]
    hidden = [hidden_0, hidden_1]
    queries = [query_0, query_1]
    keyvals_all = [keyvals_0, keyvals_1]
    gains = [
        (vec_params[layer_at][None, 4 * D : 5 * D], vec_params[layer_at][None, 6 * D : 7 * D])
        for layer_at in range(LAYERS)
    ]
    live = {
        "crossed": crossed,
        "left": live["left"],
        "first": live["first"],
        "second": to_owner(live["second"], wsh_count),
    }
    jobs = []
    vec_terms = [None] * LAYERS

    every = []

    def settle_back():
        state = [(job.parts, job.by_y, job.by_x, job.groups) for job in jobs]
        state, values, terms = together(state, dict(live), [one.terms for one in every])
        for one, value in zip(every, terms):
            one.terms = value
        for job, fields in zip(jobs, state):
            job.parts, job.by_y, job.by_x, job.groups = fields
        live.update(values)

    def begin(layer_at, first_block, *sets):
        ids = [layer_at * NBLK + first_block + spot for spot in range(4)]
        jobs.append(
            Summing(
                place,
                ids,
                [
                    (lefts[layer_at][spot], live["crossed"][layer_at][spot // 3], right, spot % 3)
                    for spot, right in sets
                ],
            )
        )
        return jobs[-1]

    def close_step(layer_at, flow):
        live["two"], live["ffn"], live["sums_two"] = close(flow, summed[layer_at][1], gains[layer_at][1])

    def down_job(layer_at):
        return begin(layer_at, 8, (3, live["ffn"]))

    def in_job(layer_at):
        return begin(layer_at, 0, (0, live["joined"]), (1, live["branch_in"]))

    def up_job(layer_at):
        return begin(layer_at, 4, (2, live["hid"]))

    def feed_step(layer_at):
        w_in, w_up, w_down = blocks[layer_at]
        live["hid"], live["branch"], attn_grad, live["one"], live["sums_one"], live["sums_up"] = feed_back(
            live["two"], live["ffn"], summed[layer_at][0], hidden[layer_at], w_down, w_up, w_in, gains[layer_at][0]
        )
        live["attn_grad"] = attn_grad

    def attend_step(layer_at):
        live["grad_q"], mine, other = attend_back(
            queries[layer_at], keyvals_all[layer_at], live["attn_grad"], mask
        )
        live["pair"] = [mine, other]

    def send_step():
        mine, other = live["pair"]
        arrived = place.take(other, "core", 1)
        sums = [mine[:, step].astype(F32) + arrived[:, step].astype(F32) for step in range(count_y)]
        live["kv"] = [sums[0]] + [
            place.take(sums[step].astype(BF16), "y", -step) for step in range(1, count_y)
        ]

    def input_step(layer_at):
        live["joined"], grad_x, in_sums = input_back(live["grad_q"], live["kv"], live["one"], blocks[layer_at][0])
        sums_two, sums_one = live["sums_two"], live["sums_one"]
        vec_terms[layer_at] = jnp.concatenate(
            [
                in_sums[0, 0],
                in_sums[2, 0],
                sums_one[0],
                sums_two[0],
                sums_one[1:3].reshape(-1),
                sums_two[1:3].reshape(-1),
                live["sums_up"].reshape(-1),
            ]
        )
        live["branch_in"] = live["branch"]
        return grad_x

    close_step(1, cotangent[0])
    down_1 = down_job(1)
    feed_step(1)
    settle_back()
    down_1.first_y()
    down_1.first_x()
    up_1 = up_job(1)
    settle_back()
    down_1.second_x()
    down_1.second_y()
    up_1.first_y()
    up_1.first_x()
    attend_step(1)
    settle_back()
    send_step()
    down_1.third()
    up_1.second_x()
    settle_back()
    up_1.second_y()
    grad_flow = input_step(1)
    close_step(0, grad_flow)
    settle_back()
    up_1.third()
    in_1 = in_job(1)
    down_0 = down_job(0)
    settle_back()
    in_1.first_y()
    in_1.first_x()
    feed_step(0)
    settle_back()
    in_1.second_x()
    in_1.second_y()
    down_0.first_y()
    down_0.first_x()
    attend_step(0)
    settle_back()
    send_step()
    in_1.third()
    down_0.second_x()
    down_0.second_y()
    up_0 = up_job(0)
    settle_back()
    down_0.third()
    up_0.first_y()
    up_0.first_x()
    grad_flow = input_step(0)
    every.append(EverySum(place, jnp.stack(vec_terms)))
    settle_back()
    every[0].step("core")
    up_0.second_x()
    up_0.second_y()
    in_0 = in_job(0)
    settle_back()
    up_0.third()
    every[0].step("y")
    in_0.first_y()
    in_0.first_x()
    settle_back()
    every[0].step("x")
    in_0.second_x()
    in_0.second_y()
    settle_back()
    every[0].step("z", 1)
    in_0.third()
    settle_back()
    every[0].step("z", 2)
    stream_grad = grad_flow[None]
    vec_grads = every[0].total() * scaling
    groups = [group for job in jobs for group in job.groups]
    ids = [block for job in jobs for block in job.ids]

    owner_flat = owner_slots.reshape(-1)
    block_count = LAYERS * NBLK
    owner_sorted = jnp.stack([owner_flat[block] for block in ids])
    picks = owner_sorted[None, :] == jnp.arange(slot_total, dtype=jnp.int32)[:, None]
    spots = jnp.where(
        jnp.any(picks, axis=1), jnp.argmax(picks, axis=1).astype(jnp.int32), block_count
    )
    by_slot = route(groups, spots, slots_dev, wsh_count, scaling)

    arrived = lax.all_to_all(
        by_slot.reshape(ctx_count * wsh_count, rows_dev, width), ("ctx", "wsh"), 0, 0, tiled=True
    )
    quarter_parts = []
    for step in range(ctx_count):
        step_y, step_core = step // CORES, step % CORES
        to_ctx = ((place.at["y"] + step_y) % count_y) * CORES + (place.at["core"] + step_core) % CORES
        part = lax.dynamic_index_in_dim(by_slot, to_ctx, 0, False)[:slots_dev]
        pairs = [
            (y * CORES + core, ((y + step_y) % count_y) * CORES + (core + step_core) % CORES)
            for y in range(count_y)
            for core in range(CORES)
        ]
        quarter_parts.append(lax.ppermute(part, "ctx", pairs) if step else part)
    arrived, quarter_parts = together(arrived, quarter_parts)
    quarters = [(source % CORES) * count_y + source // CORES for source in range(ctx_count)]
    slot_own = jnp.minimum(lax.axis_index("wsh"), slots_dev - 1).reshape(1)
    rotated_own, update_own = rotate(
        arrived.reshape(ctx_count, BLK, width), quarters, right_bases, slot_own, live["left"], live["first"], live["second"]
    )

    by_rows = jnp.stack(quarter_parts)
    by_source = [
        lax.dynamic_index_in_dim(
            by_rows,
            ((place.at["y"] - source // CORES) % count_y) * CORES + (place.at["core"] - source % CORES) % CORES,
            0,
            False,
        )
        for source in range(ctx_count)
    ]
    by_source = jnp.stack([by_source[quarters.index(quarter)] for quarter in range(ctx_count)])
    block_grads = by_source.transpose(1, 2, 0, 3).reshape(slots_dev, rows_dev, BLK).astype(F32)
    update = from_owner(update_own, wsh_count, slots_dev)
    update, block_grads, vec_grads = together(update, block_grads, vec_grads)
    master_low = (master - LR_BLOCK * update.astype(F32)).astype(BF16)
    master_low, update, rotated_own = together(master_low, update, rotated_own)
    parts = gather_list(place, master_low, "y")
    rotated = from_owner(rotated_own, wsh_count, slots_dev)
    across = place.take(master_low, "core", 1)
    new_master = master - LR_BLOCK * update.astype(F32)
    parts = parts + [across] + [place.take(value, "core", 1) for value in parts[1:]]
    owner_ctx, owner_at = owner_flat // slots_dev, owner_flat % slots_dev
    step_y = (owner_ctx // CORES - place.at["y"]) % count_y
    step_core = (owner_ctx % CORES - place.at["core"]) % CORES
    table = jnp.stack([step_core * count_y + step_y, owner_at]).astype(jnp.int32)
    new_weights = pick(parts, table).reshape(LAYERS, NBLK, rows_dev, BLK)
    new_weights, new_master, rotated = together(new_weights, new_master, rotated)
    rotated = rotated.astype(F32)

    new_moment1 = DECAY_RATE * moment1 + (1.0 - DECAY_RATE) * rotated
    new_moment2 = DECAY_RATE * moment2 + (1.0 - DECAY_RATE) * rotated * rotated

    new_vec_moment1 = DECAY_RATE * vec_moment1 + (1.0 - DECAY_RATE) * vec_grads
    new_vec_moment2 = DECAY_RATE * vec_moment2 + (1.0 - DECAY_RATE) * vec_grads * vec_grads
    new_vec_params = vec_params - LR_VEC * new_vec_moment1 / (jnp.sqrt(new_vec_moment2) + EPS_ADAM)
    return (
        stream_out,
        stream_grad,
        block_grads,
        new_moment1,
        new_moment2,
        new_master,
        new_weights,
        vec_grads,
        new_vec_params,
        new_vec_moment1,
        new_vec_moment2,
    )


def solution(mesh):
    rows = P("ctx", "wsh", None)
    placed = (
        P("wsh", "ctx", None),
        P("wsh", None),
        P("wsh", "ctx", None),
        P(None, None, "wsh", None),
        P(),
        P(),
        rows,
        rows,
        P("ctx", None, None),
        rows,
        rows,
        P(),
        P(),
    )
    return jax.shard_map(
        on_device,
        mesh=mesh,
        in_specs=placed,
        out_specs=(
            P("wsh", "ctx", None),
            P("wsh", "ctx", None),
            rows,
            rows,
            rows,
            rows,
            P(None, None, "wsh", None),
            P(),
            P(),
            P(),
            P(),
        ),
        check_vma=False,
    )
```

```python
import functools

import jax
import jax.numpy as jnp
import numpy as np
from jax import lax
from jax.experimental import pallas as pl
from jax.experimental.pallas import tpu as pltpu
from jax.sharding import PartitionSpec as P

D = 1024
HEADS = 16
HEAD_DIM = 64
FF = 4096
BLK = 1024
LAYERS = 2
NBLK = 12
CORES = 2
DEPTH_Z = 4

EPS_NORM = 1e-05
EPS_ADAM = 1e-08
LR_BLOCK = 0.1
LR_VEC = 0.25
DECAY_RATE = 0.5
VMEM_BYTES = 56 * 1024 * 1024
BF16 = jnp.bfloat16
F32 = jnp.float32


class Place:
    def __init__(self, ctx_count, wsh_count):
        self.size = {
            "core": CORES,
            "y": ctx_count // CORES,
            "z": DEPTH_Z,
            "x": wsh_count // DEPTH_Z,
        }
        ctx_at = lax.axis_index("ctx")
        wsh_at = lax.axis_index("wsh")
        self.at = {
            "core": ctx_at % CORES,
            "y": ctx_at // CORES,
            "z": wsh_at // self.size["x"],
            "x": wsh_at % self.size["x"],
        }

    def take(self, value, axis, step):
        name, slow, fast = {
            "core": ("ctx", "y", "core"),
            "y": ("ctx", "y", "core"),
            "z": ("wsh", "z", "x"),
            "x": ("wsh", "z", "x"),
        }[axis]
        extent = self.size[axis]
        pairs = []
        for slow_at in range(self.size[slow]):
            for fast_at in range(self.size[fast]):
                if axis == fast:
                    other = (slow_at, (fast_at + step) % extent)
                else:
                    other = ((slow_at + step) % extent, fast_at)
                pairs.append(
                    (
                        other[0] * self.size[fast] + other[1],
                        slow_at * self.size[fast] + fast_at,
                    )
                )
        return lax.ppermute(value, name, pairs)

    def gather(self, value, axis):
        steps = range(1, self.size[axis])
        return jnp.stack([value] + [self.take(value, axis, step) for step in steps])

    def collect(self, values, axis):
        steps = range(1, self.size[axis])
        return [values[0]] + [self.take(values[step], axis, -step) for step in steps]

    def swap_z(self, values):
        count_x = self.size["x"]
        lines = [[z * count_x + x for z in range(self.size["z"])] for x in range(count_x)]
        return lax.all_to_all(values, "wsh", 0, 0, tiled=True, axis_index_groups=lines)

    def scatter(self, values, axis):
        total = values[0].astype(F32)
        for step in range(1, self.size[axis]):
            total = total + self.take(values[step], axis, -step).astype(F32)
        return total


def vector_parts(vector):
    pieces = [vector[spot * D : (spot + 1) * D] for spot in range(8)]
    return pieces + [vector[8 * D :]]


def dot(left, right):
    return jnp.dot(left, right, preferred_element_type=F32)


def dot_t(left, right):
    return lax.dot_general(left, right, (((1,), (1,)), ((), ())), preferred_element_type=F32)


def after(value, *others):
    return lax.optimization_barrier((value,) + others)[0]


def together(*values):
    return lax.optimization_barrier(values)


def add_up(values):
    return sum(value.astype(F32) for value in values)


class Gathering:
    def __init__(self, place, shard, split_count):
        self.place = place
        self.count, self.rows, _ = shard.shape
        half_rows, half_cols = self.rows // 2, BLK // 2
        has_y = place.size["y"] == 2
        self.split_count = split_count if has_y else 0
        whole_count = self.count - self.split_count
        mine = lax.dynamic_slice_in_dim(shard, place.at["core"] * half_rows, half_rows, 1)
        whole = mine[self.split_count :]
        pieces = [
            part
            for block in range(whole_count)
            for part in (whole[block, :, :half_cols], whole[block, :, half_cols:])
        ]
        parts = []
        if pieces:
            parts.append(jnp.stack(pieces))
        if has_y:
            parts.insert(
                0,
                lax.dynamic_slice_in_dim(
                    mine[: self.split_count], place.at["y"] * half_cols, half_cols, 2
                ),
            )
        self.held = [jnp.concatenate(parts)]
        self.crossed = []

    def step_z(self):
        piece = self.held[0]
        copies = jnp.broadcast_to(piece[None], (self.place.size["z"],) + piece.shape)
        self.held = [self.place.swap_z(copies)]

    def step_x(self):
        self.held = gather_list(self.place, self.held[0], "x")

    def step_y(self):
        self.held = [jnp.stack(self.held)]
        if self.split_count:
            value = self.held[0][:, :, : self.split_count]
            self.held.append(self.place.take(value, "y", 1))
        self.crossed = [self.place.take(self.held[0], "core", 1)]

    def step_core(self):
        if self.split_count:
            self.crossed.append(self.place.take(self.held[1], "core", 1))

    def pieces(self):
        split, mine, crossed = self.split_count, self.held, self.crossed
        part = (mine[0].shape[:2]) + (1,) + mine[0].shape[3:]

        def spec(place_of):
            return pl.BlockSpec(part, lambda i, where: (0, 0, place_of(i), 0, 0))

        last = mine[0].shape[2] - 1
        low = spec(lambda i: jnp.where(i < split, i, 2 * i - split))
        high = spec(lambda i: jnp.minimum(jnp.where(i < split, split + 1, 2 * i - split + 1), last))
        operands = [mine[0], crossed[0], mine[0], crossed[0]]
        specs = [low, low, high, high]
        if split:
            operands += [mine[1], crossed[1]]
            specs += [spec(lambda i: jnp.minimum(i, split - 1))] * 2
        return operands, specs

    def where(self):
        return jnp.stack([self.place.at[name] for name in ("x", "y", "core")]).astype(jnp.int32)


def open_block(split, where, pieces, out):
    spot = pl.program_id(0)
    extent_x, extent_z, _, half_rows, half_cols = pieces[0].shape
    x_at, y_at, core_at = where[0], where[1], where[2]

    def put(first_col, sources):
        low_col = pl.ds(pl.multiple_of(first_col * half_cols, half_cols), half_cols)
        high_col = pl.ds(pl.multiple_of((1 - first_col) * half_cols, half_cols), half_cols)
        for step_x in range(extent_x):
            for z in range(extent_z):
                base = (z * extent_x + lax.rem(x_at + step_x, extent_x)) * 2
                mine = pl.ds(pl.multiple_of((base + core_at) * half_rows, half_rows), half_rows)
                other = pl.ds(pl.multiple_of((base + 1 - core_at) * half_rows, half_rows), half_rows)
                out[0, mine, low_col] = sources[0][step_x, z, 0]
                out[0, other, low_col] = sources[1][step_x, z, 0]
                out[0, mine, high_col] = sources[2][step_x, z, 0]
                out[0, other, high_col] = sources[3][step_x, z, 0]

    if split:
        pl.when(spot < split)(lambda: put(y_at, list(pieces[:2]) + list(pieces[4:])))
        pl.when(spot >= split)(lambda: put(0, pieces[:4]))
    else:
        put(0, pieces[:4])


def call(body, grid, in_specs, out_specs, out_shape, scratch=(), prefetch=0, cost=1.0, name=None):
    return pl.pallas_call(
        body,
        grid_spec=pltpu.PrefetchScalarGridSpec(
            num_scalar_prefetch=prefetch,
            grid=grid,
            in_specs=in_specs,
            out_specs=out_specs,
            scratch_shapes=list(scratch),
        ),
        out_shape=out_shape,
        compiler_params=pltpu.CompilerParams(vmem_limit_bytes=VMEM_BYTES),
        cost_estimate=pl.CostEstimate(flops=int(cost * 2e7), bytes_accessed=0, transcendentals=0),
        name=name,
    )


def shaped(shape, dtype):
    return jax.ShapeDtypeStruct(shape, dtype)


def fixed(shape):
    return pl.BlockSpec(shape, lambda *at: (0,) * len(shape))


def norm_stats(summed):
    average = jnp.mean(summed, axis=-1, keepdims=True)
    centred = summed - average
    variance = jnp.mean(centred * centred, axis=-1, keepdims=True)
    scale = lax.rsqrt(variance + EPS_NORM)
    return centred * scale, scale


def norm_back(grad, normed, scale, gain):
    flow = grad * gain
    return (
        flow
        - jnp.mean(flow, axis=-1, keepdims=True)
        - normed * jnp.mean(flow * normed, axis=-1, keepdims=True)
    ) * scale


BLOCK = pl.BlockSpec((1, BLK, BLK), lambda i, *at: (i, 0, 0))
BLOCKS = jax.ShapeDtypeStruct((4, BLK, BLK), BF16)


def project_kernel(split, where, x_low, bias, *refs):
    pieces, (query, keyval, weight) = refs[:-3], refs[-3:]
    open_block(split, where, pieces, weight)

    def value():
        return (dot(x_low[...], weight[0]) + bias[0]).astype(BF16)

    @pl.when(pl.program_id(0) == 0)
    def _():
        query[...] = value() * HEAD_DIM ** (-0.5)

    @pl.when((pl.program_id(0) > 0) & (pl.program_id(0) < 3))
    def _():
        keyval[...] = value()


def project(x_low, chunk, bias):
    tokens = x_low.shape[0]
    pieces, specs = chunk.pieces()
    return call(
        functools.partial(project_kernel, chunk.split_count),
        (4,),
        [fixed((tokens, D)), pl.BlockSpec((1, 1, D), lambda i, where: (jnp.minimum(i, 2), 0, 0))] + specs,
        [
            fixed((tokens, D)),
            pl.BlockSpec((tokens, D), lambda i, where: (0, jnp.clip(i - 1, 0, 1))),
            BLOCK,
        ],
        [shaped((tokens, D), BF16), shaped((tokens, 2 * D), BF16), BLOCKS],
        prefetch=1,
        cost=8.0,
        name="project",
    )(chunk.where(), x_low, bias, *pieces)


def head_probs(query_h, keys_h, masks):
    scores = [
        dot_t(key, query_h) + mask for key, mask in zip(keys_h, masks)
    ]
    peak = functools.reduce(
        jnp.maximum, [jnp.max(score, axis=0, keepdims=True) for score in scores]
    )
    scores = [jnp.exp(score - peak) for score in scores]
    total = sum(jnp.sum(score, axis=0, keepdims=True) for score in scores)
    inverse = 1.0 / total
    return [score * inverse for score in scores]


def dot_tt(left, right):
    return lax.dot_general(left, right, (((0,), (0,)), ((), ())), preferred_element_type=F32)


def head_of(ref, head):
    return ref[:, pl.ds(head * HEAD_DIM, HEAD_DIM)]


def attend_kernel(count, tokens, query, mask, *refs):
    keys, values, out = refs[:count], refs[count : 2 * count], refs[-1]
    masks = [mask[pl.ds(spot * tokens, tokens), :] for spot in range(count)]
    mixed = []
    for head in range(2):
        probs = head_probs(head_of(query, head), [head_of(key, head) for key in keys], masks)
        mixed.append(
            sum(dot_tt(head_of(value, head), prob.astype(BF16)) for value, prob in zip(values, probs))
        )
    out[...] = jnp.concatenate(mixed, axis=0).T.astype(BF16)


def pair_specs(tokens, count):
    pair = 2 * HEAD_DIM
    half = D // pair
    return (
        [pl.BlockSpec((tokens, pair), lambda i: (0, i))] * count
        + [pl.BlockSpec((tokens, pair), lambda i: (0, half + i))] * count
    )


def attend(query, keyvals, mask):
    tokens = query.shape[0]
    count = len(keyvals)
    pair = 2 * HEAD_DIM
    return call(
        functools.partial(attend_kernel, count, tokens),
        (D // pair,),
        [pl.BlockSpec((tokens, pair), lambda i: (0, i)), fixed(mask.shape)]
        + pair_specs(tokens, count),
        pl.BlockSpec((tokens, pair), lambda i: (0, i)),
        shaped((tokens, D), BF16),
        cost=14.0,
        name="attend",
    )(query, mask, *keyvals, *keyvals)


def attend_back_kernel(count, count_y, tokens, query, grad, mask, *refs):
    keys, values = refs[:count], refs[count : 2 * count]
    grad_q, mine, other = refs[2 * count :]
    masks = [mask[pl.ds(spot * tokens, tokens), :] for spot in range(count)]
    scale = HEAD_DIM ** (-0.5)
    grads_q = []
    grads_k = [[] for _ in range(count)]
    grads_v = [[] for _ in range(count)]
    for head in range(2):
        query_h = head_of(query, head)
        grad_h = head_of(grad, head)
        keys_h = [head_of(key, head) for key in keys]
        probs = head_probs(query_h, keys_h, masks)
        grad_probs = [dot_t(head_of(value, head), grad_h) for value in values]
        inner = sum(
            jnp.sum(prob * grad_prob, axis=0, keepdims=True)
            for prob, grad_prob in zip(probs, grad_probs)
        )
        flow_q = 0.0
        for spot in range(count):
            grad_score = (probs[spot] * (grad_probs[spot] - inner)).astype(BF16)
            flow_q = flow_q + dot_tt(keys_h[spot], grad_score)
            grads_k[spot].append(dot(grad_score, query_h))
            grads_v[spot].append(dot(probs[spot].astype(BF16), grad_h))
        grads_q.append(flow_q * scale)
    grad_q[...] = jnp.concatenate(grads_q, axis=0).T.astype(BF16)
    for spot in range(count):
        out = mine if spot < count_y else other
        out[spot % count_y, 0] = jnp.concatenate(grads_k[spot], axis=1).astype(BF16)
        out[spot % count_y, 1] = jnp.concatenate(grads_v[spot], axis=1).astype(BF16)


def attend_back(query, keyvals, grad, mask):
    tokens = query.shape[0]
    count = len(keyvals)
    count_y = count // CORES
    pair = 2 * HEAD_DIM
    part = pl.BlockSpec((count_y, 2, tokens, pair), lambda i: (0, 0, 0, i))
    return call(
        functools.partial(attend_back_kernel, count, count_y, tokens),
        (D // pair,),
        [pl.BlockSpec((tokens, pair), lambda i: (0, i))] * 2
        + [fixed(mask.shape)]
        + pair_specs(tokens, count),
        [pl.BlockSpec((tokens, pair), lambda i: (0, i)), part, part],
        [shaped((tokens, D), BF16)] + [shaped((count_y, 2, tokens, D), BF16)] * 2,
        cost=21.0,
        name="attend_back",
    )(query, grad, mask, *keyvals, *keyvals)


def mix_kernel(attn, weight, carried, vecs, summed, middle, middle_low):
    value = carried[...].astype(F32) + (dot(attn[...], weight[0]) + vecs[0:1, :])
    summed[...] = value
    normed, _ = norm_stats(value)
    value = normed * vecs[1:2, :] + vecs[2:3, :]
    middle[...] = value
    middle_low[...] = value.astype(BF16)


def mix(attn, w_in, carried, vecs):
    tokens = attn.shape[0]
    full = fixed((tokens, D))
    return call(
        mix_kernel,
        (1,),
        [full, pl.BlockSpec((1, BLK, BLK), lambda i: (3, 0, 0)), full, fixed(vecs.shape)],
        [full, full, full],
        [shaped((tokens, D), F32), shaped((tokens, D), F32), shaped((tokens, D), BF16)],
        cost=4.0,
        name="mix",
    )(attn, w_in, carried, vecs)


def erf_part(hidden):
    return (1.0 + lax.erf(hidden * (0.5**0.5))) * 0.5


def up_kernel(split, where, middle_low, bias, *refs):
    pieces, (hidden, act, weight) = refs[:-3], refs[-3:]
    open_block(split, where, pieces, weight)
    value = dot(middle_low[...], weight[0]) + bias[0]
    hidden[...] = value
    act[...] = (value * erf_part(value)).astype(BF16)


def up(middle_low, chunk, bias):
    tokens = middle_low.shape[0]
    pieces, specs = chunk.pieces()
    part = pl.BlockSpec((tokens, BLK), lambda i, where: (0, i))
    return call(
        functools.partial(up_kernel, chunk.split_count),
        (FF // BLK,),
        [fixed((tokens, D)), pl.BlockSpec((1, 1, BLK), lambda i, where: (i, 0, 0))] + specs,
        [part, part, BLOCK],
        [shaped((tokens, FF), F32), shaped((tokens, FF), BF16), BLOCKS],
        prefetch=1,
        cost=8.0,
        name="up",
    )(chunk.where(), middle_low, bias, *pieces)


def down_kernel(split, where, act, middle, vecs, *refs):
    pieces, (summed, result, result_low, weight, total) = refs[:-5], refs[-5:]
    open_block(split, where, pieces, weight)
    spot = pl.program_id(0)
    value = dot(act[...], weight[0])

    @pl.when(spot == 0)
    def _():
        total[...] = value

    @pl.when(spot > 0)
    def _():
        total[...] += value

    @pl.when(spot == pl.num_programs(0) - 1)
    def _():
        value = middle[...] + (total[...] + vecs[0:1, :])
        summed[...] = value
        normed, _ = norm_stats(value)
        value = normed * vecs[1:2, :] + vecs[2:3, :]
        result[...] = value
        result_low[...] = value.astype(BF16)


def down(act, chunk, middle, vecs):
    tokens = act.shape[0]
    full = fixed((tokens, D))
    pieces, specs = chunk.pieces()
    return call(
        functools.partial(down_kernel, chunk.split_count),
        (FF // BLK,),
        [pl.BlockSpec((tokens, BLK), lambda i, where: (0, i)), full, fixed(vecs.shape)] + specs,
        [full, full, full, BLOCK],
        [shaped((tokens, D), F32), shaped((tokens, D), F32), shaped((tokens, D), BF16), BLOCKS],
        scratch=[pltpu.VMEM((tokens, D), F32)],
        prefetch=1,
        cost=8.0,
        name="down",
    )(chunk.where(), act, middle, vecs, *pieces)


def column_sum(value):
    return jnp.sum(value, axis=0, keepdims=True)


def close_kernel(flow, summed, gain, back_out, low_out, sums):
    grad = flow[...].astype(F32)
    normed, scale = norm_stats(summed[...])
    back = norm_back(grad, normed, scale, gain[...])
    back_out[...] = back
    low = back.astype(BF16)
    low_out[...] = low
    sums[0:1, :] = column_sum(low.astype(F32))
    sums[1:2, :] = column_sum(grad * normed)
    sums[2:3, :] = column_sum(grad)
    sums[3:8, :] = jnp.zeros((5, D), F32)


def close(flow, summed, gain):
    tokens = flow.shape[0]
    full = fixed((tokens, D))
    return call(
        close_kernel,
        (1,),
        [full, full, fixed((1, D))],
        [full, full, fixed((8, D))],
        [shaped((tokens, D), F32), shaped((tokens, D), BF16), shaped((8, D), F32)],
        cost=3.0,
        name="close",
    )(flow, summed, gain)


def feed_back_kernel(
    grad_two, ffn_low, summed_one, hidden, w_down, w_up, w_out, gain,
    hid_low, branch_low, attn_grad, grad_one, sums, bias_sums, total,
):
    spot = pl.program_id(0)

    @pl.when(spot == 0)
    def _():
        total[...] = grad_two[...]

    value = hidden[...]
    slope = erf_part(value) + value * jnp.exp(-0.5 * value * value) * ((2.0 * np.pi) ** -0.5)
    low = (dot_t(ffn_low[...], w_down[0]) * slope).astype(BF16)
    hid_low[...] = low
    bias_sums[0] = column_sum(low.astype(F32))
    total[...] += dot_t(low, w_up[0])

    @pl.when(spot == pl.num_programs(0) - 1)
    def _():
        grad = total[...]
        normed, scale = norm_stats(summed_one[...])
        back = norm_back(grad, normed, scale, gain[...])
        grad_one[...] = back
        low = back.astype(BF16)
        branch_low[...] = low
        sums[0:1, :] = column_sum(low.astype(F32))
        sums[1:2, :] = column_sum(grad * normed)
        sums[2:3, :] = column_sum(grad)
        sums[3:8, :] = jnp.zeros((5, D), F32)
        attn_grad[...] = dot_t(low, w_out[0]).astype(BF16)


def feed_back(grad_two, ffn_low, summed_one, hidden, w_down, w_up, w_in, gain):
    tokens = ffn_low.shape[0]
    full = fixed((tokens, D))
    part = pl.BlockSpec((tokens, BLK), lambda i: (0, i))
    weight = pl.BlockSpec((1, BLK, BLK), lambda i: (i, 0, 0))
    return call(
        feed_back_kernel,
        (FF // BLK,),
        [full, full, full, part, weight, weight, pl.BlockSpec((1, BLK, BLK), lambda i: (3, 0, 0)), fixed((1, D))],
        [part, full, full, full, fixed((8, D)), pl.BlockSpec((1, 1, BLK), lambda i: (i, 0, 0))],
        [
            shaped((tokens, FF), BF16),
            shaped((tokens, D), BF16),
            shaped((tokens, D), BF16),
            shaped((tokens, D), F32),
            shaped((8, D), F32),
            shaped((FF // BLK, 1, BLK), F32),
        ],
        scratch=[pltpu.VMEM((tokens, D), F32)],
        cost=15.0,
        name="feed_back",
    )(grad_two, ffn_low, summed_one, hidden, w_down, w_up, w_in, gain)


def input_back_kernel(count, grad_q, grad_one, weight, *refs):
    parts, (joined, result, sums, total) = refs[:count], refs[count:]
    spot = pl.program_id(0)

    @pl.when(spot == 0)
    def _():
        joined[...] = grad_q[...]
        total[...] = grad_one[...]

    @pl.when(spot > 0)
    def _():
        joined[...] = sum(part[0].astype(F32) for part in parts).astype(BF16)

    low = joined[...]
    sums[0] = column_sum(low.astype(F32))
    total[...] += dot_t(low, weight[0])

    @pl.when(spot == pl.num_programs(0) - 1)
    def _():
        result[...] = total[...]


def input_back(grad_q, parts, grad_one, w_in):
    tokens = grad_q.shape[0]
    full = fixed((tokens, D))
    return call(
        functools.partial(input_back_kernel, len(parts)),
        (3,),
        [full, full, pl.BlockSpec((1, BLK, BLK), lambda i: (i, 0, 0))]
        + [pl.BlockSpec((1, tokens, D), lambda i: (jnp.maximum(i - 1, 0), 0, 0))] * len(parts),
        [pl.BlockSpec((tokens, D), lambda i: (0, i)), full, pl.BlockSpec((1, 1, D), lambda i: (i, 0, 0))],
        [shaped((tokens, 3 * D), BF16), shaped((tokens, D), F32), shaped((3, 1, D), F32)],
        scratch=[pltpu.VMEM((tokens, D), F32)],
        cost=8.0,
        name="input_back",
    )(grad_q, grad_one, w_in, *parts)


def gather_list(place, value, axis):
    return [value] + [place.take(value, axis, step) for step in range(1, place.size[axis])]


def project_step(place, carried_low, chunk, vector):
    parts = vector_parts(vector)
    bias_in = jnp.stack([parts[0], jnp.zeros((D,), F32), parts[1]])[:, None]
    query, keyval, w_in = project(carried_low, chunk, bias_in)
    keyvals = [keyval, *gather_list(place, keyval, "y")[1:], place.take(keyval, "core", 1)]
    return query, keyvals, w_in


def mix_step(query, keyvals, carried, w_in, vector, mask):
    parts = vector_parts(vector)
    attn_low = attend(query, keyvals, mask)
    return attn_low, *mix(attn_low, w_in, carried, jnp.stack([parts[2], parts[4], parts[5]]))


def up_step(mid_low, chunk, vector):
    return up(mid_low, chunk, vector[8 * D :].reshape(FF // BLK, 1, BLK))


def down_step(act_low, chunk, middle, vector):
    parts = vector_parts(vector)
    return down(act_low, chunk, middle, jnp.stack([parts[3], parts[6], parts[7]]))


def sum_kernel(count_one, first_half, sizes, turned, where, *refs):
    sets = (refs[:4], refs[4:8]) if count_one is not None else (refs[:4],)
    outs, shared, product = refs[4 * len(sets) : -2], refs[-2], refs[-1]
    x_at, y_at = where[1], where[2]
    extent_z, extent_x, extent_y, rows = sizes
    cols = BLK // (CORES * extent_y)
    spot = pl.program_id(0)

    def both(mine, other):
        return jnp.concatenate([mine[...], other[...]], axis=0)

    def share(left_mine, left_other, right_mine, right_other):
        shared[...] = (both(right_mine, right_other) if turned else both(left_mine, left_other)).T

    def multiply(left_mine, left_other, right_mine, right_other):
        value = both(left_mine, left_other) if turned else both(right_mine, right_other)
        product[...] = dot(shared[...], value).astype(BF16)

    pl.when(spot == 0)(lambda: share(*sets[0]))
    if len(sets) == 1:
        multiply(*sets[0])
    else:
        pl.when(spot == count_one)(lambda: share(*sets[1]))
        pl.when(spot < count_one)(lambda: multiply(*sets[0]))
        pl.when(spot >= count_one)(lambda: multiply(*sets[1]))

    def put(y_first):
        for step_y in range(extent_y):
            from_col = pl.multiple_of(lax.rem(y_at + step_y, extent_y) * cols, cols)
            for step_x in range(extent_x):
                for z in range(extent_z):
                    row_block = z * extent_x + lax.rem(x_at + step_x, extent_x)
                    from_row = pl.multiple_of(row_block * rows, rows)
                    if turned:
                        value = product[pl.ds(from_col, cols), pl.ds(from_row, rows)]
                    else:
                        value = product[pl.ds(from_row, rows), pl.ds(from_col, cols)]
                    if y_first:
                        outs[step_y][step_x, z, 0] = value
                    else:
                        outs[extent_y + step_x][step_y, z, 0] = value

    pl.when(spot < first_half)(lambda: put(True))
    pl.when(spot >= first_half)(lambda: put(False))


def partial_sums(place, sets):
    tokens = sets[0][0].shape[0]
    extent_z, extent_x, extent_y = (place.size[name] for name in ("z", "x", "y"))
    rows = BLK // (extent_z * extent_x)
    half = BLK // CORES
    cols = half // extent_y
    where = jnp.stack([place.at[name] for name in ("z", "x", "y", "core")]).astype(jnp.int32)
    counts = [max(one[0].shape[1], one[2].shape[1]) // BLK for one in sets]
    count = sum(counts)
    first_half = count // 2
    specs = []
    start = 0
    for one, amount in zip(sets, counts):

        def at(i, start=start, amount=amount):
            return jnp.clip(i - start, 0, amount - 1)

        many_left, many_right = one[0].shape[1] > BLK, one[2].shape[1] > BLK
        for first in (0, one[4]):
            specs.append(
                pl.BlockSpec(
                    (tokens, BLK),
                    lambda i, where, at=at, many=many_left, first=first: (0, first + (at(i) if many else 0)),
                )
            )
        specs += [
            pl.BlockSpec(
                (tokens, half),
                lambda i, where, at=at, many=many_right: (0, (at(i) * CORES if many else 0) + where[3]),
            )
        ] * 2
        start += amount
    turned = sets[0][0].shape[1] > BLK
    tile = (cols, rows) if turned else (rows, cols)
    part_y = (extent_x, extent_z, 1) + tile
    part_x = (extent_y, extent_z, 1) + tile
    spec_y = pl.BlockSpec(part_y, lambda i, where: (0, 0, jnp.minimum(i, first_half - 1), 0, 0))
    spec_x = pl.BlockSpec(part_x, lambda i, where: (0, 0, jnp.maximum(i - first_half, 0), 0, 0))
    outs = call(
        functools.partial(
            sum_kernel,
            counts[0] if len(sets) > 1 else None,
            first_half,
            (extent_z, extent_x, extent_y, rows),
            turned,
        ),
        (count,),
        specs,
        [spec_y] * extent_y + [spec_x] * extent_x,
        [shaped((extent_x, extent_z, first_half) + tile, BF16)] * extent_y
        + [shaped((extent_y, extent_z, count - first_half) + tile, BF16)] * extent_x,
        scratch=[
            pltpu.VMEM((half if turned else BLK, 2 * tokens), BF16),
            pltpu.VMEM((half, BLK) if turned else (BLK, half), BF16),
        ],
        prefetch=1,
        cost=8.0,
        name="partial_sums",
    )(where, *[value for one in sets for value in one[:4]])
    return outs[:extent_y], outs[extent_y:]


class Summing:
    def __init__(self, place, ids, sets):
        self.place = place
        self.ids = ids
        self.turned = False
        if (BLK // (CORES * place.size["y"])) % 128:
            self.plain = True
            self.parts = self.by_y = self.by_x = ()
            self.groups = [sum_job_plain(place, one[0], one[2], "y")[None] for one in sets]
        else:
            self.plain = False
            sets = [(one[0], one[1], one[2], place.take(one[2], "core", 1), one[3]) for one in sets]
            self.turned = sets[0][0].shape[1] > BLK
            self.parts = partial_sums(place, sets)
            self.by_y = self.by_x = ()
            self.groups = ()

    def first_y(self):
        if not self.plain:
            self.by_y = self.place.collect(self.parts[0], "y")

    def first_x(self):
        if not self.plain:
            self.by_x = self.place.collect(self.parts[1], "x")

    def second_x(self):
        if not self.plain:
            total = add_up(self.by_y)
            parts = [total[step].astype(BF16) for step in range(self.place.size["x"])]
            self.by_y = self.place.collect(parts, "x")

    def second_y(self):
        if not self.plain:
            total = add_up(self.by_x)
            parts = [total[step].astype(BF16) for step in range(self.place.size["y"])]
            self.by_x = self.place.collect(parts, "y")

    def third(self):
        if not self.plain:
            both = jnp.concatenate([add_up(self.by_y), add_up(self.by_x)], axis=1)
            self.groups = [self.place.swap_z(both.astype(BF16))]


def route_kernel(turned, slots, scaling, spots, *refs):
    parts, (out, total) = refs[: len(turned)], refs[len(turned) :]
    at = 0
    for part, turn in zip(parts, turned):
        for block in range(part.shape[1]):
            value = sum(part[addend, block].astype(F32) for addend in range(part.shape[0]))
            value = value * scaling
            total[at] = (value.T if turn else value).astype(BF16)
            at += 1
    total[at] = jnp.zeros(total.shape[1:], BF16)
    for ctx in range(out.shape[0]):
        for spot in range(out.shape[1]):
            if spot < slots:
                out[ctx, spot] = total[spots[ctx * slots + spot]]
            else:
                out[ctx, spot] = total[at]


def route(groups, turned, spots, slots, wsh_count, rows, scaling):
    cols = groups[0].shape[2] * groups[0].shape[3] // rows
    blocks = sum(group.shape[1] for group in groups)
    shape = (spots.shape[0] // slots, wsh_count, rows, cols)
    return call(
        functools.partial(route_kernel, turned, slots, scaling),
        (1,),
        [fixed(group.shape) for group in groups],
        fixed(shape),
        shaped(shape, BF16),
        scratch=[pltpu.VMEM((blocks + 1, rows, cols), BF16)],
        prefetch=1,
        cost=6.0,
        name="route",
    )(spots, *groups)


def rotate_kernel(quarters, grads, right, left, first, second, rotated, update, total, low):
    step = BLK // 4
    for at in range(4):
        rows = pl.ds(at * step, step)
        product = 0.0
        for source, quarter in enumerate(quarters):
            width = grads.shape[2]
            product = product + dot(
                grads[source, rows, :], right[pl.ds(quarter * width, width), :]
            )
        value = dot_tt(left[rows, :], product.astype(BF16))
        if at:
            total[...] += value
        else:
            total[...] = value
    for at in range(4):
        rows = pl.ds(at * step, step)
        turned = total[rows, :]
        rotated[rows, :] = turned.astype(BF16)
        first_new = DECAY_RATE * first[rows, :].astype(F32) + (1.0 - DECAY_RATE) * turned
        second_new = DECAY_RATE * second[rows, :].astype(F32) + (1.0 - DECAY_RATE) * turned * turned
        direction = first_new / (jnp.sqrt(second_new) + EPS_ADAM)
        low[rows, :] = dot_t(direction.astype(BF16), right[...]).astype(BF16)
    for at in range(4):
        rows = pl.ds(at * step, step)
        update[rows, :] = dot(left[rows, :], low[...]).astype(BF16)


def rotate(grads, quarters, right, left, first, second):
    full = fixed((BLK, BLK))
    return call(
        functools.partial(rotate_kernel, quarters),
        (1,),
        [fixed(grads.shape), full, full, full, full],
        [full, full],
        [shaped((BLK, BLK), BF16)] * 2,
        scratch=[pltpu.VMEM((BLK, BLK), F32), pltpu.VMEM((BLK, BLK), BF16)],
        cost=16.0,
        name="rotate",
    )(grads, right, left, first, second)


def pick_kernel(count, amount, table, *refs):
    parts, out = refs[:count], refs[count]
    first = pl.program_id(0) * amount

    def put(spot, part):
        out[spot] = parts[part][table[1, first + spot]]

    for spot in range(amount):
        for part in range(count):
            pl.when(table[0, first + spot] == part)(functools.partial(put, spot, part))


def pick(parts, table):
    blocks = table.shape[1]
    amount = 4
    shape = (blocks,) + parts[0].shape[1:]
    return call(
        functools.partial(pick_kernel, len(parts), amount),
        (blocks // amount,),
        [fixed(value.shape) for value in parts],
        pl.BlockSpec((amount,) + shape[1:], lambda i, table: (i, 0, 0)),
        shaped(shape, BF16),
        prefetch=1,
        cost=12.0,
        name="pick",
    )(table, *parts)


def left_order(place, left):
    tokens, cols = left.shape
    count_z, count_x = place.size["z"], place.size["x"]
    blocks = cols // BLK
    rows = BLK // (count_z * count_x)
    value = left.reshape(tokens, blocks, count_z, count_x, rows)
    value = jnp.roll(value, (-place.at["z"], -place.at["x"]), axis=(2, 3))
    return value.transpose(0, 3, 2, 1, 4).reshape(tokens, cols)


def right_halves(place, right):
    tokens, cols = right.shape
    count_y = place.size["y"]
    width = BLK // (CORES * count_y)
    value = right.reshape(tokens, cols // BLK, CORES, count_y, width)
    halves = []
    for step in range(CORES):
        half = lax.dynamic_index_in_dim(value, (place.at["core"] + step) % CORES, 2, False)
        half = jnp.roll(half, -place.at["y"], axis=2)
        halves.append(half.transpose(2, 0, 1, 3).reshape(count_y, tokens, -1))
    return halves


def sum_job_plain(place, left, right, first):
    count_z, count_x, count_y = place.size["z"], place.size["x"], place.size["y"]
    left = left_order(place, left)
    right_mine, right_other = right_halves(place, right)
    left_both = jnp.concatenate([left, place.take(left, "core", 1)], axis=0)
    right_both = jnp.concatenate([right_mine, place.take(right_other, "core", 1)], axis=1)
    partial = [
        lax.dot_general(left_both, right_both[step], (((0,), (0,)), ((), ())), preferred_element_type=F32)
        .astype(BF16)
        .reshape(count_x, count_z, -1, right_both.shape[2])
        for step in range(count_y)
    ]
    if first == "y":
        total = place.scatter(partial, "y").astype(BF16)
        total = place.scatter(total, "x").astype(BF16)
    else:
        parts = [[value[step] for value in partial] for step in range(count_x)]
        parts = [jnp.stack(part) for part in parts]
        total = place.scatter(parts, "x").astype(BF16)
        total = place.scatter(total, "y").astype(BF16)
    total = place.scatter(total, "z")
    rows = BLK // (count_z * count_x)
    width = BLK // (CORES * count_y)
    if left.shape[1] > BLK:
        return total.reshape(-1, rows, width)
    return total.reshape(rows, -1, width).transpose(1, 0, 2)


class EverySum:
    def __init__(self, place, value):
        self.place = place
        self.terms = [value]
        self.plain = place.size["y"] != 2 or place.size["x"] != 2

    def step(self, axis, bit=0):
        if self.plain:
            return
        value = sum(self.terms)
        if axis == "z":
            pairs = self.place.size["x"]
            swap = [
                (z * pairs + x, (z ^ bit) * pairs + x) for z in range(DEPTH_Z) for x in range(pairs)
            ]
            self.terms = [value, lax.ppermute(value, "wsh", swap)]
        else:
            self.terms = [value, self.place.take(value, axis, 1)]

    def total(self):
        if self.plain:
            return lax.psum(self.terms[0], ("ctx", "wsh"))
        return sum(self.terms)


def doc_ids(lengths, position):
    starts = jnp.cumsum(lengths) - lengths
    return jnp.sum((position[:, None] >= starts[None, :]).astype(jnp.int32), axis=1)


def fill_up(rows_value, wsh_count):
    slots = rows_value.shape[0]
    return jnp.pad(rows_value.astype(BF16), ((0, wsh_count - slots), (0, 0), (0, 0)))


def to_owner(padded):
    return lax.all_to_all(padded, "wsh", 0, 0, tiled=True).reshape(BLK, BLK)


def from_owner(whole, wsh_count):
    cut = whole.astype(BF16).reshape(wsh_count, BLK // wsh_count, BLK)
    return lax.all_to_all(cut, "wsh", 0, 0, tiled=True)


def on_device(
    stream_in,
    doc_lengths,
    cotangent,
    weights,
    vec_params,
    owner_slots,
    master,
    left_bases,
    right_bases,
    moment1,
    moment2,
    vec_moment1,
    vec_moment2,
):
    tokens = stream_in.shape[1]
    ctx_count = lax.axis_size("ctx")
    wsh_count = lax.axis_size("wsh")
    place = Place(ctx_count, wsh_count)
    seq_len = tokens * ctx_count
    scaling = (wsh_count * seq_len) ** (-0.5)
    slots_dev, rows_dev = master.shape[0], master.shape[1]
    slot_total = ctx_count * slots_dev
    count_y = place.size["y"]
    width = BLK // ctx_count

    core_of = (place.at["core"] + jnp.arange(CORES)) % CORES
    y_of = (place.at["y"] + jnp.arange(count_y)) % count_y
    ctx_of = (y_of[None, :] * CORES + core_of[:, None]).reshape(-1)
    key_pos = (ctx_of[:, None] * tokens + jnp.arange(tokens)[None, :]).reshape(-1)
    doc_keys = doc_ids(doc_lengths[0], key_pos)
    mask = jnp.where(doc_keys[:, None] == doc_keys[None, :tokens], 0.0, -1e30).astype(F32)

    chunks = [
        Gathering(place, weights[layer_at, first : first + 4], split_count)
        for layer_at, first, split_count in (
            (0, 0, 2),
            (0, 4, 2),
            (0, 8, 2),
            (1, 0, 2),
            (1, 4, 2),
            (1, 8, 4),
        )
    ]

    live = {}

    def settle():
        going = [chunk for chunk in chunks if chunk]
        state = [(chunk.held, chunk.crossed) for chunk in going]
        state, values = together(state, {name: live[name] for name in live})
        for chunk, (held, crossed) in zip(going, state):
            chunk.held, chunk.crossed = held, crossed
        live.update(values)

    def finish(spot):
        chunk = chunks[spot]
        chunk.step_core()
        chunks[spot] = None
        return chunk

    def keyvals_of(layer_at):
        keyvals = live[f"keyvals{layer_at}"]
        return keyvals + [place.take(value, "core", 1) for value in keyvals[1:count_y]]

    kept = [{}, {}]
    slot_own = jnp.minimum(lax.axis_index("wsh"), slots_dev - 1)
    live["left"] = fill_up(left_bases, wsh_count)
    live["first"] = fill_up(moment1, wsh_count)
    live["second"] = fill_up(moment2, wsh_count)
    live["right"] = lax.dynamic_index_in_dim(right_bases, slot_own, 0, False).astype(BF16)
    chunks[0].step_z()
    settle()
    chunks[0].step_x()
    chunks[1].step_z()
    settle()
    chunks[0].step_y()
    chunks[1].step_x()
    chunks[2].step_z()
    settle()
    chunks[1].step_y()
    chunks[2].step_x()
    chunks[3].step_z()
    query_0, live["keyvals0"], w_in_0 = project_step(place, stream_in[0], finish(0), vec_params[0])
    live["query"] = query_0
    settle()
    chunks[2].step_y()
    chunks[3].step_x()
    chunks[4].step_z()
    keyvals_0 = keyvals_of(0)
    query_0 = live["query"]
    attn_0, summed_one_0, middle_0, mid_low_0 = mix_step(
        query_0, keyvals_0, stream_in[0], w_in_0, vec_params[0], mask
    )
    hidden_0, live["act"], w_up_0 = up_step(mid_low_0, finish(1), vec_params[0])
    settle()
    chunks[3].step_y()
    chunks[4].step_x()
    chunks[5].step_z()
    act_0 = live["act"]
    summed_two_0, live["result"], live["result_low"], w_down_0 = down_step(
        act_0, finish(2), middle_0, vec_params[0]
    )
    settle()
    chunks[4].step_y()
    chunks[5].step_x()
    result_0, result_low_0 = live["result"], live["result_low"]
    query_1, live["keyvals1"], w_in_1 = project_step(place, result_low_0, finish(3), vec_params[1])
    live["query"] = query_1
    live["left"] = to_owner(live["left"])
    settle()
    chunks[5].step_y()
    live["first"] = to_owner(live["first"])
    keyvals_1 = keyvals_of(1)
    query_1 = live["query"]
    attn_1, summed_one_1, middle_1, mid_low_1 = mix_step(
        query_1, keyvals_1, result_0, w_in_1, vec_params[1], mask
    )
    hidden_1, live["act"], w_up_1 = up_step(mid_low_1, finish(4), vec_params[1])
    settle()
    act_1 = live["act"]
    summed_two_1, _, result_low_1, w_down_1 = down_step(act_1, finish(5), middle_1, vec_params[1])
    stream_out = result_low_1[None]

    blocks = [(w_in_0, w_up_0, w_down_0), (w_in_1, w_up_1, w_down_1)]
    lefts = [
        (stream_in[0], attn_0, mid_low_0, act_0),
        (result_low_0, attn_1, mid_low_1, act_1),
    ]
    crossed = [
        (place.take(jnp.concatenate(values[:3], axis=1), "core", 1), place.take(values[3], "core", 1))
        for values in lefts
    ]
    summed = [(summed_one_0, summed_two_0), (summed_one_1, summed_two_1)]
    hidden = [hidden_0, hidden_1]
    queries = [query_0, query_1]
    keyvals_all = [keyvals_0, keyvals_1]
    gains = [
        (vec_params[layer_at][None, 4 * D : 5 * D], vec_params[layer_at][None, 6 * D : 7 * D])
        for layer_at in range(LAYERS)
    ]
    live = {
        "crossed": crossed,
        "left": live["left"],
        "first": live["first"],
        "second": to_owner(live["second"]),
        "right": live["right"],
    }
    jobs = []
    vec_terms = [None] * LAYERS

    every = []

    def settle_back():
        state = [(job.parts, job.by_y, job.by_x, job.groups) for job in jobs]
        state, values, terms = together(state, dict(live), [one.terms for one in every])
        for one, value in zip(every, terms):
            one.terms = value
        for job, fields in zip(jobs, state):
            job.parts, job.by_y, job.by_x, job.groups = fields
        live.update(values)

    def begin(layer_at, first_block, *sets):
        ids = [layer_at * NBLK + first_block + spot for spot in range(4)]
        jobs.append(
            Summing(
                place,
                ids,
                [
                    (lefts[layer_at][spot], live["crossed"][layer_at][spot // 3], right, spot % 3)
                    for spot, right in sets
                ],
            )
        )
        return jobs[-1]

    def close_step(layer_at, flow):
        live["two"], live["ffn"], live["sums_two"] = close(flow, summed[layer_at][1], gains[layer_at][1])

    def down_job(layer_at):
        return begin(layer_at, 8, (3, live["ffn"]))

    def in_job(layer_at):
        return begin(layer_at, 0, (0, live["joined"]), (1, live["branch_in"]))

    def up_job(layer_at):
        return begin(layer_at, 4, (2, live["hid"]))

    def feed_step(layer_at):
        w_in, w_up, w_down = blocks[layer_at]
        live["hid"], live["branch"], attn_grad, live["one"], live["sums_one"], live["sums_up"] = feed_back(
            live["two"], live["ffn"], summed[layer_at][0], hidden[layer_at], w_down, w_up, w_in, gains[layer_at][0]
        )
        live["attn_grad"] = attn_grad

    def attend_step(layer_at):
        live["grad_q"], mine, other = attend_back(
            queries[layer_at], keyvals_all[layer_at], live["attn_grad"], mask
        )
        live["pair"] = [mine, other]

    def send_step():
        mine, other = live["pair"]
        arrived = place.take(other, "core", 1)
        sums = [mine[step].astype(F32) + arrived[step].astype(F32) for step in range(count_y)]
        live["kv"] = [sums[0]] + [
            place.take(sums[step].astype(BF16), "y", -step) for step in range(1, count_y)
        ]

    def input_step(layer_at):
        live["joined"], grad_x, in_sums = input_back(live["grad_q"], live["kv"], live["one"], blocks[layer_at][0])
        sums_two, sums_one = live["sums_two"], live["sums_one"]
        vec_terms[layer_at] = jnp.concatenate(
            [
                in_sums[0, 0],
                in_sums[2, 0],
                sums_one[0],
                sums_two[0],
                sums_one[1:3].reshape(-1),
                sums_two[1:3].reshape(-1),
                live["sums_up"].reshape(-1),
            ]
        )
        live["branch_in"] = live["branch"]
        return grad_x

    close_step(1, cotangent[0])
    down_1 = down_job(1)
    feed_step(1)
    settle_back()
    down_1.first_y()
    down_1.first_x()
    up_1 = up_job(1)
    settle_back()
    down_1.second_x()
    down_1.second_y()
    up_1.first_y()
    up_1.first_x()
    attend_step(1)
    settle_back()
    send_step()
    down_1.third()
    up_1.second_x()
    settle_back()
    up_1.second_y()
    grad_flow = input_step(1)
    close_step(0, grad_flow)
    settle_back()
    up_1.third()
    in_1 = in_job(1)
    down_0 = down_job(0)
    settle_back()
    in_1.first_y()
    in_1.first_x()
    feed_step(0)
    settle_back()
    in_1.second_x()
    in_1.second_y()
    down_0.first_y()
    down_0.first_x()
    attend_step(0)
    settle_back()
    send_step()
    in_1.third()
    down_0.second_x()
    down_0.second_y()
    up_0 = up_job(0)
    settle_back()
    down_0.third()
    up_0.first_y()
    up_0.first_x()
    grad_flow = input_step(0)
    every.append(EverySum(place, jnp.stack(vec_terms)))
    settle_back()
    every[0].step("core")
    up_0.second_x()
    up_0.second_y()
    in_0 = in_job(0)
    settle_back()
    up_0.third()
    every[0].step("y")
    in_0.first_y()
    in_0.first_x()
    settle_back()
    every[0].step("x")
    in_0.second_x()
    in_0.second_y()
    settle_back()
    every[0].step("z", 1)
    in_0.third()
    settle_back()
    every[0].step("z", 2)
    stream_grad = grad_flow[None]
    vec_grads = every[0].total() * scaling
    groups = [group for job in jobs for group in job.groups]
    turned = [job.turned for job in jobs for group in job.groups]
    ids = [block for job in jobs for block in job.ids]

    owner_flat = owner_slots.reshape(-1)
    block_count = LAYERS * NBLK
    owner_sorted = jnp.stack([owner_flat[block] for block in ids])
    picks = owner_sorted[None, :] == jnp.arange(slot_total, dtype=jnp.int32)[:, None]
    spots = jnp.where(
        jnp.any(picks, axis=1), jnp.argmax(picks, axis=1).astype(jnp.int32), block_count
    )
    by_slot = route(groups, turned, spots, slots_dev, wsh_count, rows_dev, scaling)

    arrived = lax.all_to_all(
        by_slot.reshape(ctx_count * wsh_count, rows_dev, width), ("ctx", "wsh"), 0, 0, tiled=True
    )
    quarter_parts = []
    for step in range(ctx_count):
        step_y, step_core = step // CORES, step % CORES
        to_ctx = ((place.at["y"] + step_y) % count_y) * CORES + (place.at["core"] + step_core) % CORES
        part = lax.dynamic_index_in_dim(by_slot, to_ctx, 0, False)[:slots_dev]
        pairs = [
            (y * CORES + core, ((y + step_y) % count_y) * CORES + (core + step_core) % CORES)
            for y in range(count_y)
            for core in range(CORES)
        ]
        quarter_parts.append(lax.ppermute(part, "ctx", pairs) if step else part)
    quarters = [(source % CORES) * count_y + source // CORES for source in range(ctx_count)]
    by_rows = jnp.stack(quarter_parts)
    by_source = [
        lax.dynamic_index_in_dim(
            by_rows,
            ((place.at["y"] - source // CORES) % count_y) * CORES + (place.at["core"] - source % CORES) % CORES,
            0,
            False,
        )
        for source in range(ctx_count)
    ]
    by_source = jnp.stack([by_source[quarters.index(quarter)] for quarter in range(ctx_count)])
    block_grads = by_source.transpose(1, 2, 0, 3).reshape(slots_dev, rows_dev, BLK).astype(F32)
    arrived, block_grads = together(arrived, block_grads)
    rotated_own, update_own = rotate(
        arrived.reshape(ctx_count, BLK, width), quarters, live["right"], live["left"], live["first"], live["second"]
    )

    update = from_owner(update_own, wsh_count)
    update, vec_grads = together(update, vec_grads)
    master_low = (master - LR_BLOCK * update[:slots_dev].astype(F32)).astype(BF16)
    master_low, update, rotated_own = together(master_low, update, rotated_own)
    parts = gather_list(place, master_low, "y")
    rotated = from_owner(rotated_own, wsh_count)
    across = place.take(master_low, "core", 1)
    new_master = master - LR_BLOCK * update[:slots_dev].astype(F32)
    parts = parts + [across] + [place.take(value, "core", 1) for value in parts[1:]]
    owner_ctx, owner_at = owner_flat // slots_dev, owner_flat % slots_dev
    step_y = (owner_ctx // CORES - place.at["y"]) % count_y
    step_core = (owner_ctx % CORES - place.at["core"]) % CORES
    table = jnp.stack([step_core * count_y + step_y, owner_at]).astype(jnp.int32)
    new_weights = pick(parts, table).reshape(LAYERS, NBLK, rows_dev, BLK)
    rotated, _ = together(rotated, (new_weights[0, 0, :8, :128], new_master[0, :8, :128]))
    rotated = rotated[:slots_dev].astype(F32)

    new_moment1 = DECAY_RATE * moment1 + (1.0 - DECAY_RATE) * rotated
    new_moment2 = DECAY_RATE * moment2 + (1.0 - DECAY_RATE) * rotated * rotated

    new_vec_moment1 = DECAY_RATE * vec_moment1 + (1.0 - DECAY_RATE) * vec_grads
    new_vec_moment2 = DECAY_RATE * vec_moment2 + (1.0 - DECAY_RATE) * vec_grads * vec_grads
    new_vec_params = vec_params - LR_VEC * new_vec_moment1 / (jnp.sqrt(new_vec_moment2) + EPS_ADAM)
    return (
        stream_out,
        stream_grad,
        block_grads,
        new_moment1,
        new_moment2,
        new_master,
        new_weights,
        vec_grads,
        new_vec_params,
        new_vec_moment1,
        new_vec_moment2,
    )


def solution(mesh):
    rows = P("ctx", "wsh", None)
    placed = (
        P("wsh", "ctx", None),
        P("wsh", None),
        P("wsh", "ctx", None),
        P(None, None, "wsh", None),
        P(),
        P(),
        rows,
        rows,
        P("ctx", None, None),
        rows,
        rows,
        P(),
        P(),
    )
    return jax.shard_map(
        on_device,
        mesh=mesh,
        in_specs=placed,
        out_specs=(
            P("wsh", "ctx", None),
            P("wsh", "ctx", None),
            rows,
            rows,
            rows,
            rows,
            P(None, None, "wsh", None),
            P(),
            P(),
            P(),
            P(),
        ),
        check_vma=False,
    )
```

```python
import functools

import jax
import jax.numpy as jnp
import numpy as np
from jax import lax
from jax.experimental import pallas as pl
from jax.experimental.pallas import tpu as pltpu
from jax.sharding import PartitionSpec as P

D = 1024
HEADS = 16
HEAD_DIM = 64
FF = 4096
BLK = 1024
LAYERS = 2
NBLK = 12
CORES = 2
DEPTH_Z = 4

EPS_NORM = 1e-05
EPS_ADAM = 1e-08
LR_BLOCK = 0.1
LR_VEC = 0.25
DECAY_RATE = 0.5
VMEM_BYTES = 56 * 1024 * 1024
BF16 = jnp.bfloat16
F32 = jnp.float32


class Place:
    def __init__(self, ctx_count, wsh_count):
        self.size = {
            "core": CORES,
            "y": ctx_count // CORES,
            "z": DEPTH_Z,
            "x": wsh_count // DEPTH_Z,
        }
        ctx_at = lax.axis_index("ctx")
        wsh_at = lax.axis_index("wsh")
        self.at = {
            "core": ctx_at % CORES,
            "y": ctx_at // CORES,
            "z": wsh_at // self.size["x"],
            "x": wsh_at % self.size["x"],
        }

    def take(self, value, axis, step):
        name, slow, fast = {
            "core": ("ctx", "y", "core"),
            "y": ("ctx", "y", "core"),
            "z": ("wsh", "z", "x"),
            "x": ("wsh", "z", "x"),
        }[axis]
        extent = self.size[axis]
        pairs = []
        for slow_at in range(self.size[slow]):
            for fast_at in range(self.size[fast]):
                if axis == fast:
                    other = (slow_at, (fast_at + step) % extent)
                else:
                    other = ((slow_at + step) % extent, fast_at)
                pairs.append(
                    (
                        other[0] * self.size[fast] + other[1],
                        slow_at * self.size[fast] + fast_at,
                    )
                )
        return lax.ppermute(value, name, pairs)

    def gather(self, value, axis):
        steps = range(1, self.size[axis])
        return jnp.stack([value] + [self.take(value, axis, step) for step in steps])

    def collect(self, values, axis):
        steps = range(1, self.size[axis])
        return [values[0]] + [self.take(values[step], axis, -step) for step in steps]

    def swap_z(self, values):
        count_x = self.size["x"]
        lines = [[z * count_x + x for z in range(self.size["z"])] for x in range(count_x)]
        return lax.all_to_all(values, "wsh", 0, 0, tiled=True, axis_index_groups=lines)

    def scatter(self, values, axis):
        total = values[0].astype(F32)
        for step in range(1, self.size[axis]):
            total = total + self.take(values[step], axis, -step).astype(F32)
        return total


def vector_parts(vector):
    pieces = [vector[spot * D : (spot + 1) * D] for spot in range(8)]
    return pieces + [vector[8 * D :]]


def dot(left, right):
    return jnp.dot(left, right, preferred_element_type=F32)


def dot_t(left, right):
    return lax.dot_general(left, right, (((1,), (1,)), ((), ())), preferred_element_type=F32)


def after(value, *others):
    return lax.optimization_barrier((value,) + others)[0]


def together(*values):
    return lax.optimization_barrier(values)


def add_up(values):
    return sum(value.astype(F32) for value in values)


class Gathering:
    def __init__(self, place, shard, split_count):
        self.place = place
        self.count, self.rows, _ = shard.shape
        half_rows, half_cols = self.rows // 2, BLK // 2
        has_y = place.size["y"] == 2
        self.split_count = split_count if has_y else 0
        whole_count = self.count - self.split_count
        mine = lax.dynamic_slice_in_dim(shard, place.at["core"] * half_rows, half_rows, 1)
        whole = mine[self.split_count :]
        pieces = [
            part
            for block in range(whole_count)
            for part in (whole[block, :, :half_cols], whole[block, :, half_cols:])
        ]
        parts = []
        if pieces:
            parts.append(jnp.stack(pieces))
        if has_y:
            parts.insert(
                0,
                lax.dynamic_slice_in_dim(
                    mine[: self.split_count], place.at["y"] * half_cols, half_cols, 2
                ),
            )
        self.held = [jnp.concatenate(parts)]
        self.crossed = []

    def step_z(self):
        piece = self.held[0]
        copies = jnp.broadcast_to(piece[None], (self.place.size["z"],) + piece.shape)
        self.held = [self.place.swap_z(copies)]

    def step_x(self):
        self.held = gather_list(self.place, self.held[0], "x")

    def step_y(self):
        self.held = [jnp.stack(self.held)]
        if self.split_count:
            value = self.held[0][:, :, : self.split_count]
            self.held.append(self.place.take(value, "y", 1))
        self.crossed = [self.place.take(self.held[0], "core", 1)]

    def step_core(self):
        if self.split_count:
            self.crossed.append(self.place.take(self.held[1], "core", 1))

    def pieces(self):
        split, mine, crossed = self.split_count, self.held, self.crossed
        part = (mine[0].shape[:2]) + (1,) + mine[0].shape[3:]

        def spec(place_of):
            return pl.BlockSpec(part, lambda i, where: (0, 0, place_of(i), 0, 0))

        last = mine[0].shape[2] - 1
        low = spec(lambda i: jnp.where(i < split, i, 2 * i - split))
        high = spec(lambda i: jnp.minimum(jnp.where(i < split, split + 1, 2 * i - split + 1), last))
        operands = [mine[0], crossed[0], mine[0], crossed[0]]
        specs = [low, low, high, high]
        if split:
            operands += [mine[1], crossed[1]]
            specs += [spec(lambda i: jnp.minimum(i, split - 1))] * 2
        return operands, specs

    def where(self):
        return jnp.stack([self.place.at[name] for name in ("x", "y", "core")]).astype(jnp.int32)


def open_block(split, where, pieces, out):
    spot = pl.program_id(0)
    extent_x, extent_z, _, half_rows, half_cols = pieces[0].shape
    x_at, y_at, core_at = where[0], where[1], where[2]

    def put(first_col, sources):
        low_col = pl.ds(first_col * half_cols, half_cols)
        high_col = pl.ds((1 - first_col) * half_cols, half_cols)
        for step_x in range(extent_x):
            for z in range(extent_z):
                base = (z * extent_x + lax.rem(x_at + step_x, extent_x)) * 2
                mine = pl.ds(pl.multiple_of((base + core_at) * half_rows, half_rows), half_rows)
                other = pl.ds(pl.multiple_of((base + 1 - core_at) * half_rows, half_rows), half_rows)
                out[0, mine, low_col] = sources[0][step_x, z, 0]
                out[0, other, low_col] = sources[1][step_x, z, 0]
                out[0, mine, high_col] = sources[2][step_x, z, 0]
                out[0, other, high_col] = sources[3][step_x, z, 0]

    if split:
        sources = list(pieces[:2]) + list(pieces[4:])
        for y in range(2):
            pl.when((spot < split) & (y_at == y))(functools.partial(put, y, sources))
        pl.when(spot >= split)(lambda: put(0, pieces[:4]))
    else:
        put(0, pieces[:4])


def call(body, grid, in_specs, out_specs, out_shape, scratch=(), prefetch=0, cost=1.0, name=None):
    return pl.pallas_call(
        body,
        grid_spec=pltpu.PrefetchScalarGridSpec(
            num_scalar_prefetch=prefetch,
            grid=grid,
            in_specs=in_specs,
            out_specs=out_specs,
            scratch_shapes=list(scratch),
        ),
        out_shape=out_shape,
        compiler_params=pltpu.CompilerParams(vmem_limit_bytes=VMEM_BYTES),
        cost_estimate=pl.CostEstimate(flops=int(cost * 2e7), bytes_accessed=0, transcendentals=0),
        name=name,
    )


def shaped(shape, dtype):
    return jax.ShapeDtypeStruct(shape, dtype)


def fixed(shape):
    return pl.BlockSpec(shape, lambda *at: (0,) * len(shape))


def norm_stats(summed):
    average = jnp.mean(summed, axis=-1, keepdims=True)
    centred = summed - average
    variance = jnp.mean(centred * centred, axis=-1, keepdims=True)
    scale = lax.rsqrt(variance + EPS_NORM)
    return centred * scale, scale


def norm_back(grad, normed, scale, gain):
    flow = grad * gain
    return (
        flow
        - jnp.mean(flow, axis=-1, keepdims=True)
        - normed * jnp.mean(flow * normed, axis=-1, keepdims=True)
    ) * scale


BLOCK = pl.BlockSpec((1, BLK, BLK), lambda i, *at: (i, 0, 0))
BLOCKS = jax.ShapeDtypeStruct((4, BLK, BLK), BF16)


def project_kernel(split, where, x_low, bias, *refs):
    pieces, (query, keyval, weight) = refs[:-3], refs[-3:]
    open_block(split, where, pieces, weight)

    def value():
        return (dot(x_low[...], weight[0]) + bias[0]).astype(BF16)

    @pl.when(pl.program_id(0) == 0)
    def _():
        query[...] = value() * HEAD_DIM ** (-0.5)

    @pl.when((pl.program_id(0) > 0) & (pl.program_id(0) < 3))
    def _():
        keyval[...] = value()


def project(x_low, chunk, bias):
    tokens = x_low.shape[0]
    pieces, specs = chunk.pieces()
    return call(
        functools.partial(project_kernel, chunk.split_count),
        (4,),
        [fixed((tokens, D)), pl.BlockSpec((1, 1, D), lambda i, where: (jnp.minimum(i, 2), 0, 0))] + specs,
        [
            fixed((tokens, D)),
            pl.BlockSpec((tokens, D), lambda i, where: (0, jnp.clip(i - 1, 0, 1))),
            BLOCK,
        ],
        [shaped((tokens, D), BF16), shaped((tokens, 2 * D), BF16), BLOCKS],
        prefetch=1,
        cost=8.0,
        name="project",
    )(chunk.where(), x_low, bias, *pieces)


def head_weights(query_h, keys_h, masks):
    scores = [
        dot_t(key, query_h) + mask for key, mask in zip(keys_h, masks)
    ]
    peak = functools.reduce(
        jnp.maximum, [jnp.max(score, axis=0, keepdims=True) for score in scores]
    )
    scores = [jnp.exp(score - peak) for score in scores]
    total = sum(jnp.sum(score, axis=0, keepdims=True) for score in scores)
    return scores, 1.0 / total


def dot_tt(left, right):
    return lax.dot_general(left, right, (((0,), (0,)), ((), ())), preferred_element_type=F32)


def head_of(ref, head):
    return ref[:, pl.ds(head * HEAD_DIM, HEAD_DIM)]


def attend_kernel(count, tokens, query, mask, *refs):
    keys, values, out = refs[:count], refs[count : 2 * count], refs[-1]
    masks = [mask[pl.ds(spot * tokens, tokens), :] for spot in range(count)]
    mixed = []
    for head in range(2):
        weights, inverse = head_weights(head_of(query, head), [head_of(key, head) for key in keys], masks)
        total = sum(
            dot_tt(head_of(value, head), weight.astype(BF16)) for value, weight in zip(values, weights)
        )
        mixed.append(total * inverse)
    out[...] = jnp.concatenate(mixed, axis=0).T.astype(BF16)


def pair_specs(tokens, count):
    pair = 2 * HEAD_DIM
    half = D // pair
    return (
        [pl.BlockSpec((tokens, pair), lambda i: (0, i))] * count
        + [pl.BlockSpec((tokens, pair), lambda i: (0, half + i))] * count
    )


def attend(query, keyvals, mask):
    tokens = query.shape[0]
    count = len(keyvals)
    pair = 2 * HEAD_DIM
    return call(
        functools.partial(attend_kernel, count, tokens),
        (D // pair,),
        [pl.BlockSpec((tokens, pair), lambda i: (0, i)), fixed(mask.shape)]
        + pair_specs(tokens, count),
        pl.BlockSpec((tokens, pair), lambda i: (0, i)),
        shaped((tokens, D), BF16),
        cost=14.0,
        name="attend",
    )(query, mask, *keyvals, *keyvals)


def attend_back_kernel(count, count_y, tokens, query, grad, mask, *refs):
    keys, values = refs[:count], refs[count : 2 * count]
    grad_q, mine, other = refs[2 * count :]
    masks = [mask[pl.ds(spot * tokens, tokens), :] for spot in range(count)]
    scale = HEAD_DIM ** (-0.5)
    grads_q = []
    grads_k = [[] for _ in range(count)]
    grads_v = [[] for _ in range(count)]
    for head in range(2):
        query_h = head_of(query, head)
        grad_h = head_of(grad, head)
        keys_h = [head_of(key, head) for key in keys]
        weights, inverse = head_weights(query_h, keys_h, masks)
        probs = [weight * inverse for weight in weights]
        grad_probs = [dot_t(head_of(value, head), grad_h) for value in values]
        inner = sum(
            jnp.sum(prob * grad_prob, axis=0, keepdims=True)
            for prob, grad_prob in zip(probs, grad_probs)
        )
        flow_q = 0.0
        for spot in range(count):
            grad_score = (probs[spot] * (grad_probs[spot] - inner)).astype(BF16)
            flow_q = flow_q + dot_tt(keys_h[spot], grad_score)
            grads_k[spot].append(dot(grad_score, query_h))
            grads_v[spot].append(dot(probs[spot].astype(BF16), grad_h))
        grads_q.append(flow_q * scale)
    grad_q[...] = jnp.concatenate(grads_q, axis=0).T.astype(BF16)
    for spot in range(count):
        out = mine if spot < count_y else other
        out[spot % count_y, 0] = jnp.concatenate(grads_k[spot], axis=1).astype(BF16)
        out[spot % count_y, 1] = jnp.concatenate(grads_v[spot], axis=1).astype(BF16)


def attend_back(query, keyvals, grad, mask):
    tokens = query.shape[0]
    count = len(keyvals)
    count_y = count // CORES
    pair = 2 * HEAD_DIM
    part = pl.BlockSpec((count_y, 2, tokens, pair), lambda i: (0, 0, 0, i))
    return call(
        functools.partial(attend_back_kernel, count, count_y, tokens),
        (D // pair,),
        [pl.BlockSpec((tokens, pair), lambda i: (0, i))] * 2
        + [fixed(mask.shape)]
        + pair_specs(tokens, count),
        [pl.BlockSpec((tokens, pair), lambda i: (0, i)), part, part],
        [shaped((tokens, D), BF16)] + [shaped((count_y, 2, tokens, D), BF16)] * 2,
        cost=21.0,
        name="attend_back",
    )(query, grad, mask, *keyvals, *keyvals)


def mix_kernel(attn, weight, carried, vecs, summed, middle, middle_low):
    value = carried[...].astype(F32) + (dot(attn[...], weight[0]) + vecs[0:1, :])
    summed[...] = value
    normed, _ = norm_stats(value)
    value = normed * vecs[1:2, :] + vecs[2:3, :]
    middle[...] = value
    middle_low[...] = value.astype(BF16)


def mix(attn, w_in, carried, vecs):
    tokens = attn.shape[0]
    full = fixed((tokens, D))
    return call(
        mix_kernel,
        (1,),
        [full, pl.BlockSpec((1, BLK, BLK), lambda i: (3, 0, 0)), full, fixed(vecs.shape)],
        [full, full, full],
        [shaped((tokens, D), F32), shaped((tokens, D), F32), shaped((tokens, D), BF16)],
        cost=4.0,
        name="mix",
    )(attn, w_in, carried, vecs)


def erf_part(hidden):
    return (1.0 + lax.erf(hidden * (0.5**0.5))) * 0.5


def up_kernel(split, where, middle_low, bias, *refs):
    pieces, (hidden, act, weight) = refs[:-3], refs[-3:]
    open_block(split, where, pieces, weight)
    value = dot(middle_low[...], weight[0]) + bias[0]
    hidden[...] = value
    act[...] = (value * erf_part(value)).astype(BF16)


def up(middle_low, chunk, bias):
    tokens = middle_low.shape[0]
    pieces, specs = chunk.pieces()
    part = pl.BlockSpec((tokens, BLK), lambda i, where: (0, i))
    return call(
        functools.partial(up_kernel, chunk.split_count),
        (FF // BLK,),
        [fixed((tokens, D)), pl.BlockSpec((1, 1, BLK), lambda i, where: (i, 0, 0))] + specs,
        [part, part, BLOCK],
        [shaped((tokens, FF), F32), shaped((tokens, FF), BF16), BLOCKS],
        prefetch=1,
        cost=8.0,
        name="up",
    )(chunk.where(), middle_low, bias, *pieces)


def down_kernel(split, where, act, middle, vecs, *refs):
    pieces, (summed, result, result_low, weight, total) = refs[:-5], refs[-5:]
    open_block(split, where, pieces, weight)
    spot = pl.program_id(0)
    value = dot(act[...], weight[0])

    @pl.when(spot == 0)
    def _():
        total[...] = value

    @pl.when(spot > 0)
    def _():
        total[...] += value

    @pl.when(spot == pl.num_programs(0) - 1)
    def _():
        value = middle[...] + (total[...] + vecs[0:1, :])
        summed[...] = value
        normed, _ = norm_stats(value)
        value = normed * vecs[1:2, :] + vecs[2:3, :]
        result[...] = value
        result_low[...] = value.astype(BF16)


def down(act, chunk, middle, vecs):
    tokens = act.shape[0]
    full = fixed((tokens, D))
    pieces, specs = chunk.pieces()
    return call(
        functools.partial(down_kernel, chunk.split_count),
        (FF // BLK,),
        [pl.BlockSpec((tokens, BLK), lambda i, where: (0, i)), full, fixed(vecs.shape)] + specs,
        [full, full, full, BLOCK],
        [shaped((tokens, D), F32), shaped((tokens, D), F32), shaped((tokens, D), BF16), BLOCKS],
        scratch=[pltpu.VMEM((tokens, D), F32)],
        prefetch=1,
        cost=8.0,
        name="down",
    )(chunk.where(), act, middle, vecs, *pieces)


def column_sum(value):
    return jnp.sum(value, axis=0, keepdims=True)


def close_kernel(flow, summed, gain, back_out, low_out, sums):
    grad = flow[...].astype(F32)
    normed, scale = norm_stats(summed[...])
    back = norm_back(grad, normed, scale, gain[...])
    back_out[...] = back
    low = back.astype(BF16)
    low_out[...] = low
    sums[0:1, :] = column_sum(low.astype(F32))
    sums[1:2, :] = column_sum(grad * normed)
    sums[2:3, :] = column_sum(grad)
    sums[3:8, :] = jnp.zeros((5, D), F32)


def close(flow, summed, gain):
    tokens = flow.shape[0]
    full = fixed((tokens, D))
    return call(
        close_kernel,
        (1,),
        [full, full, fixed((1, D))],
        [full, full, fixed((8, D))],
        [shaped((tokens, D), F32), shaped((tokens, D), BF16), shaped((8, D), F32)],
        cost=3.0,
        name="close",
    )(flow, summed, gain)


def feed_back_kernel(
    grad_two, ffn_low, summed_one, hidden, w_down, w_up, w_out, gain,
    hid_low, branch_low, attn_grad, grad_one, sums, bias_sums, total,
):
    spot = pl.program_id(0)

    @pl.when(spot == 0)
    def _():
        total[...] = grad_two[...]

    value = hidden[...]
    slope = erf_part(value) + value * jnp.exp(-0.5 * value * value) * ((2.0 * np.pi) ** -0.5)
    low = (dot_t(ffn_low[...], w_down[0]) * slope).astype(BF16)
    hid_low[...] = low
    bias_sums[0] = column_sum(low.astype(F32))
    total[...] += dot_t(low, w_up[0])

    @pl.when(spot == pl.num_programs(0) - 1)
    def _():
        grad = total[...]
        normed, scale = norm_stats(summed_one[...])
        back = norm_back(grad, normed, scale, gain[...])
        grad_one[...] = back
        low = back.astype(BF16)
        branch_low[...] = low
        sums[0:1, :] = column_sum(low.astype(F32))
        sums[1:2, :] = column_sum(grad * normed)
        sums[2:3, :] = column_sum(grad)
        sums[3:8, :] = jnp.zeros((5, D), F32)
        attn_grad[...] = dot_t(low, w_out[0]).astype(BF16)


def feed_back(grad_two, ffn_low, summed_one, hidden, w_down, w_up, w_in, gain):
    tokens = ffn_low.shape[0]
    full = fixed((tokens, D))
    part = pl.BlockSpec((tokens, BLK), lambda i: (0, i))
    weight = pl.BlockSpec((1, BLK, BLK), lambda i: (i, 0, 0))
    return call(
        feed_back_kernel,
        (FF // BLK,),
        [full, full, full, part, weight, weight, pl.BlockSpec((1, BLK, BLK), lambda i: (3, 0, 0)), fixed((1, D))],
        [part, full, full, full, fixed((8, D)), pl.BlockSpec((1, 1, BLK), lambda i: (i, 0, 0))],
        [
            shaped((tokens, FF), BF16),
            shaped((tokens, D), BF16),
            shaped((tokens, D), BF16),
            shaped((tokens, D), F32),
            shaped((8, D), F32),
            shaped((FF // BLK, 1, BLK), F32),
        ],
        scratch=[pltpu.VMEM((tokens, D), F32)],
        cost=15.0,
        name="feed_back",
    )(grad_two, ffn_low, summed_one, hidden, w_down, w_up, w_in, gain)


def input_back_kernel(count, grad_q, grad_one, weight, *refs):
    parts, (joined, result, sums, total) = refs[:count], refs[count:]
    spot = pl.program_id(0)

    @pl.when(spot == 0)
    def _():
        joined[...] = grad_q[...]
        total[...] = grad_one[...]

    @pl.when(spot > 0)
    def _():
        joined[...] = sum(part[0, 0].astype(F32) for part in parts).astype(BF16)

    low = joined[...]
    sums[0] = column_sum(low.astype(F32))
    total[...] += dot_t(low, weight[0])

    @pl.when(spot == pl.num_programs(0) - 1)
    def _():
        result[...] = total[...]


def input_back(grad_q, parts, grad_one, w_in):
    tokens = grad_q.shape[0]
    full = fixed((tokens, D))
    return call(
        functools.partial(input_back_kernel, len(parts)),
        (3,),
        [full, full, pl.BlockSpec((1, BLK, BLK), lambda i: (i, 0, 0))]
        + [pl.BlockSpec((1, 1, tokens, D), lambda i: (0, jnp.maximum(i - 1, 0), 0, 0))] * len(parts),
        [pl.BlockSpec((tokens, D), lambda i: (0, i)), full, pl.BlockSpec((1, 1, D), lambda i: (i, 0, 0))],
        [shaped((tokens, 3 * D), BF16), shaped((tokens, D), F32), shaped((3, 1, D), F32)],
        scratch=[pltpu.VMEM((tokens, D), F32)],
        cost=8.0,
        name="input_back",
    )(grad_q, grad_one, w_in, *parts)


def gather_list(place, value, axis):
    return [value] + [place.take(value, axis, step) for step in range(1, place.size[axis])]


def vector_sets(vector):
    parts = vector_parts(vector)
    return {
        "project": jnp.stack([parts[0], jnp.zeros((D,), F32), parts[1]])[:, None],
        "mix": jnp.stack([parts[2], parts[4], parts[5]]),
        "up": parts[8].reshape(FF // BLK, 1, BLK),
        "down": jnp.stack([parts[3], parts[6], parts[7]]),
        "gain_one": parts[4][None],
        "gain_two": parts[6][None],
    }


def project_step(place, carried_low, chunk, vectors):
    query, keyval, w_in = project(carried_low, chunk, vectors["project"])
    keyvals = [keyval, *gather_list(place, keyval, "y")[1:], place.take(keyval, "core", 1)]
    return query, keyvals, w_in


def mix_step(query, keyvals, carried, w_in, vectors, mask):
    attn_low = attend(query, keyvals, mask)
    return attn_low, *mix(attn_low, w_in, carried, vectors["mix"])


def up_step(mid_low, chunk, vectors):
    return up(mid_low, chunk, vectors["up"])


def down_step(act_low, chunk, middle, vectors):
    return down(act_low, chunk, middle, vectors["down"])


def sum_kernel(count_one, first_half, sizes, turned, where, *refs):
    sets = (refs[:4], refs[4:8]) if count_one is not None else (refs[:4],)
    outs, shared, product = refs[4 * len(sets) : -2], refs[-2], refs[-1]
    x_at, y_at = where[1], where[2]
    extent_z, extent_x, extent_y, rows = sizes
    cols = BLK // (CORES * extent_y)
    spot = pl.program_id(0)

    def both(mine, other):
        return jnp.concatenate([mine[...], other[...]], axis=0)

    def share(left_mine, left_other, right_mine, right_other):
        shared[...] = (both(right_mine, right_other) if turned else both(left_mine, left_other)).T

    def multiply(left_mine, left_other, right_mine, right_other):
        value = both(left_mine, left_other) if turned else both(right_mine, right_other)
        product[...] = dot(shared[...], value).astype(BF16)

    pl.when(spot == 0)(lambda: share(*sets[0]))
    if len(sets) == 1:
        multiply(*sets[0])
    else:
        pl.when(spot == count_one)(lambda: share(*sets[1]))
        pl.when(spot < count_one)(lambda: multiply(*sets[0]))
        pl.when(spot >= count_one)(lambda: multiply(*sets[1]))

    def put(y_first, x, y):
        for step_y in range(extent_y):
            from_col = (y + step_y) % extent_y * cols
            for step_x in range(extent_x):
                for z in range(extent_z):
                    from_row = (z * extent_x + (x + step_x) % extent_x) * rows
                    if turned:
                        value = product[pl.ds(from_col, cols), pl.ds(from_row, rows)]
                    else:
                        value = product[pl.ds(from_row, rows), pl.ds(from_col, cols)]
                    if y_first:
                        outs[step_y][step_x, z, 0] = value
                    else:
                        outs[extent_y + step_x][step_y, z, 0] = value

    for x in range(extent_x):
        for y in range(extent_y):
            here = (x_at == x) & (y_at == y)
            pl.when(here & (spot < first_half))(functools.partial(put, True, x, y))
            pl.when(here & (spot >= first_half))(functools.partial(put, False, x, y))


def partial_sums(place, sets):
    tokens = sets[0][0].shape[0]
    extent_z, extent_x, extent_y = (place.size[name] for name in ("z", "x", "y"))
    rows = BLK // (extent_z * extent_x)
    half = BLK // CORES
    cols = half // extent_y
    where = jnp.stack([place.at[name] for name in ("z", "x", "y", "core")]).astype(jnp.int32)
    counts = [max(one[0].shape[1], one[2].shape[1]) // BLK for one in sets]
    count = sum(counts)
    first_half = count // 2
    specs = []
    start = 0
    for one, amount in zip(sets, counts):

        def at(i, start=start, amount=amount):
            return jnp.clip(i - start, 0, amount - 1)

        many_left, many_right = one[0].shape[1] > BLK, one[2].shape[1] > BLK
        for first in (0, one[4]):
            specs.append(
                pl.BlockSpec(
                    (tokens, BLK),
                    lambda i, where, at=at, many=many_left, first=first: (0, first + (at(i) if many else 0)),
                )
            )
        specs += [
            pl.BlockSpec(
                (tokens, half),
                lambda i, where, at=at, many=many_right: (0, (at(i) * CORES if many else 0) + where[3]),
            )
        ] * 2
        start += amount
    turned = sets[0][0].shape[1] > BLK
    tile = (cols, rows) if turned else (rows, cols)
    part_y = (extent_x, extent_z, 1) + tile
    part_x = (extent_y, extent_z, 1) + tile
    spec_y = pl.BlockSpec(part_y, lambda i, where: (0, 0, jnp.minimum(i, first_half - 1), 0, 0))
    spec_x = pl.BlockSpec(part_x, lambda i, where: (0, 0, jnp.maximum(i - first_half, 0), 0, 0))
    outs = call(
        functools.partial(
            sum_kernel,
            counts[0] if len(sets) > 1 else None,
            first_half,
            (extent_z, extent_x, extent_y, rows),
            turned,
        ),
        (count,),
        specs,
        [spec_y] * extent_y + [spec_x] * extent_x,
        [shaped((extent_x, extent_z, first_half) + tile, BF16)] * extent_y
        + [shaped((extent_y, extent_z, count - first_half) + tile, BF16)] * extent_x,
        scratch=[
            pltpu.VMEM((half if turned else BLK, 2 * tokens), BF16),
            pltpu.VMEM((half, BLK) if turned else (BLK, half), BF16),
        ],
        prefetch=1,
        cost=8.0,
        name="partial_sums",
    )(where, *[value for one in sets for value in one[:4]])
    return outs[:extent_y], outs[extent_y:]


class Summing:
    def __init__(self, place, ids, sets):
        self.place = place
        self.ids = ids
        self.turned = False
        if (BLK // (CORES * place.size["y"])) % 128:
            self.plain = True
            self.parts = self.by_y = self.by_x = ()
            self.groups = [sum_job_plain(place, one[0], one[2], "y")[None] for one in sets]
        else:
            self.plain = False
            sets = [(one[0], one[1], one[2], place.take(one[2], "core", 1), one[3]) for one in sets]
            self.turned = sets[0][0].shape[1] > BLK
            self.parts = partial_sums(place, sets)
            self.by_y = self.by_x = ()
            self.groups = ()

    def first_y(self):
        if not self.plain:
            self.by_y = self.place.collect(self.parts[0], "y")

    def first_x(self):
        if not self.plain:
            self.by_x = self.place.collect(self.parts[1], "x")

    def second_x(self):
        if not self.plain:
            total = add_up(self.by_y)
            parts = [total[step].astype(BF16) for step in range(self.place.size["x"])]
            self.by_y = self.place.collect(parts, "x")

    def second_y(self):
        if not self.plain:
            total = add_up(self.by_x)
            parts = [total[step].astype(BF16) for step in range(self.place.size["y"])]
            self.by_x = self.place.collect(parts, "y")

    def third(self):
        if not self.plain:
            both = jnp.concatenate([add_up(self.by_y), add_up(self.by_x)], axis=1)
            self.groups = [self.place.swap_z(both.astype(BF16))]


def route_kernel(turned, slots, scaling, spots, *refs):
    parts, (out, total) = refs[: len(turned)], refs[len(turned) :]
    at = 0
    for part, turn in zip(parts, turned):
        for block in range(part.shape[1]):
            value = sum(part[addend, block].astype(F32) for addend in range(part.shape[0]))
            value = value * scaling
            total[at] = (value.T if turn else value).astype(BF16)
            at += 1
    total[at] = jnp.zeros(total.shape[1:], BF16)
    for ctx in range(out.shape[0]):
        for spot in range(out.shape[1]):
            if spot < slots:
                out[ctx, spot] = total[spots[ctx * slots + spot]]
            else:
                out[ctx, spot] = total[at]


def route(groups, turned, spots, slots, wsh_count, rows, scaling):
    cols = groups[0].shape[2] * groups[0].shape[3] // rows
    blocks = sum(group.shape[1] for group in groups)
    shape = (spots.shape[0] // slots, wsh_count, rows, cols)
    return call(
        functools.partial(route_kernel, turned, slots, scaling),
        (1,),
        [fixed(group.shape) for group in groups],
        fixed(shape),
        shaped(shape, BF16),
        scratch=[pltpu.VMEM((blocks + 1, rows, cols), BF16)],
        prefetch=1,
        cost=6.0,
        name="route",
    )(spots, *groups)


def rotate_kernel(quarters, grads, right, left, first, second, rotated, update, total, low):
    step = BLK // 4
    for at in range(4):
        rows = pl.ds(at * step, step)
        product = 0.0
        for source, quarter in enumerate(quarters):
            width = grads.shape[2]
            product = product + dot(
                grads[source, rows, :], right[pl.ds(quarter * width, width), :]
            )
        value = dot_tt(left[rows, :], product.astype(BF16))
        if at:
            total[...] += value
        else:
            total[...] = value
    for at in range(4):
        rows = pl.ds(at * step, step)
        turned = total[rows, :]
        rotated[rows, :] = turned.astype(BF16)
        first_new = DECAY_RATE * first[rows, :].astype(F32) + (1.0 - DECAY_RATE) * turned
        second_new = DECAY_RATE * second[rows, :].astype(F32) + (1.0 - DECAY_RATE) * turned * turned
        direction = first_new / (jnp.sqrt(second_new) + EPS_ADAM)
        low[rows, :] = dot_t(direction.astype(BF16), right[...]).astype(BF16)
    for at in range(4):
        rows = pl.ds(at * step, step)
        update[rows, :] = dot(left[rows, :], low[...]).astype(BF16)


def rotate(grads, quarters, right, left, first, second):
    full = fixed((BLK, BLK))
    return call(
        functools.partial(rotate_kernel, quarters),
        (1,),
        [fixed(grads.shape), full, full, full, full],
        [full, full],
        [shaped((BLK, BLK), BF16)] * 2,
        scratch=[pltpu.VMEM((BLK, BLK), F32), pltpu.VMEM((BLK, BLK), BF16)],
        cost=16.0,
        name="rotate",
    )(grads, right, left, first, second)


def pick_kernel(count, amount, table, *refs):
    parts, out = refs[:count], refs[count]
    first = pl.program_id(0) * amount

    def put(spot, part):
        out[spot] = parts[part][table[1, first + spot]]

    for spot in range(amount):
        for part in range(count):
            pl.when(table[0, first + spot] == part)(functools.partial(put, spot, part))


def pick(parts, table):
    blocks = table.shape[1]
    amount = 4
    shape = (blocks,) + parts[0].shape[1:]
    return call(
        functools.partial(pick_kernel, len(parts), amount),
        (blocks // amount,),
        [fixed(value.shape) for value in parts],
        pl.BlockSpec((amount,) + shape[1:], lambda i, table: (i, 0, 0)),
        shaped(shape, BF16),
        prefetch=1,
        cost=12.0,
        name="pick",
    )(table, *parts)


def left_order(place, left):
    tokens, cols = left.shape
    count_z, count_x = place.size["z"], place.size["x"]
    blocks = cols // BLK
    rows = BLK // (count_z * count_x)
    value = left.reshape(tokens, blocks, count_z, count_x, rows)
    value = jnp.roll(value, (-place.at["z"], -place.at["x"]), axis=(2, 3))
    return value.transpose(0, 3, 2, 1, 4).reshape(tokens, cols)


def right_halves(place, right):
    tokens, cols = right.shape
    count_y = place.size["y"]
    width = BLK // (CORES * count_y)
    value = right.reshape(tokens, cols // BLK, CORES, count_y, width)
    halves = []
    for step in range(CORES):
        half = lax.dynamic_index_in_dim(value, (place.at["core"] + step) % CORES, 2, False)
        half = jnp.roll(half, -place.at["y"], axis=2)
        halves.append(half.transpose(2, 0, 1, 3).reshape(count_y, tokens, -1))
    return halves


def sum_job_plain(place, left, right, first):
    count_z, count_x, count_y = place.size["z"], place.size["x"], place.size["y"]
    left = left_order(place, left)
    right_mine, right_other = right_halves(place, right)
    left_both = jnp.concatenate([left, place.take(left, "core", 1)], axis=0)
    right_both = jnp.concatenate([right_mine, place.take(right_other, "core", 1)], axis=1)
    partial = [
        lax.dot_general(left_both, right_both[step], (((0,), (0,)), ((), ())), preferred_element_type=F32)
        .astype(BF16)
        .reshape(count_x, count_z, -1, right_both.shape[2])
        for step in range(count_y)
    ]
    if first == "y":
        total = place.scatter(partial, "y").astype(BF16)
        total = place.scatter(total, "x").astype(BF16)
    else:
        parts = [[value[step] for value in partial] for step in range(count_x)]
        parts = [jnp.stack(part) for part in parts]
        total = place.scatter(parts, "x").astype(BF16)
        total = place.scatter(total, "y").astype(BF16)
    total = place.scatter(total, "z")
    rows = BLK // (count_z * count_x)
    width = BLK // (CORES * count_y)
    if left.shape[1] > BLK:
        return total.reshape(-1, rows, width)
    return total.reshape(rows, -1, width).transpose(1, 0, 2)


class EverySum:
    def __init__(self, place, value):
        self.place = place
        self.terms = [value]
        self.plain = place.size["y"] != 2 or place.size["x"] != 2

    def step(self, axis, bit=0):
        if self.plain:
            return
        value = sum(self.terms)
        if axis == "z":
            pairs = self.place.size["x"]
            swap = [
                (z * pairs + x, (z ^ bit) * pairs + x) for z in range(DEPTH_Z) for x in range(pairs)
            ]
            self.terms = [value, lax.ppermute(value, "wsh", swap)]
        else:
            self.terms = [value, self.place.take(value, axis, 1)]

    def total(self):
        if self.plain:
            return lax.psum(self.terms[0], ("ctx", "wsh"))
        return sum(self.terms)


def doc_ids(lengths, position):
    starts = jnp.cumsum(lengths) - lengths
    return jnp.sum((position[:, None] >= starts[None, :]).astype(jnp.int32), axis=1)


def fill_up(rows_value, wsh_count):
    slots = rows_value.shape[0]
    return jnp.pad(rows_value.astype(BF16), ((0, wsh_count - slots), (0, 0), (0, 0)))


def to_owner(padded):
    return lax.all_to_all(padded, "wsh", 0, 0, tiled=True).reshape(BLK, BLK)


def from_owner(whole, wsh_count):
    cut = whole.astype(BF16).reshape(wsh_count, BLK // wsh_count, BLK)
    return lax.all_to_all(cut, "wsh", 0, 0, tiled=True)


def on_device(
    stream_in,
    doc_lengths,
    cotangent,
    weights,
    vec_params,
    owner_slots,
    master,
    left_bases,
    right_bases,
    moment1,
    moment2,
    vec_moment1,
    vec_moment2,
):
    tokens = stream_in.shape[1]
    ctx_count = lax.axis_size("ctx")
    wsh_count = lax.axis_size("wsh")
    place = Place(ctx_count, wsh_count)
    seq_len = tokens * ctx_count
    scaling = (wsh_count * seq_len) ** (-0.5)
    slots_dev, rows_dev = master.shape[0], master.shape[1]
    slot_total = ctx_count * slots_dev
    count_y = place.size["y"]
    width = BLK // ctx_count

    core_of = (place.at["core"] + jnp.arange(CORES)) % CORES
    y_of = (place.at["y"] + jnp.arange(count_y)) % count_y
    ctx_of = (y_of[None, :] * CORES + core_of[:, None]).reshape(-1)
    key_pos = (ctx_of[:, None] * tokens + jnp.arange(tokens)[None, :]).reshape(-1)
    doc_keys = doc_ids(doc_lengths[0], key_pos)
    mask = jnp.where(doc_keys[:, None] == doc_keys[None, :tokens], 0.0, -1e30).astype(F32)

    chunks = [
        Gathering(place, weights[layer_at, first : first + 4], split_count)
        for layer_at, first, split_count in (
            (0, 0, 3),
            (0, 4, 2),
            (0, 8, 2),
            (1, 0, 2),
            (1, 4, 2),
            (1, 8, 4),
        )
    ]

    live = {}

    def settle():
        going = [chunk for chunk in chunks if chunk]
        state = [(chunk.held, chunk.crossed) for chunk in going]
        state, values = together(state, {name: live[name] for name in live})
        for chunk, (held, crossed) in zip(going, state):
            chunk.held, chunk.crossed = held, crossed
        live.update(values)

    def finish(spot):
        chunk = chunks[spot]
        chunk.step_core()
        chunks[spot] = None
        return chunk

    def keyvals_of(layer_at):
        keyvals = live[f"keyvals{layer_at}"]
        return keyvals + [place.take(value, "core", 1) for value in keyvals[1:count_y]]

    kept = [{}, {}]
    slot_own = jnp.minimum(lax.axis_index("wsh"), slots_dev - 1)
    live["bases"] = (left_bases, right_bases)
    live["moments"] = (moment1, moment2)
    chunks[0].step_z()
    settle()
    left_rows, right_all = live.pop("bases")
    live["mask"] = mask
    live["vectors"] = [vector_sets(vec_params[layer_at]) for layer_at in range(LAYERS)]
    live["left"] = fill_up(left_rows, wsh_count)
    live["right"] = lax.dynamic_index_in_dim(right_all, slot_own, 0, False).astype(BF16)
    chunks[0].step_x()
    chunks[1].step_z()
    settle()
    first_rows, second_rows = live.pop("moments")
    mask = live.pop("mask")
    vectors = live.pop("vectors")
    live["first"] = fill_up(first_rows, wsh_count)
    live["second"] = fill_up(second_rows, wsh_count)
    chunks[0].step_y()
    chunks[1].step_x()
    chunks[2].step_z()
    settle()
    chunks[1].step_y()
    chunks[2].step_x()
    chunks[3].step_z()
    query_0, live["keyvals0"], w_in_0 = project_step(place, stream_in[0], finish(0), vectors[0])
    live["query"] = query_0
    settle()
    chunks[2].step_y()
    chunks[3].step_x()
    chunks[4].step_z()
    keyvals_0 = keyvals_of(0)
    query_0 = live["query"]
    attn_0, summed_one_0, middle_0, mid_low_0 = mix_step(
        query_0, keyvals_0, stream_in[0], w_in_0, vectors[0], mask
    )
    hidden_0, live["act"], w_up_0 = up_step(mid_low_0, finish(1), vectors[0])
    settle()
    chunks[3].step_y()
    chunks[4].step_x()
    chunks[5].step_z()
    act_0 = live["act"]
    summed_two_0, live["result"], live["result_low"], w_down_0 = down_step(
        act_0, finish(2), middle_0, vectors[0]
    )
    settle()
    chunks[4].step_y()
    chunks[5].step_x()
    result_0, result_low_0 = live["result"], live["result_low"]
    query_1, live["keyvals1"], w_in_1 = project_step(place, result_low_0, finish(3), vectors[1])
    live["query"] = query_1
    live["left"] = to_owner(live["left"])
    settle()
    chunks[5].step_y()
    live["first"] = to_owner(live["first"])
    keyvals_1 = keyvals_of(1)
    query_1 = live["query"]
    attn_1, summed_one_1, middle_1, mid_low_1 = mix_step(
        query_1, keyvals_1, result_0, w_in_1, vectors[1], mask
    )
    hidden_1, live["act"], w_up_1 = up_step(mid_low_1, finish(4), vectors[1])
    settle()
    act_1 = live["act"]
    summed_two_1, _, result_low_1, w_down_1 = down_step(act_1, finish(5), middle_1, vectors[1])
    stream_out = result_low_1[None]

    blocks = [(w_in_0, w_up_0, w_down_0), (w_in_1, w_up_1, w_down_1)]
    lefts = [
        (stream_in[0], attn_0, mid_low_0, act_0),
        (result_low_0, attn_1, mid_low_1, act_1),
    ]
    crossed = [
        (place.take(jnp.concatenate(values[:3], axis=1), "core", 1), place.take(values[3], "core", 1))
        for values in lefts
    ]
    summed = [(summed_one_0, summed_two_0), (summed_one_1, summed_two_1)]
    hidden = [hidden_0, hidden_1]
    queries = [query_0, query_1]
    keyvals_all = [keyvals_0, keyvals_1]
    gains = [
        (vectors[layer_at]["gain_one"], vectors[layer_at]["gain_two"]) for layer_at in range(LAYERS)
    ]
    live = {
        "crossed": crossed,
        "left": live["left"],
        "first": live["first"],
        "second": to_owner(live["second"]),
        "right": live["right"],
    }
    jobs = []
    vec_terms = [None] * LAYERS

    every = []

    def settle_back():
        state = [(job.parts, job.by_y, job.by_x, job.groups) for job in jobs]
        state, values, terms = together(state, dict(live), [one.terms for one in every])
        for one, value in zip(every, terms):
            one.terms = value
        for job, fields in zip(jobs, state):
            job.parts, job.by_y, job.by_x, job.groups = fields
        live.update(values)

    def begin(layer_at, first_block, *sets):
        ids = [layer_at * NBLK + first_block + spot for spot in range(4)]
        jobs.append(
            Summing(
                place,
                ids,
                [
                    (lefts[layer_at][spot], live["crossed"][layer_at][spot // 3], right, spot % 3)
                    for spot, right in sets
                ],
            )
        )
        return jobs[-1]

    def close_step(layer_at, flow):
        live["two"], live["ffn"], live["sums_two"] = close(flow, summed[layer_at][1], gains[layer_at][1])

    def down_job(layer_at):
        return begin(layer_at, 8, (3, live["ffn"]))

    def in_job(layer_at):
        return begin(layer_at, 0, (0, live["joined"]), (1, live["branch_in"]))

    def up_job(layer_at):
        return begin(layer_at, 4, (2, live["hid"]))

    def feed_step(layer_at):
        w_in, w_up, w_down = blocks[layer_at]
        live["hid"], live["branch"], attn_grad, live["one"], live["sums_one"], live["sums_up"] = feed_back(
            live["two"], live["ffn"], summed[layer_at][0], hidden[layer_at], w_down, w_up, w_in, gains[layer_at][0]
        )
        live["attn_grad"] = attn_grad

    def attend_step(layer_at):
        live["grad_q"], mine, other = attend_back(
            queries[layer_at], keyvals_all[layer_at], live["attn_grad"], mask
        )
        live["pair"] = [mine, other]

    def send_step():
        mine, other = live["pair"]
        arrived = place.take(other, "core", 1)
        live["kv"] = [mine, arrived] + [
            place.take((mine[step].astype(F32) + arrived[step].astype(F32)).astype(BF16), "y", -step)[None]
            for step in range(1, count_y)
        ]

    def input_step(layer_at):
        live["joined"], grad_x, in_sums = input_back(live["grad_q"], live["kv"], live["one"], blocks[layer_at][0])
        sums_two, sums_one = live["sums_two"], live["sums_one"]
        vec_terms[layer_at] = jnp.concatenate(
            [
                in_sums[0, 0],
                in_sums[2, 0],
                sums_one[0],
                sums_two[0],
                sums_one[1:3].reshape(-1),
                sums_two[1:3].reshape(-1),
                live["sums_up"].reshape(-1),
            ]
        )
        live["branch_in"] = live["branch"]
        return grad_x

    close_step(1, cotangent[0])
    down_1 = down_job(1)
    feed_step(1)
    settle_back()
    down_1.first_y()
    down_1.first_x()
    up_1 = up_job(1)
    settle_back()
    down_1.second_x()
    down_1.second_y()
    up_1.first_y()
    up_1.first_x()
    attend_step(1)
    settle_back()
    send_step()
    down_1.third()
    up_1.second_x()
    settle_back()
    up_1.second_y()
    grad_flow = input_step(1)
    close_step(0, grad_flow)
    settle_back()
    up_1.third()
    in_1 = in_job(1)
    down_0 = down_job(0)
    settle_back()
    in_1.first_y()
    in_1.first_x()
    feed_step(0)
    settle_back()
    in_1.second_x()
    in_1.second_y()
    down_0.first_y()
    down_0.first_x()
    attend_step(0)
    settle_back()
    send_step()
    in_1.third()
    down_0.second_x()
    down_0.second_y()
    up_0 = up_job(0)
    settle_back()
    down_0.third()
    up_0.first_y()
    up_0.first_x()
    grad_flow = input_step(0)
    every.append(EverySum(place, jnp.stack(vec_terms)))
    settle_back()
    every[0].step("core")
    up_0.second_x()
    up_0.second_y()
    in_0 = in_job(0)
    settle_back()
    up_0.third()
    every[0].step("y")
    in_0.first_y()
    in_0.first_x()
    settle_back()
    every[0].step("x")
    in_0.second_x()
    in_0.second_y()
    settle_back()
    every[0].step("z", 1)
    in_0.third()
    settle_back()
    every[0].step("z", 2)
    stream_grad = grad_flow[None]
    vec_grads = every[0].total() * scaling
    groups = [group for job in jobs for group in job.groups]
    turned = [job.turned for job in jobs for group in job.groups]
    ids = [block for job in jobs for block in job.ids]

    owner_flat = owner_slots.reshape(-1)
    block_count = LAYERS * NBLK
    owner_sorted = jnp.stack([owner_flat[block] for block in ids])
    picks = owner_sorted[None, :] == jnp.arange(slot_total, dtype=jnp.int32)[:, None]
    spots = jnp.where(
        jnp.any(picks, axis=1), jnp.argmax(picks, axis=1).astype(jnp.int32), block_count
    )
    by_slot = route(groups, turned, spots, slots_dev, wsh_count, rows_dev, scaling)

    arrived = lax.all_to_all(
        by_slot.reshape(ctx_count * wsh_count, rows_dev, width), ("ctx", "wsh"), 0, 0, tiled=True
    )
    quarter_parts = []
    for step in range(ctx_count):
        step_y, step_core = step // CORES, step % CORES
        to_ctx = ((place.at["y"] + step_y) % count_y) * CORES + (place.at["core"] + step_core) % CORES
        part = lax.dynamic_index_in_dim(by_slot, to_ctx, 0, False)[:slots_dev]
        pairs = [
            (y * CORES + core, ((y + step_y) % count_y) * CORES + (core + step_core) % CORES)
            for y in range(count_y)
            for core in range(CORES)
        ]
        quarter_parts.append(lax.ppermute(part, "ctx", pairs) if step else part)
    quarters = [(source % CORES) * count_y + source // CORES for source in range(ctx_count)]
    by_rows = jnp.stack(quarter_parts)
    by_source = [
        lax.dynamic_index_in_dim(
            by_rows,
            ((place.at["y"] - source // CORES) % count_y) * CORES + (place.at["core"] - source % CORES) % CORES,
            0,
            False,
        )
        for source in range(ctx_count)
    ]
    by_source = jnp.stack([by_source[quarters.index(quarter)] for quarter in range(ctx_count)])
    block_grads = by_source.transpose(1, 2, 0, 3).reshape(slots_dev, rows_dev, BLK).astype(F32)
    arrived, block_grads = together(arrived, block_grads)
    rotated_own, update_own = rotate(
        arrived.reshape(ctx_count, BLK, width), quarters, live["right"], live["left"], live["first"], live["second"]
    )

    update = from_owner(update_own, wsh_count)
    update, vec_grads = together(update, vec_grads)
    master_low = (master - LR_BLOCK * update[:slots_dev].astype(F32)).astype(BF16)
    master_low, update, rotated_own = together(master_low, update, rotated_own)
    parts = gather_list(place, master_low, "y")
    rotated = from_owner(rotated_own, wsh_count)
    across = place.take(master_low, "core", 1)
    new_master = master - LR_BLOCK * update[:slots_dev].astype(F32)
    parts = parts + [across] + [place.take(value, "core", 1) for value in parts[1:]]
    owner_ctx, owner_at = owner_flat // slots_dev, owner_flat % slots_dev
    step_y = (owner_ctx // CORES - place.at["y"]) % count_y
    step_core = (owner_ctx % CORES - place.at["core"]) % CORES
    table = jnp.stack([step_core * count_y + step_y, owner_at]).astype(jnp.int32)
    new_weights = pick(parts, table).reshape(LAYERS, NBLK, rows_dev, BLK)
    rotated, _ = together(rotated, (new_weights[0, 0, :8, :128], new_master[0, :8, :128]))
    rotated = rotated[:slots_dev].astype(F32)

    new_moment1 = DECAY_RATE * moment1 + (1.0 - DECAY_RATE) * rotated
    new_moment2 = DECAY_RATE * moment2 + (1.0 - DECAY_RATE) * rotated * rotated

    new_vec_moment1 = DECAY_RATE * vec_moment1 + (1.0 - DECAY_RATE) * vec_grads
    new_vec_moment2 = DECAY_RATE * vec_moment2 + (1.0 - DECAY_RATE) * vec_grads * vec_grads
    new_vec_params = vec_params - LR_VEC * new_vec_moment1 / (jnp.sqrt(new_vec_moment2) + EPS_ADAM)
    return (
        stream_out,
        stream_grad,
        block_grads,
        new_moment1,
        new_moment2,
        new_master,
        new_weights,
        vec_grads,
        new_vec_params,
        new_vec_moment1,
        new_vec_moment2,
    )


def solution(mesh):
    rows = P("ctx", "wsh", None)
    placed = (
        P("wsh", "ctx", None),
        P("wsh", None),
        P("wsh", "ctx", None),
        P(None, None, "wsh", None),
        P(),
        P(),
        rows,
        rows,
        P("ctx", None, None),
        rows,
        rows,
        P(),
        P(),
    )
    return jax.shard_map(
        on_device,
        mesh=mesh,
        in_specs=placed,
        out_specs=(
            P("wsh", "ctx", None),
            P("wsh", "ctx", None),
            rows,
            rows,
            rows,
            rows,
            P(None, None, "wsh", None),
            P(),
            P(),
            P(),
            P(),
        ),
        check_vma=False,
    )
```

```python
import functools

import jax
import jax.numpy as jnp
import numpy as np
from jax import lax
from jax.experimental import pallas as pl
from jax.experimental.pallas import tpu as pltpu
from jax.sharding import PartitionSpec as P

D = 1024
HEADS = 16
HEAD_DIM = 64
FF = 4096
BLK = 1024
LAYERS = 2
NBLK = 12
CORES = 2
DEPTH_Z = 4

EPS_NORM = 1e-05
EPS_ADAM = 1e-08
LR_BLOCK = 0.1
LR_VEC = 0.25
DECAY_RATE = 0.5
VMEM_BYTES = 56 * 1024 * 1024
BF16 = jnp.bfloat16
F32 = jnp.float32


class Place:
    def __init__(self, ctx_count, wsh_count):
        self.size = {
            "core": CORES,
            "y": ctx_count // CORES,
            "z": DEPTH_Z,
            "x": wsh_count // DEPTH_Z,
        }
        ctx_at = lax.axis_index("ctx")
        wsh_at = lax.axis_index("wsh")
        self.at = {
            "core": ctx_at % CORES,
            "y": ctx_at // CORES,
            "z": wsh_at // self.size["x"],
            "x": wsh_at % self.size["x"],
        }

    def take(self, value, axis, step):
        name, slow, fast = {
            "core": ("ctx", "y", "core"),
            "y": ("ctx", "y", "core"),
            "z": ("wsh", "z", "x"),
            "x": ("wsh", "z", "x"),
        }[axis]
        extent = self.size[axis]
        pairs = []
        for slow_at in range(self.size[slow]):
            for fast_at in range(self.size[fast]):
                if axis == fast:
                    other = (slow_at, (fast_at + step) % extent)
                else:
                    other = ((slow_at + step) % extent, fast_at)
                pairs.append(
                    (
                        other[0] * self.size[fast] + other[1],
                        slow_at * self.size[fast] + fast_at,
                    )
                )
        return lax.ppermute(value, name, pairs)

    def gather(self, value, axis):
        steps = range(1, self.size[axis])
        return jnp.stack([value] + [self.take(value, axis, step) for step in steps])

    def collect(self, values, axis):
        steps = range(1, self.size[axis])
        return [values[0]] + [self.take(values[step], axis, -step) for step in steps]

    def swap_z(self, values):
        count_x = self.size["x"]
        lines = [[z * count_x + x for z in range(self.size["z"])] for x in range(count_x)]
        return lax.all_to_all(values, "wsh", 0, 0, tiled=True, axis_index_groups=lines)

    def scatter(self, values, axis):
        total = values[0].astype(F32)
        for step in range(1, self.size[axis]):
            total = total + self.take(values[step], axis, -step).astype(F32)
        return total


def vector_parts(vector):
    pieces = [vector[spot * D : (spot + 1) * D] for spot in range(8)]
    return pieces + [vector[8 * D :]]


def dot(left, right):
    return jnp.dot(left, right, preferred_element_type=F32)


def dot_t(left, right):
    return lax.dot_general(left, right, (((1,), (1,)), ((), ())), preferred_element_type=F32)


def after(value, *others):
    return lax.optimization_barrier((value,) + others)[0]


def together(*values):
    return lax.optimization_barrier(values)


def add_up(values):
    return sum(value.astype(F32) for value in values)


class Gathering:
    def __init__(self, place, shard, split_count):
        self.place = place
        self.count, self.rows, _ = shard.shape
        half_rows, half_cols = self.rows // 2, BLK // 2
        has_y = place.size["y"] == 2
        self.split_count = split_count if has_y else 0
        whole_count = self.count - self.split_count
        mine = lax.dynamic_slice_in_dim(shard, place.at["core"] * half_rows, half_rows, 1)
        whole = mine[self.split_count :]
        pieces = [
            part
            for block in range(whole_count)
            for part in (whole[block, :, :half_cols], whole[block, :, half_cols:])
        ]
        parts = []
        if pieces:
            parts.append(jnp.stack(pieces))
        if has_y:
            parts.insert(
                0,
                lax.dynamic_slice_in_dim(
                    mine[: self.split_count], place.at["y"] * half_cols, half_cols, 2
                ),
            )
        self.held = [jnp.concatenate(parts)]
        self.crossed = []

    def step_z(self):
        piece = self.held[0]
        copies = jnp.broadcast_to(piece[None], (self.place.size["z"],) + piece.shape)
        self.held = [self.place.swap_z(copies)]

    def step_x(self):
        self.held = gather_list(self.place, self.held[0], "x")

    def step_y(self):
        self.held = [jnp.stack(self.held)]
        if self.split_count:
            value = self.held[0][:, :, : self.split_count]
            self.held.append(self.place.take(value, "y", 1))
        self.crossed = [self.place.take(self.held[0], "core", 1)]

    def step_core(self):
        if self.split_count:
            self.crossed.append(self.place.take(self.held[1], "core", 1))

    def pieces(self):
        split, mine, crossed = self.split_count, self.held, self.crossed
        part = (mine[0].shape[:2]) + (1,) + mine[0].shape[3:]

        def spec(place_of):
            return pl.BlockSpec(part, lambda i, where: (0, 0, place_of(i), 0, 0))

        last = mine[0].shape[2] - 1
        low = spec(lambda i: jnp.where(i < split, i, 2 * i - split))
        high = spec(lambda i: jnp.minimum(jnp.where(i < split, split + 1, 2 * i - split + 1), last))
        operands = [mine[0], crossed[0], mine[0], crossed[0]]
        specs = [low, low, high, high]
        if split:
            operands += [mine[1], crossed[1]]
            specs += [spec(lambda i: jnp.minimum(i, split - 1))] * 2
        return operands, specs

    def where(self):
        return jnp.stack([self.place.at[name] for name in ("x", "y", "core")]).astype(jnp.int32)


def open_block(split, where, pieces, out):
    spot = pl.program_id(0)
    extent_x, extent_z, _, half_rows, half_cols = pieces[0].shape
    x_at, y_at, core_at = where[0], where[1], where[2]

    def put(first_col, sources):
        low_col = pl.ds(first_col * half_cols, half_cols)
        high_col = pl.ds((1 - first_col) * half_cols, half_cols)
        for step_x in range(extent_x):
            for z in range(extent_z):
                base = (z * extent_x + lax.rem(x_at + step_x, extent_x)) * 2
                mine = pl.ds(pl.multiple_of((base + core_at) * half_rows, half_rows), half_rows)
                other = pl.ds(pl.multiple_of((base + 1 - core_at) * half_rows, half_rows), half_rows)
                out[0, mine, low_col] = sources[0][step_x, z, 0]
                out[0, other, low_col] = sources[1][step_x, z, 0]
                out[0, mine, high_col] = sources[2][step_x, z, 0]
                out[0, other, high_col] = sources[3][step_x, z, 0]

    if split:
        sources = list(pieces[:2]) + list(pieces[4:])
        for y in range(2):
            pl.when((spot < split) & (y_at == y))(functools.partial(put, y, sources))
        pl.when(spot >= split)(lambda: put(0, pieces[:4]))
    else:
        put(0, pieces[:4])


def call(body, grid, in_specs, out_specs, out_shape, scratch=(), prefetch=0, cost=1.0, name=None):
    return pl.pallas_call(
        body,
        grid_spec=pltpu.PrefetchScalarGridSpec(
            num_scalar_prefetch=prefetch,
            grid=grid,
            in_specs=in_specs,
            out_specs=out_specs,
            scratch_shapes=list(scratch),
        ),
        out_shape=out_shape,
        compiler_params=pltpu.CompilerParams(vmem_limit_bytes=VMEM_BYTES),
        cost_estimate=pl.CostEstimate(flops=int(cost * 2e7), bytes_accessed=0, transcendentals=0),
        name=name,
    )


def shaped(shape, dtype):
    return jax.ShapeDtypeStruct(shape, dtype)


def fixed(shape):
    return pl.BlockSpec(shape, lambda *at: (0,) * len(shape))


def norm_stats(summed):
    average = jnp.mean(summed, axis=-1, keepdims=True)
    centred = summed - average
    variance = jnp.mean(centred * centred, axis=-1, keepdims=True)
    scale = lax.rsqrt(variance + EPS_NORM)
    return centred * scale, scale


def norm_back(grad, normed, scale, gain):
    flow = grad * gain
    return (
        flow
        - jnp.mean(flow, axis=-1, keepdims=True)
        - normed * jnp.mean(flow * normed, axis=-1, keepdims=True)
    ) * scale


BLOCK = pl.BlockSpec((1, BLK, BLK), lambda i, *at: (i, 0, 0))
BLOCKS = jax.ShapeDtypeStruct((4, BLK, BLK), BF16)


def project_kernel(split, where, x_low, bias, *refs):
    pieces, (query, keyval, weight) = refs[:-3], refs[-3:]
    open_block(split, where, pieces, weight)

    def value():
        return (dot(x_low[...], weight[0]) + bias[0]).astype(BF16)

    @pl.when(pl.program_id(0) == 0)
    def _():
        query[...] = value() * HEAD_DIM ** (-0.5)

    @pl.when((pl.program_id(0) > 0) & (pl.program_id(0) < 3))
    def _():
        keyval[...] = value()


def project(x_low, chunk, bias):
    tokens = x_low.shape[0]
    pieces, specs = chunk.pieces()
    return call(
        functools.partial(project_kernel, chunk.split_count),
        (4,),
        [fixed((tokens, D)), pl.BlockSpec((1, 1, D), lambda i, where: (jnp.minimum(i, 2), 0, 0))] + specs,
        [
            fixed((tokens, D)),
            pl.BlockSpec((tokens, D), lambda i, where: (0, jnp.clip(i - 1, 0, 1))),
            BLOCK,
        ],
        [shaped((tokens, D), BF16), shaped((tokens, 2 * D), BF16), BLOCKS],
        prefetch=1,
        cost=8.0,
        name="project",
    )(chunk.where(), x_low, bias, *pieces)


def head_weights(query_h, keys_h, masks):
    scores = [
        dot_t(key, query_h) + mask for key, mask in zip(keys_h, masks)
    ]
    peak = functools.reduce(
        jnp.maximum, [jnp.max(score, axis=0, keepdims=True) for score in scores]
    )
    scores = [jnp.exp(score - peak) for score in scores]
    total = sum(jnp.sum(score, axis=0, keepdims=True) for score in scores)
    return scores, 1.0 / total


def dot_tt(left, right):
    return lax.dot_general(left, right, (((0,), (0,)), ((), ())), preferred_element_type=F32)


def head_of(ref, head):
    return ref[:, pl.ds(head * HEAD_DIM, HEAD_DIM)]


def attend_kernel(count, tokens, query, mask, *refs):
    keys, values, out = refs[:count], refs[count : 2 * count], refs[-1]
    masks = [mask[pl.ds(spot * tokens, tokens), :] for spot in range(count)]
    mixed = []
    for head in range(2):
        weights, inverse = head_weights(head_of(query, head), [head_of(key, head) for key in keys], masks)
        total = sum(
            dot_tt(head_of(value, head), weight.astype(BF16)) for value, weight in zip(values, weights)
        )
        mixed.append(total * inverse)
    out[...] = jnp.concatenate(mixed, axis=0).T.astype(BF16)


def pair_specs(tokens, count):
    pair = 2 * HEAD_DIM
    half = D // pair
    return (
        [pl.BlockSpec((tokens, pair), lambda i: (0, i))] * count
        + [pl.BlockSpec((tokens, pair), lambda i: (0, half + i))] * count
    )


def attend(query, keyvals, mask):
    tokens = query.shape[0]
    count = len(keyvals)
    pair = 2 * HEAD_DIM
    return call(
        functools.partial(attend_kernel, count, tokens),
        (D // pair,),
        [pl.BlockSpec((tokens, pair), lambda i: (0, i)), fixed(mask.shape)]
        + pair_specs(tokens, count),
        pl.BlockSpec((tokens, pair), lambda i: (0, i)),
        shaped((tokens, D), BF16),
        cost=14.0,
        name="attend",
    )(query, mask, *keyvals, *keyvals)


def attend_back_kernel(count, count_y, tokens, query, grad, mask, *refs):
    keys, values = refs[:count], refs[count : 2 * count]
    grad_q, mine, other = refs[2 * count :]
    masks = [mask[pl.ds(spot * tokens, tokens), :] for spot in range(count)]
    scale = HEAD_DIM ** (-0.5)
    grads_q = []
    grads_k = [[] for _ in range(count)]
    grads_v = [[] for _ in range(count)]
    for head in range(2):
        query_h = head_of(query, head)
        grad_h = head_of(grad, head)
        keys_h = [head_of(key, head) for key in keys]
        weights, inverse = head_weights(query_h, keys_h, masks)
        probs = [weight * inverse for weight in weights]
        grad_probs = [dot_t(head_of(value, head), grad_h) for value in values]
        inner = sum(
            jnp.sum(prob * grad_prob, axis=0, keepdims=True)
            for prob, grad_prob in zip(probs, grad_probs)
        )
        flow_q = 0.0
        for spot in range(count):
            grad_score = (probs[spot] * (grad_probs[spot] - inner)).astype(BF16)
            flow_q = flow_q + dot_tt(keys_h[spot], grad_score)
            grads_k[spot].append(dot(grad_score, query_h))
            grads_v[spot].append(dot(probs[spot].astype(BF16), grad_h))
        grads_q.append(flow_q * scale)
    grad_q[...] = jnp.concatenate(grads_q, axis=0).T.astype(BF16)
    for spot in range(count):
        out = mine if spot < count_y else other
        out[spot % count_y, 0] = jnp.concatenate(grads_k[spot], axis=1).astype(BF16)
        out[spot % count_y, 1] = jnp.concatenate(grads_v[spot], axis=1).astype(BF16)


def attend_back(query, keyvals, grad, mask):
    tokens = query.shape[0]
    count = len(keyvals)
    count_y = count // CORES
    pair = 2 * HEAD_DIM
    part = pl.BlockSpec((count_y, 2, tokens, pair), lambda i: (0, 0, 0, i))
    return call(
        functools.partial(attend_back_kernel, count, count_y, tokens),
        (D // pair,),
        [pl.BlockSpec((tokens, pair), lambda i: (0, i))] * 2
        + [fixed(mask.shape)]
        + pair_specs(tokens, count),
        [pl.BlockSpec((tokens, pair), lambda i: (0, i)), part, part],
        [shaped((tokens, D), BF16)] + [shaped((count_y, 2, tokens, D), BF16)] * 2,
        cost=21.0,
        name="attend_back",
    )(query, grad, mask, *keyvals, *keyvals)


def mix_kernel(attn, weight, carried, vecs, summed, middle, middle_low):
    value = carried[...].astype(F32) + (dot(attn[...], weight[0]) + vecs[0:1, :])
    summed[...] = value
    normed, _ = norm_stats(value)
    value = normed * vecs[1:2, :] + vecs[2:3, :]
    middle[...] = value
    middle_low[...] = value.astype(BF16)


def mix(attn, w_in, carried, vecs):
    tokens = attn.shape[0]
    full = fixed((tokens, D))
    return call(
        mix_kernel,
        (1,),
        [full, pl.BlockSpec((1, BLK, BLK), lambda i: (3, 0, 0)), full, fixed(vecs.shape)],
        [full, full, full],
        [shaped((tokens, D), F32), shaped((tokens, D), F32), shaped((tokens, D), BF16)],
        cost=4.0,
        name="mix",
    )(attn, w_in, carried, vecs)


def erf_part(hidden):
    return (1.0 + lax.erf(hidden * (0.5**0.5))) * 0.5


def up_kernel(split, where, middle_low, bias, *refs):
    pieces, (hidden, act, weight) = refs[:-3], refs[-3:]
    open_block(split, where, pieces, weight)
    value = dot(middle_low[...], weight[0]) + bias[0]
    hidden[...] = value
    act[...] = (value * erf_part(value)).astype(BF16)


def up(middle_low, chunk, bias):
    tokens = middle_low.shape[0]
    pieces, specs = chunk.pieces()
    part = pl.BlockSpec((tokens, BLK), lambda i, where: (0, i))
    return call(
        functools.partial(up_kernel, chunk.split_count),
        (FF // BLK,),
        [fixed((tokens, D)), pl.BlockSpec((1, 1, BLK), lambda i, where: (i, 0, 0))] + specs,
        [part, part, BLOCK],
        [shaped((tokens, FF), F32), shaped((tokens, FF), BF16), BLOCKS],
        prefetch=1,
        cost=8.0,
        name="up",
    )(chunk.where(), middle_low, bias, *pieces)


def down_kernel(split, where, act, middle, vecs, *refs):
    pieces, (summed, result, result_low, weight, total) = refs[:-5], refs[-5:]
    open_block(split, where, pieces, weight)
    spot = pl.program_id(0)
    value = dot(act[...], weight[0])

    @pl.when(spot == 0)
    def _():
        total[...] = value

    @pl.when(spot > 0)
    def _():
        total[...] += value

    @pl.when(spot == pl.num_programs(0) - 1)
    def _():
        value = middle[...] + (total[...] + vecs[0:1, :])
        summed[...] = value
        normed, _ = norm_stats(value)
        value = normed * vecs[1:2, :] + vecs[2:3, :]
        result[...] = value
        result_low[...] = value.astype(BF16)


def down(act, chunk, middle, vecs):
    tokens = act.shape[0]
    full = fixed((tokens, D))
    pieces, specs = chunk.pieces()
    return call(
        functools.partial(down_kernel, chunk.split_count),
        (FF // BLK,),
        [pl.BlockSpec((tokens, BLK), lambda i, where: (0, i)), full, fixed(vecs.shape)] + specs,
        [full, full, full, BLOCK],
        [shaped((tokens, D), F32), shaped((tokens, D), F32), shaped((tokens, D), BF16), BLOCKS],
        scratch=[pltpu.VMEM((tokens, D), F32)],
        prefetch=1,
        cost=8.0,
        name="down",
    )(chunk.where(), act, middle, vecs, *pieces)


def column_sum(value):
    return jnp.sum(value, axis=0, keepdims=True)


def close_kernel(flow, summed, gain, back_out, low_out, sums):
    grad = flow[...].astype(F32)
    normed, scale = norm_stats(summed[...])
    back = norm_back(grad, normed, scale, gain[...])
    back_out[...] = back
    low = back.astype(BF16)
    low_out[...] = low
    sums[0:1, :] = column_sum(low.astype(F32))
    sums[1:2, :] = column_sum(grad * normed)
    sums[2:3, :] = column_sum(grad)
    sums[3:8, :] = jnp.zeros((5, D), F32)


def close(flow, summed, gain):
    tokens = flow.shape[0]
    full = fixed((tokens, D))
    return call(
        close_kernel,
        (1,),
        [full, full, fixed((1, D))],
        [full, full, fixed((8, D))],
        [shaped((tokens, D), F32), shaped((tokens, D), BF16), shaped((8, D), F32)],
        cost=3.0,
        name="close",
    )(flow, summed, gain)


def feed_back_kernel(
    grad_two, ffn_low, summed_one, hidden, w_down, w_up, w_out, gain,
    hid_low, branch_low, attn_grad, grad_one, sums, bias_sums, total,
):
    spot = pl.program_id(0)

    @pl.when(spot == 0)
    def _():
        total[...] = grad_two[...]

    value = hidden[...]
    slope = erf_part(value) + value * jnp.exp(-0.5 * value * value) * ((2.0 * np.pi) ** -0.5)
    low = (dot_t(ffn_low[...], w_down[0]) * slope).astype(BF16)
    hid_low[...] = low
    bias_sums[0] = column_sum(low.astype(F32))
    total[...] += dot_t(low, w_up[0])

    @pl.when(spot == pl.num_programs(0) - 1)
    def _():
        grad = total[...]
        normed, scale = norm_stats(summed_one[...])
        back = norm_back(grad, normed, scale, gain[...])
        grad_one[...] = back
        low = back.astype(BF16)
        branch_low[...] = low
        sums[0:1, :] = column_sum(low.astype(F32))
        sums[1:2, :] = column_sum(grad * normed)
        sums[2:3, :] = column_sum(grad)
        sums[3:8, :] = jnp.zeros((5, D), F32)
        attn_grad[...] = dot_t(low, w_out[0]).astype(BF16)


def feed_back(grad_two, ffn_low, summed_one, hidden, w_down, w_up, w_in, gain):
    tokens = ffn_low.shape[0]
    full = fixed((tokens, D))
    part = pl.BlockSpec((tokens, BLK), lambda i: (0, i))
    weight = pl.BlockSpec((1, BLK, BLK), lambda i: (i, 0, 0))
    return call(
        feed_back_kernel,
        (FF // BLK,),
        [full, full, full, part, weight, weight, pl.BlockSpec((1, BLK, BLK), lambda i: (3, 0, 0)), fixed((1, D))],
        [part, full, full, full, fixed((8, D)), pl.BlockSpec((1, 1, BLK), lambda i: (i, 0, 0))],
        [
            shaped((tokens, FF), BF16),
            shaped((tokens, D), BF16),
            shaped((tokens, D), BF16),
            shaped((tokens, D), F32),
            shaped((8, D), F32),
            shaped((FF // BLK, 1, BLK), F32),
        ],
        scratch=[pltpu.VMEM((tokens, D), F32)],
        cost=15.0,
        name="feed_back",
    )(grad_two, ffn_low, summed_one, hidden, w_down, w_up, w_in, gain)


def input_back_kernel(count, grad_q, grad_one, weight, *refs):
    parts, (joined, result, sums, total) = refs[:count], refs[count:]
    spot = pl.program_id(0)

    @pl.when(spot == 0)
    def _():
        joined[...] = grad_q[...]
        total[...] = grad_one[...]

    @pl.when(spot > 0)
    def _():
        joined[...] = sum(part[0, 0].astype(F32) for part in parts).astype(BF16)

    low = joined[...]
    sums[0] = column_sum(low.astype(F32))
    total[...] += dot_t(low, weight[0])

    @pl.when(spot == pl.num_programs(0) - 1)
    def _():
        result[...] = total[...]


def input_back(grad_q, parts, grad_one, w_in):
    tokens = grad_q.shape[0]
    full = fixed((tokens, D))
    return call(
        functools.partial(input_back_kernel, len(parts)),
        (3,),
        [full, full, pl.BlockSpec((1, BLK, BLK), lambda i: (i, 0, 0))]
        + [pl.BlockSpec((1, 1, tokens, D), lambda i: (0, jnp.maximum(i - 1, 0), 0, 0))] * len(parts),
        [pl.BlockSpec((tokens, D), lambda i: (0, i)), full, pl.BlockSpec((1, 1, D), lambda i: (i, 0, 0))],
        [shaped((tokens, 3 * D), BF16), shaped((tokens, D), F32), shaped((3, 1, D), F32)],
        scratch=[pltpu.VMEM((tokens, D), F32)],
        cost=8.0,
        name="input_back",
    )(grad_q, grad_one, w_in, *parts)


def gather_list(place, value, axis):
    return [value] + [place.take(value, axis, step) for step in range(1, place.size[axis])]


def vector_sets(vector):
    parts = vector_parts(vector)
    return {
        "project": jnp.stack([parts[0], jnp.zeros((D,), F32), parts[1]])[:, None],
        "mix": jnp.stack([parts[2], parts[4], parts[5]]),
        "up": parts[8].reshape(FF // BLK, 1, BLK),
        "down": jnp.stack([parts[3], parts[6], parts[7]]),
        "gain_one": parts[4][None],
        "gain_two": parts[6][None],
    }


def project_step(place, carried_low, chunk, vectors):
    query, keyval, w_in = project(carried_low, chunk, vectors["project"])
    keyvals = [keyval, *gather_list(place, keyval, "y")[1:], place.take(keyval, "core", 1)]
    return query, keyvals, w_in


def mix_step(query, keyvals, carried, w_in, vectors, mask):
    attn_low = attend(query, keyvals, mask)
    return attn_low, *mix(attn_low, w_in, carried, vectors["mix"])


def up_step(mid_low, chunk, vectors):
    return up(mid_low, chunk, vectors["up"])


def down_step(act_low, chunk, middle, vectors):
    return down(act_low, chunk, middle, vectors["down"])


def sum_kernel(count_one, first_half, sizes, turned, where, *refs):
    sets = (refs[:4], refs[4:8]) if count_one is not None else (refs[:4],)
    outs, shared, product = refs[4 * len(sets) : -2], refs[-2], refs[-1]
    x_at, y_at = where[1], where[2]
    extent_z, extent_x, extent_y, rows = sizes
    cols = BLK // (CORES * extent_y)
    spot = pl.program_id(0)

    def both(mine, other):
        return jnp.concatenate([mine[...], other[...]], axis=0)

    def share(left_mine, left_other, right_mine, right_other):
        shared[...] = (both(right_mine, right_other) if turned else both(left_mine, left_other)).T

    def multiply(left_mine, left_other, right_mine, right_other):
        value = both(left_mine, left_other) if turned else both(right_mine, right_other)
        product[...] = dot(shared[...], value).astype(BF16)

    pl.when(spot == 0)(lambda: share(*sets[0]))
    if len(sets) == 1:
        multiply(*sets[0])
    else:
        pl.when(spot == count_one)(lambda: share(*sets[1]))
        pl.when(spot < count_one)(lambda: multiply(*sets[0]))
        pl.when(spot >= count_one)(lambda: multiply(*sets[1]))

    def put(y_first, x, y):
        for step_y in range(extent_y):
            from_col = (y + step_y) % extent_y * cols
            for step_x in range(extent_x):
                for z in range(extent_z):
                    from_row = (z * extent_x + (x + step_x) % extent_x) * rows
                    if turned:
                        value = product[pl.ds(from_col, cols), pl.ds(from_row, rows)]
                    else:
                        value = product[pl.ds(from_row, rows), pl.ds(from_col, cols)]
                    if y_first:
                        outs[step_y][step_x, z, 0] = value
                    else:
                        outs[extent_y + step_x][step_y, z, 0] = value

    for x in range(extent_x):
        for y in range(extent_y):
            here = (x_at == x) & (y_at == y)
            pl.when(here & (spot < first_half))(functools.partial(put, True, x, y))
            pl.when(here & (spot >= first_half))(functools.partial(put, False, x, y))


def partial_sums(place, sets):
    tokens = sets[0][0].shape[0]
    extent_z, extent_x, extent_y = (place.size[name] for name in ("z", "x", "y"))
    rows = BLK // (extent_z * extent_x)
    half = BLK // CORES
    cols = half // extent_y
    where = jnp.stack([place.at[name] for name in ("z", "x", "y", "core")]).astype(jnp.int32)
    counts = [max(one[0].shape[1], one[2].shape[1]) // BLK for one in sets]
    count = sum(counts)
    first_half = count // 2
    specs = []
    start = 0
    for one, amount in zip(sets, counts):

        def at(i, start=start, amount=amount):
            return jnp.clip(i - start, 0, amount - 1)

        many_left, many_right = one[0].shape[1] > BLK, one[2].shape[1] > BLK
        for first in (0, one[4]):
            specs.append(
                pl.BlockSpec(
                    (tokens, BLK),
                    lambda i, where, at=at, many=many_left, first=first: (0, first + (at(i) if many else 0)),
                )
            )
        specs += [
            pl.BlockSpec(
                (tokens, half),
                lambda i, where, at=at, many=many_right: (0, (at(i) * CORES if many else 0) + where[3]),
            )
        ] * 2
        start += amount
    turned = sets[0][0].shape[1] > BLK
    tile = (cols, rows) if turned else (rows, cols)
    part_y = (extent_x, extent_z, 1) + tile
    part_x = (extent_y, extent_z, 1) + tile
    spec_y = pl.BlockSpec(part_y, lambda i, where: (0, 0, jnp.minimum(i, first_half - 1), 0, 0))
    spec_x = pl.BlockSpec(part_x, lambda i, where: (0, 0, jnp.maximum(i - first_half, 0), 0, 0))
    outs = call(
        functools.partial(
            sum_kernel,
            counts[0] if len(sets) > 1 else None,
            first_half,
            (extent_z, extent_x, extent_y, rows),
            turned,
        ),
        (count,),
        specs,
        [spec_y] * extent_y + [spec_x] * extent_x,
        [shaped((extent_x, extent_z, first_half) + tile, BF16)] * extent_y
        + [shaped((extent_y, extent_z, count - first_half) + tile, BF16)] * extent_x,
        scratch=[
            pltpu.VMEM((half if turned else BLK, 2 * tokens), BF16),
            pltpu.VMEM((half, BLK) if turned else (BLK, half), BF16),
        ],
        prefetch=1,
        cost=8.0,
        name="partial_sums",
    )(where, *[value for one in sets for value in one[:4]])
    return outs[:extent_y], outs[extent_y:]


class Summing:
    def __init__(self, place, ids, sets):
        self.place = place
        self.ids = ids
        self.turned = False
        if (BLK // (CORES * place.size["y"])) % 128:
            self.plain = True
            self.parts = self.by_y = self.by_x = ()
            self.groups = [sum_job_plain(place, one[0], one[2], "y")[None] for one in sets]
        else:
            self.plain = False
            sets = [
                (*one[:3], place.take(one[2], "core", 1) if one[4] is None else one[4], one[3])
                for one in sets
            ]
            self.turned = sets[0][0].shape[1] > BLK
            self.parts = partial_sums(place, sets)
            self.by_y = self.by_x = ()
            self.groups = ()

    def first_y(self):
        if not self.plain:
            self.by_y = self.place.collect(self.parts[0], "y")

    def first_x(self):
        if not self.plain:
            self.by_x = self.place.collect(self.parts[1], "x")

    def second_x(self):
        if not self.plain:
            total = add_up(self.by_y)
            parts = [total[step].astype(BF16) for step in range(self.place.size["x"])]
            self.by_y = self.place.collect(parts, "x")

    def second_y(self):
        if not self.plain:
            total = add_up(self.by_x)
            parts = [total[step].astype(BF16) for step in range(self.place.size["y"])]
            self.by_x = self.place.collect(parts, "y")

    def third(self):
        if not self.plain:
            both = jnp.concatenate([add_up(self.by_y), add_up(self.by_x)], axis=1)
            self.groups = [self.place.swap_z(both.astype(BF16))]


def route_kernel(turned, slots, scaling, spots, *refs):
    parts, (out, total) = refs[: len(turned)], refs[len(turned) :]
    at = 0
    for part, turn in zip(parts, turned):
        for block in range(part.shape[1]):
            value = sum(part[addend, block].astype(F32) for addend in range(part.shape[0]))
            value = value * scaling
            total[at] = (value.T if turn else value).astype(BF16)
            at += 1
    total[at] = jnp.zeros(total.shape[1:], BF16)
    for ctx in range(out.shape[0]):
        for spot in range(out.shape[1]):
            if spot < slots:
                out[ctx, spot] = total[spots[ctx * slots + spot]]
            else:
                out[ctx, spot] = total[at]


def route(groups, turned, spots, slots, wsh_count, rows, scaling):
    cols = groups[0].shape[2] * groups[0].shape[3] // rows
    blocks = sum(group.shape[1] for group in groups)
    shape = (spots.shape[0] // slots, wsh_count, rows, cols)
    return call(
        functools.partial(route_kernel, turned, slots, scaling),
        (1,),
        [fixed(group.shape) for group in groups],
        fixed(shape),
        shaped(shape, BF16),
        scratch=[pltpu.VMEM((blocks + 1, rows, cols), BF16)],
        prefetch=1,
        cost=6.0,
        name="route",
    )(spots, *groups)


def rotate_kernel(quarters, grads, right, left, first, second, rotated, update, total, low):
    step = BLK // 4
    for at in range(4):
        rows = pl.ds(at * step, step)
        product = 0.0
        for source, quarter in enumerate(quarters):
            width = grads.shape[2]
            product = product + dot(
                grads[source, rows, :], right[pl.ds(quarter * width, width), :]
            )
        value = dot_tt(left[rows, :], product.astype(BF16))
        if at:
            total[...] += value
        else:
            total[...] = value
    for at in range(4):
        rows = pl.ds(at * step, step)
        turned = total[rows, :]
        rotated[rows, :] = turned.astype(BF16)
        first_new = DECAY_RATE * first[rows, :].astype(F32) + (1.0 - DECAY_RATE) * turned
        second_new = DECAY_RATE * second[rows, :].astype(F32) + (1.0 - DECAY_RATE) * turned * turned
        direction = first_new / (jnp.sqrt(second_new) + EPS_ADAM)
        low[rows, :] = dot_t(direction.astype(BF16), right[...]).astype(BF16)
    for at in range(4):
        rows = pl.ds(at * step, step)
        update[rows, :] = dot(left[rows, :], low[...]).astype(BF16)


def rotate(grads, quarters, right, left, first, second):
    full = fixed((BLK, BLK))
    return call(
        functools.partial(rotate_kernel, quarters),
        (1,),
        [fixed(grads.shape), full, full, full, full],
        [full, full],
        [shaped((BLK, BLK), BF16)] * 2,
        scratch=[pltpu.VMEM((BLK, BLK), F32), pltpu.VMEM((BLK, BLK), BF16)],
        cost=16.0,
        name="rotate",
    )(grads, right, left, first, second)


def pick_kernel(count, amount, table, *refs):
    parts, out = refs[:count], refs[count]
    first = pl.program_id(0) * amount

    def put(spot, part):
        out[spot] = parts[part][table[1, first + spot]]

    for spot in range(amount):
        for part in range(count):
            pl.when(table[0, first + spot] == part)(functools.partial(put, spot, part))


def pick(parts, table):
    blocks = table.shape[1]
    amount = 4
    shape = (blocks,) + parts[0].shape[1:]
    return call(
        functools.partial(pick_kernel, len(parts), amount),
        (blocks // amount,),
        [fixed(value.shape) for value in parts],
        pl.BlockSpec((amount,) + shape[1:], lambda i, table: (i, 0, 0)),
        shaped(shape, BF16),
        prefetch=1,
        cost=12.0,
        name="pick",
    )(table, *parts)


def left_order(place, left):
    tokens, cols = left.shape
    count_z, count_x = place.size["z"], place.size["x"]
    blocks = cols // BLK
    rows = BLK // (count_z * count_x)
    value = left.reshape(tokens, blocks, count_z, count_x, rows)
    value = jnp.roll(value, (-place.at["z"], -place.at["x"]), axis=(2, 3))
    return value.transpose(0, 3, 2, 1, 4).reshape(tokens, cols)


def right_halves(place, right):
    tokens, cols = right.shape
    count_y = place.size["y"]
    width = BLK // (CORES * count_y)
    value = right.reshape(tokens, cols // BLK, CORES, count_y, width)
    halves = []
    for step in range(CORES):
        half = lax.dynamic_index_in_dim(value, (place.at["core"] + step) % CORES, 2, False)
        half = jnp.roll(half, -place.at["y"], axis=2)
        halves.append(half.transpose(2, 0, 1, 3).reshape(count_y, tokens, -1))
    return halves


def sum_job_plain(place, left, right, first):
    count_z, count_x, count_y = place.size["z"], place.size["x"], place.size["y"]
    left = left_order(place, left)
    right_mine, right_other = right_halves(place, right)
    left_both = jnp.concatenate([left, place.take(left, "core", 1)], axis=0)
    right_both = jnp.concatenate([right_mine, place.take(right_other, "core", 1)], axis=1)
    partial = [
        lax.dot_general(left_both, right_both[step], (((0,), (0,)), ((), ())), preferred_element_type=F32)
        .astype(BF16)
        .reshape(count_x, count_z, -1, right_both.shape[2])
        for step in range(count_y)
    ]
    if first == "y":
        total = place.scatter(partial, "y").astype(BF16)
        total = place.scatter(total, "x").astype(BF16)
    else:
        parts = [[value[step] for value in partial] for step in range(count_x)]
        parts = [jnp.stack(part) for part in parts]
        total = place.scatter(parts, "x").astype(BF16)
        total = place.scatter(total, "y").astype(BF16)
    total = place.scatter(total, "z")
    rows = BLK // (count_z * count_x)
    width = BLK // (CORES * count_y)
    if left.shape[1] > BLK:
        return total.reshape(-1, rows, width)
    return total.reshape(rows, -1, width).transpose(1, 0, 2)


class EverySum:
    def __init__(self, place, value):
        self.place = place
        self.terms = [value]
        self.plain = place.size["y"] != 2 or place.size["x"] != 2

    def step(self, axis, bit=0):
        if self.plain:
            return
        value = sum(self.terms)
        if axis == "z":
            pairs = self.place.size["x"]
            swap = [
                (z * pairs + x, (z ^ bit) * pairs + x) for z in range(DEPTH_Z) for x in range(pairs)
            ]
            self.terms = [value, lax.ppermute(value, "wsh", swap)]
        else:
            self.terms = [value, self.place.take(value, axis, 1)]

    def total(self):
        if self.plain:
            return lax.psum(self.terms[0], ("ctx", "wsh"))
        return sum(self.terms)


def doc_ids(lengths, position):
    starts = jnp.cumsum(lengths) - lengths
    return jnp.sum((position[:, None] >= starts[None, :]).astype(jnp.int32), axis=1)


def fill_up(rows_value, wsh_count):
    slots = rows_value.shape[0]
    return jnp.pad(rows_value.astype(BF16), ((0, wsh_count - slots), (0, 0), (0, 0)))


def to_owner(padded):
    return lax.all_to_all(padded, "wsh", 0, 0, tiled=True).reshape(BLK, BLK)


def from_owner(whole, wsh_count):
    cut = whole.astype(BF16).reshape(wsh_count, BLK // wsh_count, BLK)
    return lax.all_to_all(cut, "wsh", 0, 0, tiled=True)


def on_device(
    stream_in,
    doc_lengths,
    cotangent,
    weights,
    vec_params,
    owner_slots,
    master,
    left_bases,
    right_bases,
    moment1,
    moment2,
    vec_moment1,
    vec_moment2,
):
    tokens = stream_in.shape[1]
    ctx_count = lax.axis_size("ctx")
    wsh_count = lax.axis_size("wsh")
    place = Place(ctx_count, wsh_count)
    seq_len = tokens * ctx_count
    scaling = (wsh_count * seq_len) ** (-0.5)
    slots_dev, rows_dev = master.shape[0], master.shape[1]
    slot_total = ctx_count * slots_dev
    count_y = place.size["y"]
    width = BLK // ctx_count

    core_of = (place.at["core"] + jnp.arange(CORES)) % CORES
    y_of = (place.at["y"] + jnp.arange(count_y)) % count_y
    ctx_of = (y_of[None, :] * CORES + core_of[:, None]).reshape(-1)
    key_pos = (ctx_of[:, None] * tokens + jnp.arange(tokens)[None, :]).reshape(-1)
    doc_keys = doc_ids(doc_lengths[0], key_pos)
    mask = jnp.where(doc_keys[:, None] == doc_keys[None, :tokens], 0.0, -1e30).astype(F32)

    chunks = [
        Gathering(place, weights[layer_at, first : first + 4], split_count)
        for layer_at, first, split_count in (
            (0, 0, 3),
            (0, 4, 2),
            (0, 8, 2),
            (1, 0, 2),
            (1, 4, 2),
            (1, 8, 4),
        )
    ]

    live = {}

    def settle():
        going = [chunk for chunk in chunks if chunk]
        state = [(chunk.held, chunk.crossed) for chunk in going]
        state, values = together(state, {name: live[name] for name in live})
        for chunk, (held, crossed) in zip(going, state):
            chunk.held, chunk.crossed = held, crossed
        live.update(values)

    def finish(spot):
        chunk = chunks[spot]
        chunk.step_core()
        chunks[spot] = None
        return chunk

    def keyvals_of(layer_at):
        keyvals = live[f"keyvals{layer_at}"]
        return keyvals + [place.take(value, "core", 1) for value in keyvals[1:count_y]]

    kept = [{}, {}]
    slot_own = jnp.minimum(lax.axis_index("wsh"), slots_dev - 1)
    live["bases"] = (left_bases, right_bases)
    live["moments"] = (moment1, moment2)
    chunks[0].step_z()
    settle()
    left_rows, right_all = live.pop("bases")
    live["mask"] = mask
    live["vectors"] = [vector_sets(vec_params[layer_at]) for layer_at in range(LAYERS)]
    live["left"] = fill_up(left_rows, wsh_count)
    live["right"] = lax.dynamic_index_in_dim(right_all, slot_own, 0, False).astype(BF16)
    chunks[0].step_x()
    chunks[1].step_z()
    settle()
    first_rows, second_rows = live.pop("moments")
    mask = live.pop("mask")
    vectors = live.pop("vectors")
    live["first"] = fill_up(first_rows, wsh_count)
    live["second"] = fill_up(second_rows, wsh_count)
    chunks[0].step_y()
    chunks[1].step_x()
    chunks[2].step_z()
    settle()
    chunks[1].step_y()
    chunks[2].step_x()
    chunks[3].step_z()
    query_0, live["keyvals0"], w_in_0 = project_step(place, stream_in[0], finish(0), vectors[0])
    live["query"] = query_0
    settle()
    chunks[2].step_y()
    chunks[3].step_x()
    chunks[4].step_z()
    keyvals_0 = keyvals_of(0)
    query_0 = live["query"]
    attn_0, summed_one_0, middle_0, mid_low_0 = mix_step(
        query_0, keyvals_0, stream_in[0], w_in_0, vectors[0], mask
    )
    hidden_0, live["act"], w_up_0 = up_step(mid_low_0, finish(1), vectors[0])
    settle()
    chunks[3].step_y()
    chunks[4].step_x()
    chunks[5].step_z()
    act_0 = live["act"]
    summed_two_0, live["result"], live["result_low"], w_down_0 = down_step(
        act_0, finish(2), middle_0, vectors[0]
    )
    settle()
    chunks[4].step_y()
    chunks[5].step_x()
    result_0, result_low_0 = live["result"], live["result_low"]
    query_1, live["keyvals1"], w_in_1 = project_step(place, result_low_0, finish(3), vectors[1])
    live["query"] = query_1
    live["left"] = to_owner(live["left"])
    settle()
    chunks[5].step_y()
    live["first"] = to_owner(live["first"])
    keyvals_1 = keyvals_of(1)
    query_1 = live["query"]
    attn_1, summed_one_1, middle_1, mid_low_1 = mix_step(
        query_1, keyvals_1, result_0, w_in_1, vectors[1], mask
    )
    hidden_1, live["act"], w_up_1 = up_step(mid_low_1, finish(4), vectors[1])
    settle()
    act_1 = live["act"]
    summed_two_1, _, result_low_1, w_down_1 = down_step(act_1, finish(5), middle_1, vectors[1])
    stream_out = result_low_1[None]

    blocks = [(w_in_0, w_up_0, w_down_0), (w_in_1, w_up_1, w_down_1)]
    lefts = [
        (stream_in[0], attn_0, mid_low_0, act_0),
        (result_low_0, attn_1, mid_low_1, act_1),
    ]
    crossed = [
        (place.take(jnp.concatenate(values[:3], axis=1), "core", 1), place.take(values[3], "core", 1))
        for values in lefts
    ]
    summed = [(summed_one_0, summed_two_0), (summed_one_1, summed_two_1)]
    hidden = [hidden_0, hidden_1]
    queries = [query_0, query_1]
    keyvals_all = [keyvals_0, keyvals_1]
    gains = [
        (vectors[layer_at]["gain_one"], vectors[layer_at]["gain_two"]) for layer_at in range(LAYERS)
    ]
    live = {
        "crossed": crossed,
        "left": live["left"],
        "first": live["first"],
        "second": to_owner(live["second"]),
        "right": live["right"],
    }
    jobs = []
    vec_terms = [None] * LAYERS

    every = []

    def settle_back():
        state = [(job.parts, job.by_y, job.by_x, job.groups) for job in jobs]
        state, values, terms = together(state, dict(live), [one.terms for one in every])
        for one, value in zip(every, terms):
            one.terms = value
        for job, fields in zip(jobs, state):
            job.parts, job.by_y, job.by_x, job.groups = fields
        live.update(values)

    def begin(layer_at, first_block, *sets, right_other=None):
        ids = [layer_at * NBLK + first_block + spot for spot in range(4)]
        jobs.append(
            Summing(
                place,
                ids,
                [
                    (lefts[layer_at][spot], live["crossed"][layer_at][spot // 3], right, spot % 3, right_other)
                    for spot, right in sets
                ],
            )
        )
        return jobs[-1]

    def close_step(layer_at, flow):
        live["two"], live["ffn"], live["sums_two"] = close(flow, summed[layer_at][1], gains[layer_at][1])

    def down_job(layer_at, right_other=None):
        return begin(layer_at, 8, (3, live["ffn"]), right_other=right_other)

    def in_job(layer_at):
        return begin(layer_at, 0, (0, live["joined"]), (1, live["branch_in"]))

    def up_job(layer_at):
        return begin(layer_at, 4, (2, live["hid"]))

    def feed_step(layer_at):
        w_in, w_up, w_down = blocks[layer_at]
        live["hid"], live["branch"], attn_grad, live["one"], live["sums_one"], live["sums_up"] = feed_back(
            live["two"], live["ffn"], summed[layer_at][0], hidden[layer_at], w_down, w_up, w_in, gains[layer_at][0]
        )
        live["attn_grad"] = attn_grad

    def attend_step(layer_at):
        live["grad_q"], mine, other = attend_back(
            queries[layer_at], keyvals_all[layer_at], live["attn_grad"], mask
        )
        live["pair"] = [mine, other]

    def send_step():
        mine, other = live["pair"]
        arrived = place.take(other, "core", 1)
        live["kv"] = [mine, arrived] + [
            place.take((mine[step].astype(F32) + arrived[step].astype(F32)).astype(BF16), "y", -step)[None]
            for step in range(1, count_y)
        ]

    def input_step(layer_at):
        live["joined"], grad_x, in_sums = input_back(live["grad_q"], live["kv"], live["one"], blocks[layer_at][0])
        sums_two, sums_one = live["sums_two"], live["sums_one"]
        vec_terms[layer_at] = jnp.concatenate(
            [
                in_sums[0, 0],
                in_sums[2, 0],
                sums_one[0],
                sums_two[0],
                sums_one[1:3].reshape(-1),
                sums_two[1:3].reshape(-1),
                live["sums_up"].reshape(-1),
            ]
        )
        live["branch_in"] = live["branch"]
        return grad_x

    close_step(1, cotangent[0])
    down_1 = down_job(1)
    feed_step(1)
    settle_back()
    down_1.first_y()
    down_1.first_x()
    up_1 = up_job(1)
    settle_back()
    down_1.second_x()
    down_1.second_y()
    up_1.first_y()
    up_1.first_x()
    attend_step(1)
    settle_back()
    send_step()
    down_1.third()
    up_1.second_x()
    settle_back()
    up_1.second_y()
    grad_flow = input_step(1)
    close_step(0, grad_flow)
    settle_back()
    in_1 = in_job(1)
    live["ffn_other"] = place.take(live["ffn"], "core", 1)
    settle_back()
    up_1.third()
    in_1.first_y()
    in_1.first_x()
    feed_step(0)
    down_0 = down_job(0, live.pop("ffn_other"))
    settle_back()
    in_1.second_x()
    in_1.second_y()
    down_0.first_y()
    down_0.first_x()
    attend_step(0)
    settle_back()
    send_step()
    in_1.third()
    down_0.second_x()
    down_0.second_y()
    up_0 = up_job(0)
    settle_back()
    down_0.third()
    up_0.first_y()
    up_0.first_x()
    grad_flow = input_step(0)
    every.append(EverySum(place, jnp.stack(vec_terms)))
    settle_back()
    every[0].step("core")
    up_0.second_x()
    up_0.second_y()
    in_0 = in_job(0)
    settle_back()
    up_0.third()
    every[0].step("y")
    in_0.first_y()
    in_0.first_x()
    settle_back()
    every[0].step("x")
    in_0.second_x()
    in_0.second_y()
    settle_back()
    every[0].step("z", 1)
    in_0.third()
    settle_back()
    every[0].step("z", 2)
    stream_grad = grad_flow[None]
    vec_grads = every[0].total() * scaling
    groups = [group for job in jobs for group in job.groups]
    turned = [job.turned for job in jobs for group in job.groups]
    ids = [block for job in jobs for block in job.ids]

    owner_flat = owner_slots.reshape(-1)
    block_count = LAYERS * NBLK
    owner_sorted = jnp.stack([owner_flat[block] for block in ids])
    picks = owner_sorted[None, :] == jnp.arange(slot_total, dtype=jnp.int32)[:, None]
    spots = jnp.where(
        jnp.any(picks, axis=1), jnp.argmax(picks, axis=1).astype(jnp.int32), block_count
    )
    by_slot = route(groups, turned, spots, slots_dev, wsh_count, rows_dev, scaling)

    arrived = lax.all_to_all(
        by_slot.reshape(ctx_count * wsh_count, rows_dev, width), ("ctx", "wsh"), 0, 0, tiled=True
    )
    quarter_parts = []
    for step in range(ctx_count):
        step_y, step_core = step // CORES, step % CORES
        to_ctx = ((place.at["y"] + step_y) % count_y) * CORES + (place.at["core"] + step_core) % CORES
        part = lax.dynamic_index_in_dim(by_slot, to_ctx, 0, False)[:slots_dev]
        pairs = [
            (y * CORES + core, ((y + step_y) % count_y) * CORES + (core + step_core) % CORES)
            for y in range(count_y)
            for core in range(CORES)
        ]
        quarter_parts.append(lax.ppermute(part, "ctx", pairs) if step else part)
    quarters = [(source % CORES) * count_y + source // CORES for source in range(ctx_count)]
    by_rows = jnp.stack(quarter_parts)
    by_source = [
        lax.dynamic_index_in_dim(
            by_rows,
            ((place.at["y"] - source // CORES) % count_y) * CORES + (place.at["core"] - source % CORES) % CORES,
            0,
            False,
        )
        for source in range(ctx_count)
    ]
    by_source = jnp.stack([by_source[quarters.index(quarter)] for quarter in range(ctx_count)])
    block_grads = by_source.transpose(1, 2, 0, 3).reshape(slots_dev, rows_dev, BLK).astype(F32)
    arrived, block_grads = together(arrived, block_grads)
    rotated_own, update_own = rotate(
        arrived.reshape(ctx_count, BLK, width), quarters, live["right"], live["left"], live["first"], live["second"]
    )

    update = from_owner(update_own, wsh_count)
    update, vec_grads = together(update, vec_grads)
    master_low = (master - LR_BLOCK * update[:slots_dev].astype(F32)).astype(BF16)
    master_low, update, rotated_own = together(master_low, update, rotated_own)
    parts = gather_list(place, master_low, "y")
    rotated = from_owner(rotated_own, wsh_count)
    across = place.take(master_low, "core", 1)
    new_master = master - LR_BLOCK * update[:slots_dev].astype(F32)
    parts = parts + [across] + [place.take(value, "core", 1) for value in parts[1:]]
    owner_ctx, owner_at = owner_flat // slots_dev, owner_flat % slots_dev
    step_y = (owner_ctx // CORES - place.at["y"]) % count_y
    step_core = (owner_ctx % CORES - place.at["core"]) % CORES
    table = jnp.stack([step_core * count_y + step_y, owner_at]).astype(jnp.int32)
    new_weights = pick(parts, table).reshape(LAYERS, NBLK, rows_dev, BLK)
    rotated, _ = together(rotated, (new_weights[0, 0, :8, :128], new_master[0, :8, :128]))
    rotated = rotated[:slots_dev].astype(F32)

    new_moment1 = DECAY_RATE * moment1 + (1.0 - DECAY_RATE) * rotated
    new_moment2 = DECAY_RATE * moment2 + (1.0 - DECAY_RATE) * rotated * rotated

    new_vec_moment1 = DECAY_RATE * vec_moment1 + (1.0 - DECAY_RATE) * vec_grads
    new_vec_moment2 = DECAY_RATE * vec_moment2 + (1.0 - DECAY_RATE) * vec_grads * vec_grads
    new_vec_params = vec_params - LR_VEC * new_vec_moment1 / (jnp.sqrt(new_vec_moment2) + EPS_ADAM)
    return (
        stream_out,
        stream_grad,
        block_grads,
        new_moment1,
        new_moment2,
        new_master,
        new_weights,
        vec_grads,
        new_vec_params,
        new_vec_moment1,
        new_vec_moment2,
    )


def solution(mesh):
    rows = P("ctx", "wsh", None)
    placed = (
        P("wsh", "ctx", None),
        P("wsh", None),
        P("wsh", "ctx", None),
        P(None, None, "wsh", None),
        P(),
        P(),
        rows,
        rows,
        P("ctx", None, None),
        rows,
        rows,
        P(),
        P(),
    )
    return jax.shard_map(
        on_device,
        mesh=mesh,
        in_specs=placed,
        out_specs=(
            P("wsh", "ctx", None),
            P("wsh", "ctx", None),
            rows,
            rows,
            rows,
            rows,
            P(None, None, "wsh", None),
            P(),
            P(),
            P(),
            P(),
        ),
        check_vma=False,
    )
```
